128 devices in a mesh: section: 2 (over y_lo), dp: 32 (over x, z, core), tensor: 2 (over y_hi).
Axes of the slice: x: 4, y: 4 (y_hi: 2, y_lo: 2; y = y_hi * 2 + y_lo), z: 4, core: 2. Of those that a mesh axis runs over, the one named last changes fastest.
Arguments:
- inputs: bfloat16 [2, 4608, 1536], P(None, ('dp', 'tensor')), may hold values from -16 to 16
- out_grad: bfloat16 [2, 4608, 1536], P(None, ('dp', 'tensor')), may hold values from -6 to 6
- lengths: int32 [2, 32, 4], replicated, may hold values from 1 to 128, 144 in all within a row
- order: int32 [2, 32], replicated, may hold values from 0 to 31, each once within a row
- gelu_weight: bfloat16 [2, 1536, 2048], P('section', 'dp', 'tensor'), may hold values from -0.15625 to 0.15625
- lru_weight: bfloat16 [2, 1536, 2048], P('section', 'dp', 'tensor'), may hold values from -0.15625 to 0.15625
- rate_weight: bfloat16 [2, 16, 128, 128], P('section', 'tensor', 'dp'), may hold values from -0.5 to 0.5
- input_weight: bfloat16 [2, 16, 128, 128], P('section', 'tensor', 'dp'), may hold values from -0.5 to 0.5
- rate_bias: bfloat16 [2, 16, 128], P('section', 'tensor', 'dp'), may hold values from -3 to 3
- input_bias: bfloat16 [2, 16, 128], P('section', 'tensor', 'dp'), may hold values from -3 to 3
- decay_param: bfloat16 [2, 16, 128], P('section', 'tensor', 'dp'), may hold values from 0.5 to 8
- filter_taps: bfloat16 [2, 4, 16, 128], P('section', None, 'tensor', 'dp'), may hold values from -2 to 2
- filter_bias: bfloat16 [2, 16, 128], P('section', 'tensor', 'dp'), may hold values from -2 to 2
- out_weight: bfloat16 [2, 2048, 1536], P('section', 'tensor', 'dp'), may hold values from -0.25 to 0.25
- gate_weight: bfloat16 [2, 1536, 4608], P('section', 'dp', 'tensor'), may hold values from -0.15625 to 0.15625
- up_weight: bfloat16 [2, 1536, 4608], P('section', 'dp', 'tensor'), may hold values from -0.15625 to 0.15625
- down_weight: bfloat16 [2, 4608, 1536], P('section', 'tensor', 'dp'), may hold values from -0.1875 to 0.1875
- norm_first: bfloat16 [2, 1536], P('section', 'dp'), may hold values from 0.5 to 1.5
- norm_second: bfloat16 [2, 1536], P('section', 'dp'), may hold values from 0.5 to 1.5
Outputs:
- hidden_out: float32 [2, 2, 4608, 1536], P('section', None, ('dp', 'tensor'))
- input_grad: float32 [2, 2, 4608, 1536], P('section', None, ('dp', 'tensor'))
- grad_gelu_weight: float32 [2, 1536, 2048], P('section', 'dp', 'tensor')
- grad_lru_weight: float32 [2, 1536, 2048], P('section', 'dp', 'tensor')
- grad_rate_weight: float32 [2, 16, 128, 128], P('section', 'tensor', 'dp')
- grad_input_weight: float32 [2, 16, 128, 128], P('section', 'tensor', 'dp')
- grad_rate_bias: float32 [2, 16, 128], P('section', 'tensor', 'dp')
- grad_input_bias: float32 [2, 16, 128], P('section', 'tensor', 'dp')
- grad_decay_param: float32 [2, 16, 128], P('section', 'tensor', 'dp')
- grad_filter_taps: float32 [2, 4, 16, 128], P('section', None, 'tensor', 'dp')
- grad_filter_bias: float32 [2, 16, 128], P('section', 'tensor', 'dp')
- grad_out_weight: float32 [2, 2048, 1536], P('section', 'tensor', 'dp')
- grad_gate_weight: float32 [2, 1536, 4608], P('section', 'dp', 'tensor')
- grad_up_weight: float32 [2, 1536, 4608], P('section', 'dp', 'tensor')
- grad_down_weight: float32 [2, 4608, 1536], P('section', 'tensor', 'dp')
- grad_norm_first: float32 [2, 1536], P('section', 'dp')
- grad_norm_second: float32 [2, 1536], P('section', 'dp')
The draws below stay inside these ranges and needn't reach their ends.
Inputs may be any that keep to these rules, and one draw needn't show every extreme that they name: Each row lengths[m, g, :] holds 4 document lengths that sum to 144; the longest in every row is exactly 128. Each row order[m, :] names every data group exactly once.
All inputs are finite; a program needn't handle non-finite values.
Results may differ from the reference program's by a relative error of at most 0.039.
Values may be sent and summed in bfloat16 or wider, within the bound.
A program may use at most 320 MiB of HBM per device.

```python
import math
import jax
import jax.numpy as jnp
import numpy as np
from jax import lax

D = 1536
R = 2048
FF = 4608
NBLK = 16
CONV = 4
MB = 2
DOCS = 4
BS = 128
GROUP = 144
LONGEST = 128
GROUPS = 32
TOKENS = 4608
BLOCKS = 2


def strengthened(values, key, source, target, shards_of, factor):
    owner, partner = [(jnp.arange(values.shape[dim]) // (values.shape[dim] // shards_of)).reshape([-1 if axis == dim else 1 for axis in range(values.ndim)]) for dim in (source, target)]
    chosen = jax.random.permutation(key, shards_of)[partner]
    strong = (owner == chosen) | (owner == (partner + shards_of // 2) % shards_of)
    return jnp.where(strong, factor * values, values)


def steps_of(key, shape, pieces, least, largest):
    factor_of = 1.0
    for dim, parts in pieces:
        heights = jax.random.uniform(jax.random.fold_in(jax.random.fold_in(key, 6), dim), (parts,), jnp.float32, least / len(pieces), largest / len(pieces))
        factor_of = factor_of * jnp.repeat(jnp.exp(heights), shape[dim] // parts).reshape((-1,) + (1,) * (len(shape) - 1 - dim))
    return factor_of


def split_up(count, total, bound, slope):
    weights = [(1 << 20) // math.isqrt(standing ** slope) + 1 for standing in range(2, count + 1)]
    spare, counts = total - bound - (count - 1), [1] * (count - 1)
    while spare > 0:
        movable = [i for i in range(count - 1) if counts[i] < bound]
        mass, left = sum([weights[i] for i in movable]), spare
        for i in movable:
            addition = min(bound - counts[i], max(1, left * weights[i] // mass), spare)
            counts[i] = counts[i] + addition
            spare = spare - addition
    return np.array([bound] + counts)


def ragged_sizes(own_key, count, total, bound, lean):
    if count == 2:
        one = jax.random.randint(own_key, (), max(1, total - bound), min(bound, total - 1) + 1)
        return jnp.stack([one, total - one])
    sizes = jnp.asarray(split_up(count, total, bound, lean), jnp.int32)
    pairs = (count - 1) // 2
    source_of, receiver = sizes[1:1 + 2 * pairs:2], sizes[2:2 + 2 * pairs:2]
    room = jnp.minimum(source_of - 1, bound - receiver)
    moved = jax.random.randint(jax.random.fold_in(own_key, 1), (pairs,), 0, 1 << 20) % (room + 1)
    sizes = sizes.at[1:1 + 2 * pairs:2].set(source_of - moved).at[2:2 + 2 * pairs:2].set(receiver + moved)
    return sizes[jax.random.permutation(jax.random.fold_in(own_key, 2), count)]


def centred(rng, dims, scale, limit, split=(), kind=jnp.bfloat16):
    factor_of = steps_of(rng, dims, split, -0.22, 0.18) if split else 1.0
    drawn = jax.random.normal(rng, dims, jnp.float32) * scale * factor_of
    return jnp.minimum(jnp.maximum(drawn, -limit), limit).astype(kind)


def gaussian_with(stream_key, shape, deviation, reach, shards, heavy, held_as=jnp.bfloat16):
    entries = deviation * jax.random.normal(stream_key, shape, jnp.float32)
    if shards:
        entries = entries * steps_of(stream_key, shape, shards, -0.22, 0.18)
    return jnp.clip(strengthened(entries, jax.random.fold_in(stream_key, 3), *heavy), -reach, reach).astype(held_as)


def setup_inputs(seed: int = 0) -> dict:
    key_of = jax.random.split(jax.random.key(seed), 20)
    return {
        "inputs": gaussian_with(key_of[0], (MB, TOKENS, D), 1.0, 16.0, ((1, 64),), (1, 2, 64, 4.0)),
        "out_grad": centred(key_of[1], (MB, TOKENS, D), 1.0, 6.0, ((1, 64),)),
        "lengths": jax.vmap(lambda own: ragged_sizes(own, DOCS, GROUP, LONGEST, 2))(jax.random.split(key_of[2], MB * GROUPS)).reshape((MB, GROUPS, DOCS)).astype(jnp.int32),
        "order": jax.vmap(lambda own: jax.random.permutation(own, GROUPS))(jax.random.split(key_of[3], MB)).reshape((MB, GROUPS)).astype(jnp.int32),
        "gelu_weight": centred(key_of[4], (BLOCKS, D, R), D ** -0.5, 0.15625, ((0, 2), (1, 32), (2, 2))),
        "lru_weight": centred(key_of[5], (BLOCKS, D, R), D ** -0.5, 0.15625, ((0, 2), (1, 32), (2, 2))),
        "rate_weight": centred(key_of[6], (BLOCKS, NBLK, BS, BS), BS ** -0.5, 0.5, ((0, 2), (1, 2), (2, 32))),
        "input_weight": centred(key_of[7], (BLOCKS, NBLK, BS, BS), BS ** -0.5, 0.5, ((0, 2), (1, 2), (2, 32))),
        "rate_bias": centred(key_of[8], (BLOCKS, NBLK, BS), 1.0, 3.0, ((0, 2), (1, 2), (2, 32))),
        "input_bias": centred(key_of[9], (BLOCKS, NBLK, BS), 1.0, 3.0, ((0, 2), (1, 2), (2, 32))),
        "decay_param": jnp.clip(jnp.exp(math.log(8.0) - 2.7725887 * jax.random.uniform(key_of[10], (BLOCKS, NBLK, BS), jnp.float32) ** steps_of(key_of[10], (BLOCKS, NBLK, BS), ((0, 2), (1, 2), (2, 32)), -0.2, 0.2)), 0.5, 8.0).astype(jnp.bfloat16),
        "filter_taps": centred(key_of[11], (BLOCKS, CONV, NBLK, BS), 0.5, 2.0, ((0, 2), (2, 2), (3, 32))),
        "filter_bias": centred(key_of[12], (BLOCKS, NBLK, BS), 0.5, 2.0, ((0, 2), (1, 2), (2, 32))),
        "out_weight": centred(key_of[13], (BLOCKS, R, D), (R // 4) ** -0.5, 0.25, ((0, 2), (1, 2), (2, 32))),
        "gate_weight": centred(key_of[14], (BLOCKS, D, FF), D ** -0.5, 0.15625, ((0, 2), (1, 32), (2, 2))),
        "up_weight": centred(key_of[15], (BLOCKS, D, FF), D ** -0.5, 0.15625, ((0, 2), (1, 32), (2, 2))),
        "down_weight": centred(key_of[16], (BLOCKS, FF, D), (FF // 4) ** -0.5, 0.1875, ((0, 2), (1, 2), (2, 32))),
        "norm_first": jnp.clip(1.0 + 0.1 * jax.random.normal(key_of[17], (BLOCKS, D), jnp.float32), 0.5, 1.5).astype(jnp.bfloat16),
        "norm_second": jnp.clip(1.0 + 0.1 * jax.random.normal(key_of[18], (BLOCKS, D), jnp.float32), 0.5, 1.5).astype(jnp.bfloat16),
    }


@jax.custom_vjp
def low(v):
    return lax.optimization_barrier(v.astype(jnp.bfloat16)).astype(jnp.float32)

@jax.custom_vjp
def low_back(v):
    return v

def low_keep(v):
    return (low(v), None)

def low_pass(kept, grad):
    return (grad,)

def back_keep(v):
    return (v, None)

def back_low(kept, grad):
    return (low(grad),)
low.defvjp(low_keep, low_pass)
low_back.defvjp(back_keep, back_low)
precise = lax.Precision.HIGHEST
epsilon = 1e-06
floor_value = 0.01

def matmul(left, right):
    return jnp.matmul(left, right, precision=precise)

def rms_norm(values, gain):
    return values * lax.rsqrt(lax.optimization_barrier(jnp.mean(values * values, axis=-1, keepdims=True)) + epsilon) * gain

def lag_rows(values, offset):
    if offset == 0:
        return values
    padded = jnp.pad(values, ((0, 0), (offset, 0), (0, 0)))
    return padded[:, :values.shape[1]]

def document_masks(doc_lengths):
    doc_ends = jnp.cumsum(doc_lengths, axis=-1, dtype=jnp.int32)
    position = jnp.arange(GROUP, dtype=jnp.int32)
    doc_ident = lax.optimization_barrier(jnp.sum((position[None, :, None] >= doc_ends[:, None, :]).astype(jnp.int32), axis=-1, dtype=jnp.int32))
    lag_masks = []
    for offset in range(CONV):
        before = jnp.pad(doc_ident, ((0, 0), (offset, 0)), constant_values=-1)[:, :GROUP]
        lag_masks.append((before == doc_ident).astype(jnp.float32)[:, :, None])
    return lag_masks

def linear_recurrence(carry_decay, drive):

    def advance(state_now, inputs_now):
        decay_now, drive_now = inputs_now
        state_now = decay_now * state_now + drive_now
        return (state_now, state_now)
    start = jnp.zeros((drive.shape[0], drive.shape[2]), jnp.float32)
    _, states = lax.scan(advance, start, (jnp.moveaxis(carry_decay, 1, 0), jnp.moveaxis(drive, 1, 0)))
    return jnp.moveaxis(states, 0, 1)

def recurrent_block(values, params, lag_masks):
    gelu_weight, lru_weight, rate_weight, input_weight, rate_bias, input_bias, decay_param, filter_taps, filter_bias, out_weight, gate_weight, up_weight, down_weight, norm_first, norm_second = params
    batch = values.shape[0]
    normed_one = low(rms_norm(values, norm_first))
    branch = jax.nn.gelu(low_back(matmul(normed_one, gelu_weight)))
    feature = low_back(matmul(normed_one, lru_weight))
    filtered = filter_bias.reshape(-1)
    for offset in range(CONV):
        filtered = filtered + filter_taps[offset].reshape(-1) * lag_rows(feature, offset) * lag_masks[offset]
    conv_out = low(filtered)
    blocks = conv_out.reshape(batch, GROUP, NBLK, BS)
    pre_rate = jnp.einsum('bgkc,kcd->bgkd', blocks, rate_weight, precision=precise) + rate_bias
    pre_input = jnp.einsum('bgkc,kcd->bgkd', blocks, input_weight, precision=precise) + input_bias
    rate_gate = jax.nn.sigmoid(low_back(pre_rate)).reshape(batch, GROUP, R)
    input_gate = jax.nn.sigmoid(low_back(pre_input)).reshape(batch, GROUP, R)
    forget = jax.nn.softplus(-decay_param).reshape(-1)
    decay_rate = jnp.exp(-8.0 * rate_gate * forget)
    scale_in = jnp.sqrt(jnp.maximum(1.0 - decay_rate * decay_rate, floor_value))
    state = linear_recurrence(decay_rate * lag_masks[1], scale_in * input_gate * conv_out)
    mixed = low(state * branch)
    middle = values + low_back(matmul(mixed, out_weight))
    normed_two = low(rms_norm(middle, norm_second))
    pre_gate = low_back(matmul(normed_two, gate_weight))
    pre_up = low_back(matmul(normed_two, up_weight))
    hidden = low(jax.nn.gelu(pre_gate) * pre_up)
    return middle + low_back(matmul(hidden, down_weight))

def add_trees(left_value, right_value):
    return left_value + right_value

def reference(inputs, out_grad, lengths, order, gelu_weight, lru_weight, rate_weight, input_weight, rate_bias, input_bias, decay_param, filter_taps, filter_bias, out_weight, gate_weight, up_weight, down_weight, norm_first, norm_second):
    params = [member.astype(jnp.float32) for member in (gelu_weight, lru_weight, rate_weight, input_weight, rate_bias, input_bias, decay_param, filter_taps, filter_bias, out_weight, gate_weight, up_weight, down_weight, norm_first, norm_second)]
    first = [member[0] for member in params]
    second = [member[1] for member in params]
    inverse = jnp.argsort(order, axis=-1).astype(jnp.int32)
    values_all = inputs.astype(jnp.float32).reshape(MB, GROUPS, GROUP, D)
    cotangent_all = out_grad.astype(jnp.float32).reshape(MB, GROUPS, GROUP, D)
    values_dealt = jnp.take_along_axis(values_all, inverse[:, :, None, None], axis=1)
    cotangent_dealt = jnp.take_along_axis(cotangent_all, inverse[:, :, None, None], axis=1)
    lengths_dealt = jnp.take_along_axis(lengths, inverse[:, :, None], axis=1)

    def micro_step(totals, items):
        values, cotangent, doc_lengths = items
        lag_masks = document_masks(doc_lengths)

        def forward(start_rows, probe, weights_one, weights_two):
            out_one = recurrent_block(start_rows, weights_one, lag_masks)
            out_two = recurrent_block(low_back(low(out_one)) + probe, weights_two, lag_masks)
            return (out_one, out_two)
        probe = jnp.zeros_like(values)
        outputs, pull = jax.vjp(forward, values, probe, first, second)
        grad_start, grad_probe, grad_one, grad_two = pull((jnp.zeros_like(outputs[0]), cotangent))
        totals = jax.tree.map(add_trees, totals, (grad_one, grad_two))
        return (totals, (outputs[0], outputs[1], grad_start, grad_probe))
    zeros_start = ([jnp.zeros_like(member) for member in first], [jnp.zeros_like(member) for member in second])
    totals, stacked = lax.scan(micro_step, zeros_start, (values_dealt, cotangent_dealt, lengths_dealt))
    out_one, out_two, grad_start, grad_probe = stacked
    grad_start = jnp.take_along_axis(grad_start, order[:, :, None, None], axis=1)
    grad_probe = jnp.take_along_axis(grad_probe, order[:, :, None, None], axis=1)
    hidden_out = jnp.stack([out_one, out_two]).reshape(BLOCKS, MB, TOKENS, D)
    input_grad = jnp.stack([grad_start, grad_probe]).reshape(BLOCKS, MB, TOKENS, D)
    grads = [jnp.stack([one_grad, two_grad]) for one_grad, two_grad in zip(totals[0], totals[1])]
    return (hidden_out, input_grad, grads[0], grads[1], grads[2], grads[3], grads[4], grads[5], grads[6], grads[7], grads[8], grads[9], grads[10], grads[11], grads[12], grads[13], grads[14])
```

```python
import jax
import jax.numpy as jnp
from jax import lax
from jax.experimental import pallas as pl
from jax.experimental.pallas import tpu as pltpu
from jax.sharding import PartitionSpec as P

epsilon = 1e-06
floor_value = 0.01


MESH = pl.DeviceIdType.MESH
ROWS = 48

def ag_body(w_ref, g_ref, lsem, s1s, s1r, s2s, s2r, s3s, s3r, K, L=1, SIB=True):
    dp = lax.axis_index("dp")
    c = dp % 2; z = (dp // 2) % 4; x = dp // 8
    def at(dx, dz):
        return ((x + dx) % 4) * 8 + ((z + dz) % 4) * 2 + c
    dAp, dAm = at(1 - c, c), at(3 * (1 - c), 3 * c)
    dBp, dBm = at(c, 1 - c), at(3 * c, 3 * (1 - c))
    sib = dp + 1 - 2 * c
    barrier = pltpu.get_barrier_semaphore()
    for d in (dAp, dAm, dBp, dBm, sib):
        pl.semaphore_signal(barrier, inc=1, device_id={"dp": d}, device_id_type=MESH)
    pl.semaphore_wait(barrier, 5)
    def go(r, dev, ssem, rsem):
        return pltpu.make_async_remote_copy(src_ref=r, dst_ref=r, send_sem=ssem, recv_sem=rsem,
                                            device_id={"dp": dev}, device_id_type=MESH)
    def one(k, j):
        return g_ref.at[k, (x + j * (1 - c)) % 4, (z + j * c) % 4, c]
    def p1(k, j, recv):
        d = (0, 0)[j] if j < 2 else None
        if j == 0:
            return go(one(k, 3 if recv else 0), dAp, s1s.at[k, 0], s1r.at[k, 0])
        return go(one(k, 1 if recv else 0), dAm, s1s.at[k, 1], s1r.at[k, 1])
    def p1f(k, par, recv):
        if par == 0:
            return go(one(k, 2 if recv else 3), dAp, s1s.at[k, 2], s1r.at[k, 2])
        return go(one(k, 2 if recv else 1), dAm, s1s.at[k, 2], s1r.at[k, 2])
    def byc(fn):
        @pl.when(c == 0)
        def _(): fn(0)
        @pl.when(c == 1)
        def _(): fn(1)
    def row(k, j, col):
        if col == 0: return g_ref.at[k, :, (z + j) % 4, 0]
        return g_ref.at[k, (x + j) % 4, :, 1]
    def p2(k, j, recv, col):
        if j == 0: return go(row(k, 3 if recv else 0, col), dBp, s2s.at[k, 0], s2r.at[k, 0])
        return go(row(k, 1 if recv else 0, col), dBm, s2s.at[k, 1], s2r.at[k, 1])
    def p2f(k, par, recv, col):
        if par == 0: return go(row(k, 2 if recv else 3, col), dBp, s2s.at[k, 2], s2r.at[k, 2])
        return go(row(k, 2 if recv else 1, col), dBm, s2s.at[k, 2], s2r.at[k, 2])
    def sb(k, j, col):
        return go(row(k, j, col), sib, s3s.at[k, j], s3r.at[k, j])
    own = pltpu.make_async_copy(w_ref, g_ref.at[:, x, z, c], lsem)
    own.start()
    own.wait()
    def parity(k, fn):
        @pl.when(k % 2 == 0)
        def _(): fn(0)
        @pl.when(k % 2 == 1)
        def _(): fn(1)
    def step(t, carry):
        @pl.when(t < K)
        def _():
            k = t
            p1(k, 0, False).start(); p1(k, 1, False).start()
        @pl.when(jnp.logical_and(t >= L, t - L < K))
        def _():
            k = t - L
            def f(par):
                p1(k, par, True).wait_recv()
                p1f(k, par, False).start()
                p1(k, 1 - par, True).wait_recv()
            parity(k, f)
        @pl.when(jnp.logical_and(t >= 2 * L, t - 2 * L < K))
        def _():
            k = t - 2 * L
            parity(k, lambda par: p1f(k, par, True).wait_recv())
            def f(col):
                p2(k, 0, False, col).start(); p2(k, 1, False, col).start()
                if SIB: sb(k, 0, col).start()
            byc(f)
        @pl.when(jnp.logical_and(t >= 3 * L, t - 3 * L < K))
        def _():
            k = t - 3 * L
            def g(col):
                def f(par):
                    p2(k, par, True, col).wait_recv()
                    p2f(k, par, False, col).start()
                    p2(k, 1 - par, True, col).wait_recv()
                parity(k, f)
                if SIB: sb(k, 1, col).start(); sb(k, 3, col).start()
            byc(g)
        @pl.when(t >= 4 * L)
        def _():
            k = t - 4 * L
            def g(col):
                parity(k, lambda par: p2f(k, par, True, col).wait_recv())
                if SIB: sb(k, 2, col).start()
            byc(g)
        return carry
    lax.fori_loop(0, K + 4 * L, step, 0)
    def finish(k, carry):
        p1(k, 0, False).wait_send(); p1(k, 1, False).wait_send()
        parity(k, lambda par: p1f(k, par, False).wait_send())
        def g(col):
            p2(k, 0, False, col).wait_send(); p2(k, 1, False, col).wait_send()
            parity(k, lambda par: p2f(k, par, False, col).wait_send())
            if SIB:
                for j in range(4):
                    sb(k, j, col).wait_send()
                    go(row(k, j, 1 - col), sib, s3s.at[k, j], s3r.at[k, j]).wait_recv()
        byc(g)
        return carry
    lax.fori_loop(0, K, finish, 0)

def gather(w, vmem=True, L=1, SIB=True, cid=1):
    K, _, CW = w.shape
    def kern(w_ref, o_ref, *rest):
        if vmem:
            g_ref, osem, *sems = rest
            ag_body(w_ref, g_ref, *sems, K, L, SIB)
            cp = pltpu.make_async_copy(g_ref, o_ref, osem); cp.start(); cp.wait()
        else:
            ag_body(w_ref, o_ref, *rest, K, L, SIB)
    D = pltpu.SemaphoreType.DMA
    sems = [D(()), D((K, 3)), D((K, 3)), D((K, 3)), D((K, 3)), D((K, 4)), D((K, 4))]
    shape = (K, 4, 4, 2, ROWS, CW)
    if vmem:
        sems = [pltpu.VMEM(shape, w.dtype), D(())] + sems
    return pl.pallas_call(kern, out_shape=jax.ShapeDtypeStruct(shape, w.dtype),
        in_specs=[pl.BlockSpec(memory_space=pl.ANY)], out_specs=pl.BlockSpec(memory_space=pl.ANY),
        scratch_shapes=sems,
        compiler_params=pltpu.CompilerParams(collective_id=cid, has_side_effects=True, vmem_limit_bytes=60*2**20))(w)


def from_behind(block, axis, distance):
    devices = range(lax.axis_size(axis))
    route = [(i - distance, i) for i in devices if i - distance in devices]
    return lax.ppermute(block, axis, route)


def widen(value):
    return lax.optimization_barrier(value).astype(jnp.float32)


def lag_rows(values, offset):
    if offset == 0:
        return values
    zeros_head = jnp.zeros((offset,) + values.shape[1:], values.dtype)
    return jnp.concatenate([zeros_head, values[: values.shape[0] - offset]], axis=0)


def lead_rows(values, offset):
    if offset == 0:
        return values
    zeros_tail = jnp.zeros((offset,) + values.shape[1:], values.dtype)
    return jnp.concatenate([values[offset:], zeros_tail], axis=0)


def document_masks(doc_lengths, group_rows, tap_count):
    doc_ends = jnp.cumsum(doc_lengths, dtype=jnp.int32)
    position = jnp.arange(group_rows, dtype=jnp.int32)
    doc_ident = jnp.sum(
        (position[:, None] >= doc_ends[None, :]).astype(jnp.int32), axis=1, dtype=jnp.int32
    )
    lag_masks = []
    for offset in range(tap_count):
        before = jnp.concatenate(
            [jnp.full((offset,), -1, jnp.int32), doc_ident[: group_rows - offset]]
        )
        lag_masks.append((before == doc_ident).astype(jnp.float32)[:, None])
    return lag_masks


def chain_combine(earlier, later):
    return (earlier[0] * later[0], later[0] * earlier[1] + later[1])


def contract_rows(left, right):
    return lax.dot_general(
        left, right, (((0,), (0,)), ((), ())), preferred_element_type=jnp.float32
    )


def contract_cols(left, right):
    return lax.dot_general(
        left, right, (((1,), (1,)), ((), ())), preferred_element_type=jnp.float32
    )


def rms_back(grad_normed, values, scale):
    return scale * grad_normed - values * scale * scale * scale * jnp.mean(
        grad_normed * values, axis=1, keepdims=True
    )


def spread_rows(normed):
    return lax.all_gather(normed, "tensor", axis=0, tiled=True)


def collect_rows(partial_rows):
    return lax.psum_scatter(partial_rows, "tensor", scatter_dimension=0, tiled=True)


def spread_grads(grads_low):
    return lax.all_gather(grads_low, "tensor", axis=0, tiled=True)


def collect_grads(partial_rows):
    return lax.psum_scatter(partial_rows, "tensor", scatter_dimension=0, tiled=True)


def forward_block(values, weights, lag_masks):
    (
        gelu_weight,
        lru_weight,
        rate_weight,
        input_weight,
        rate_bias,
        input_bias,
        decay_param,
        filter_taps,
        filter_bias,
        out_weight,
        gate_weight,
        up_weight,
        down_weight,
        norm_first,
        norm_second,
    ) = weights
    scale_one = lax.rsqrt(jnp.mean(values * values, axis=1, keepdims=True) + epsilon)
    rows_one = spread_rows(
        (values * scale_one * norm_first.astype(jnp.float32)).astype(jnp.bfloat16)
    )
    group_rows = rows_one.shape[0]
    pre_branch = jnp.dot(rows_one, gelu_weight, preferred_element_type=jnp.float32)
    branch = jax.nn.gelu(pre_branch)
    feature = jnp.dot(rows_one, lru_weight, preferred_element_type=jnp.float32)
    tap_weights = filter_taps.astype(jnp.float32).reshape(filter_taps.shape[0], -1)
    filtered = filter_bias.astype(jnp.float32).reshape(-1)
    for offset in range(tap_weights.shape[0]):
        filtered = filtered + tap_weights[offset] * lag_rows(feature, offset) * lag_masks[offset]
    conv_low = filtered.astype(jnp.bfloat16)
    conv_val = widen(conv_low)
    local_blocks, block_width = (rate_weight.shape[0], rate_weight.shape[1])
    blocks = conv_low.reshape(group_rows, local_blocks, block_width)
    pre_rate = jnp.einsum(
        "gkc,kcd->gkd", blocks, rate_weight, preferred_element_type=jnp.float32
    ) + rate_bias.astype(jnp.float32)
    pre_input = jnp.einsum(
        "gkc,kcd->gkd", blocks, input_weight, preferred_element_type=jnp.float32
    ) + input_bias.astype(jnp.float32)
    rate_gate = jax.nn.sigmoid(pre_rate).reshape(group_rows, -1)
    input_gate = jax.nn.sigmoid(pre_input).reshape(group_rows, -1)
    forget = jax.nn.softplus(-decay_param.astype(jnp.float32)).reshape(-1)
    decay_rate = jnp.exp(-8.0 * rate_gate * forget)
    spare_room = 1.0 - decay_rate * decay_rate
    scale_in = jnp.sqrt(jnp.maximum(spare_room, floor_value))
    carry_decay = decay_rate * lag_masks[1]
    hidden_state = lax.associative_scan(
        chain_combine, (carry_decay, scale_in * input_gate * conv_val)
    )[1]
    mixed_low = (hidden_state * branch).astype(jnp.bfloat16)
    middle = values + collect_rows(
        jnp.dot(mixed_low, out_weight, preferred_element_type=jnp.float32)
    )
    scale_two = lax.rsqrt(jnp.mean(middle * middle, axis=1, keepdims=True) + epsilon)
    rows_two = spread_rows(
        (middle * scale_two * norm_second.astype(jnp.float32)).astype(jnp.bfloat16)
    )
    pre_gate = jnp.dot(rows_two, gate_weight, preferred_element_type=jnp.float32)
    pre_up = jnp.dot(rows_two, up_weight, preferred_element_type=jnp.float32)
    hidden = (jax.nn.gelu(pre_gate) * pre_up).astype(jnp.bfloat16)
    result = middle + collect_rows(jnp.dot(hidden, down_weight, preferred_element_type=jnp.float32))
    kept_values = (
        values,
        scale_one,
        rows_one,
        pre_branch,
        branch,
        feature,
        conv_low,
        rate_gate,
        input_gate,
        forget,
        decay_rate,
        spare_room,
        scale_in,
        carry_decay,
        hidden_state,
        mixed_low,
        middle,
        scale_two,
        rows_two,
        pre_gate,
        pre_up,
        hidden,
    )
    return (result, kept_values)


def backward_feed(incoming, kept_values, weights):
    (
        gelu_weight,
        lru_weight,
        rate_weight,
        input_weight,
        rate_bias,
        input_bias,
        decay_param,
        filter_taps,
        filter_bias,
        out_weight,
        gate_weight,
        up_weight,
        down_weight,
        norm_first,
        norm_second,
    ) = weights
    (
        values,
        scale_one,
        rows_one,
        pre_branch,
        branch,
        feature,
        conv_low,
        rate_gate,
        input_gate,
        forget,
        decay_rate,
        spare_room,
        scale_in,
        carry_decay,
        hidden_state,
        mixed_low,
        middle,
        scale_two,
        rows_two,
        pre_gate,
        pre_up,
        hidden,
    ) = kept_values
    grad_low = spread_grads(incoming.astype(jnp.bfloat16))
    grad_down = contract_rows(hidden, grad_low)
    grad_hidden = contract_cols(grad_low, down_weight)
    act_gate, gelu_pull = jax.vjp(jax.nn.gelu, pre_gate)
    gate_low = gelu_pull(grad_hidden * pre_up)[0].astype(jnp.bfloat16)
    up_low = (grad_hidden * act_gate).astype(jnp.bfloat16)
    grad_gate = contract_rows(rows_two, gate_low)
    grad_up = contract_rows(rows_two, up_low)
    normed_grad = collect_grads(
        contract_cols(gate_low, gate_weight) + contract_cols(up_low, up_weight)
    )
    grad_norm_two = jnp.sum(normed_grad * middle * scale_two, axis=0)
    grad_middle = incoming + rms_back(
        normed_grad * norm_second.astype(jnp.float32), middle, scale_two
    )
    return (grad_middle, (grad_gate, grad_up, grad_down, grad_norm_two))


def backward_mixer(grad_middle, kept_values, weights, lag_masks):
    (
        gelu_weight,
        lru_weight,
        rate_weight,
        input_weight,
        rate_bias,
        input_bias,
        decay_param,
        filter_taps,
        filter_bias,
        out_weight,
        gate_weight,
        up_weight,
        down_weight,
        norm_first,
        norm_second,
    ) = weights
    (
        values,
        scale_one,
        rows_one,
        pre_branch,
        branch,
        feature,
        conv_low,
        rate_gate,
        input_gate,
        forget,
        decay_rate,
        spare_room,
        scale_in,
        carry_decay,
        hidden_state,
        mixed_low,
        middle,
        scale_two,
        rows_two,
        pre_gate,
        pre_up,
        hidden,
    ) = kept_values
    group_rows = rows_one.shape[0]
    local_blocks, block_width = (rate_weight.shape[0], rate_weight.shape[1])
    shape_pair = (local_blocks, block_width)
    conv_val = widen(conv_low)
    middle_low = spread_grads(grad_middle.astype(jnp.bfloat16))
    grad_out_weight = contract_rows(mixed_low, middle_low)
    grad_mixed = contract_cols(middle_low, out_weight)
    grad_state = grad_mixed * branch
    _, branch_pull = jax.vjp(jax.nn.gelu, pre_branch)
    branch_low = branch_pull(grad_mixed * hidden_state)[0].astype(jnp.bfloat16)
    next_decay = lead_rows(carry_decay, 1)
    grad_drive = lax.associative_scan(chain_combine, (next_decay, grad_state), reverse=True)[1]
    grad_decay = grad_drive * lag_rows(hidden_state, 1) * lag_masks[1]
    grad_scale = grad_drive * input_gate * conv_val
    grad_spare = jnp.where(spare_room > floor_value, 0.5 * grad_scale / scale_in, 0.0)
    grad_decay = grad_decay - 2.0 * decay_rate * grad_spare
    grad_log = grad_decay * decay_rate
    rate_low = (grad_log * (-8.0 * forget) * rate_gate * (1.0 - rate_gate)).astype(jnp.bfloat16)
    input_low = (grad_drive * scale_in * conv_val * input_gate * (1.0 - input_gate)).astype(
        jnp.bfloat16
    )
    grad_forget = jnp.sum(grad_log * (-8.0 * rate_gate), axis=0)
    grad_decay_param = -grad_forget * jax.nn.sigmoid(-decay_param.astype(jnp.float32)).reshape(-1)
    conv_blocks = conv_low.reshape(group_rows, local_blocks, block_width)
    rate_blocks = rate_low.reshape(group_rows, local_blocks, block_width)
    input_blocks = input_low.reshape(group_rows, local_blocks, block_width)
    grad_rate_weight = jnp.einsum(
        "gkc,gkd->kcd", conv_blocks, rate_blocks, preferred_element_type=jnp.float32
    )
    grad_input_weight = jnp.einsum(
        "gkc,gkd->kcd", conv_blocks, input_blocks, preferred_element_type=jnp.float32
    )
    grad_rate_bias = jnp.sum(rate_low.astype(jnp.float32), axis=0)
    grad_input_bias = jnp.sum(input_low.astype(jnp.float32), axis=0)
    back_gates = jnp.einsum(
        "gkd,kcd->gkc", rate_blocks, rate_weight, preferred_element_type=jnp.float32
    )
    back_gates = back_gates + jnp.einsum(
        "gkd,kcd->gkc", input_blocks, input_weight, preferred_element_type=jnp.float32
    )
    grad_conv = grad_drive * scale_in * input_gate + back_gates.reshape(group_rows, -1)
    tap_weights = filter_taps.astype(jnp.float32).reshape(filter_taps.shape[0], -1)
    grad_taps = []
    grad_feature = jnp.zeros_like(feature)
    for offset in range(tap_weights.shape[0]):
        masked = grad_conv * lag_masks[offset]
        grad_taps.append(jnp.sum(masked * lag_rows(feature, offset), axis=0))
        grad_feature = grad_feature + lead_rows(masked, offset) * tap_weights[offset]
    grad_filter_bias = jnp.sum(grad_conv, axis=0)
    feature_low = grad_feature.astype(jnp.bfloat16)
    grad_gelu_weight = contract_rows(rows_one, branch_low)
    grad_lru_weight = contract_rows(rows_one, feature_low)
    first_grad = collect_grads(
        contract_cols(branch_low, gelu_weight) + contract_cols(feature_low, lru_weight)
    )
    grad_norm_one = jnp.sum(first_grad * values * scale_one, axis=0)
    grad_values = grad_middle + rms_back(
        first_grad * norm_first.astype(jnp.float32), values, scale_one
    )
    grads = (
        grad_gelu_weight,
        grad_lru_weight,
        grad_rate_weight,
        grad_input_weight,
        grad_rate_bias.reshape(shape_pair),
        grad_input_bias.reshape(shape_pair),
        grad_decay_param.reshape(shape_pair),
        jnp.stack(grad_taps).reshape((tap_weights.shape[0],) + shape_pair),
        grad_filter_bias.reshape(shape_pair),
        grad_out_weight,
        grad_norm_one,
    )
    return (grad_values, grads)


def add_tuples(left_tuple, right_tuple):
    if left_tuple is None:
        return right_tuple
    return tuple(
        (left_total + right_total for left_total, right_total in zip(left_tuple, right_tuple))
    )


def shards(
    inputs,
    out_grad,
    lengths,
    order,
    gelu_weight,
    lru_weight,
    rate_weight,
    input_weight,
    rate_bias,
    input_bias,
    decay_param,
    filter_taps,
    filter_bias,
    out_weight,
    gate_weight,
    up_weight,
    down_weight,
    norm_first,
    norm_second,
):
    group_id = lax.axis_index("dp")
    group_count = lax.axis_size("dp")
    slot_ids = jnp.arange(group_count, dtype=jnp.int32)
    source_of = jnp.sum(jnp.where(order == group_id, slot_ids[None, :], 0), axis=1, dtype=jnp.int32)
    micro = inputs.shape[0]
    dealt_inputs, dealt_cotangent = inputs, out_grad
    dealt_lengths = lax.dynamic_index_in_dim(lengths, group_id, 1, keepdims=False)
    vectors = jnp.concatenate([rate_bias[0].reshape(-1), input_bias[0].reshape(-1), decay_param[0].reshape(-1),
        filter_taps[0].reshape(-1), filter_bias[0].reshape(-1)]).reshape(1, 256)
    gains = jnp.concatenate([norm_first[0], norm_second[0], jnp.zeros((160,), jnp.bfloat16)]).reshape(1, 256)
    gates = jnp.concatenate([rate_weight[0].reshape(32, 128), input_weight[0].reshape(32, 128)], axis=1)
    small = jnp.concatenate([gates, vectors, gains, jnp.zeros((14, 256), jnp.bfloat16)], axis=0)
    shard = jnp.concatenate([small, gelu_weight[0], lru_weight[0], out_weight[0].T, gate_weight[0], up_weight[0], down_weight[0].T], axis=1)
    pieces = shard.reshape(48, 8, 1280).transpose(1, 0, 2)
    whole = gather(pieces).reshape(8, 1536, 1280).transpose(1, 0, 2).reshape(1536, 10240)
    small = whole[:, :256].reshape(32, 48, 256)
    def unblock(part):
        return part.reshape(32, 8, 4, 128).transpose(1, 0, 2, 3).reshape(8, 128, 128)
    vec = small[:, 32].reshape(32, 8, 8, 4).transpose(1, 2, 0, 3).reshape(8, 8, 128)
    weights = (
        whole[:, 256:1280],
        whole[:, 1280:2304],
        unblock(small[:, :32, :128]),
        unblock(small[:, :32, 128:]),
        vec[0], vec[1], vec[2], vec[3:7], vec[7],
        whole[:, 2304:3328].T,
        whole[:, 3328:5632],
        whole[:, 5632:7936],
        whole[:, 7936:10240].T,
        small[:, 33, 0:48].reshape(1536),
        small[:, 33, 48:96].reshape(1536),
    )
    section_id = lax.axis_index("section")
    on_first = section_id == 0
    group_rows = inputs.shape[1] * lax.axis_size("tensor")
    tap_count = filter_taps.shape[1]
    received = jnp.zeros(inputs.shape[1:], jnp.bfloat16)
    forward_outs = []
    kept_all = []
    for moment in range(micro + 1):
        index_now = jnp.clip(moment - section_id, 0, micro - 1)
        doc_lengths = lax.dynamic_index_in_dim(dealt_lengths, index_now, 0, keepdims=False)
        lag_masks = document_masks(doc_lengths, group_rows, tap_count)
        start_rows = jnp.where(on_first, dealt_inputs[min(moment, micro - 1)], received).astype(
            jnp.float32
        )
        result, kept_values = forward_block(start_rows, weights, lag_masks)
        low_result = result.astype(jnp.bfloat16)
        forward_outs.append(result)
        kept_all.append((kept_values, tuple(lag_masks)))
        if moment < micro:
            received = from_behind(low_result, "section", 1)
    own_out = jnp.stack(
        [
            jnp.where(on_first, forward_outs[number], forward_outs[number + 1])
            for number in range(micro)
        ]
    ).astype(jnp.bfloat16)
    every_out = lax.all_gather(own_out, "dp", axis=0, tiled=False)
    hidden_out = jnp.stack(
        [lax.dynamic_index_in_dim(every_out[:, m], source_of[m], 0, keepdims=False) for m in range(micro)]
    ).astype(jnp.float32)[None]
    back_weights = weights

    def select(first_value, second_value):
        return jnp.where(on_first, first_value, second_value)

    back_received = jnp.zeros(inputs.shape[1:], jnp.bfloat16)
    feed_totals = None
    mixer_totals = None
    input_grads = []
    for period in range(micro + 1):
        kept_pair = jax.tree.map(
            select, kept_all[max(period - 1, 0)], kept_all[min(period + 1, micro)]
        )
        supplied = dealt_cotangent[min(period, micro - 1)].astype(jnp.float32) * (
            1.0 if period < micro else 0.0
        )
        incoming = jnp.where(on_first, back_received.astype(jnp.float32), supplied)
        grad_middle, feed_grads = backward_feed(incoming, kept_pair[0], back_weights)
        feed_totals = add_tuples(feed_totals, feed_grads)
        grad_values, mixer_grads = backward_mixer(
            grad_middle, kept_pair[0], back_weights, list(kept_pair[1])
        )
        mixer_totals = add_tuples(mixer_totals, mixer_grads)
        input_grads.append(grad_values)
        if period < micro:
            back_received = from_behind(grad_values.astype(jnp.bfloat16), "section", -1)
    dealt_back = jnp.stack(
        [
            jnp.where(on_first, input_grads[number + 1], input_grads[number])
            for number in range(micro)
        ]
    )
    input_grad = dealt_back[None]
    reduced = (
        lax.psum_scatter(mixer_totals[0].astype(jnp.bfloat16), "dp", scatter_dimension=0, tiled=True).astype(jnp.float32),
        lax.psum_scatter(mixer_totals[1].astype(jnp.bfloat16), "dp", scatter_dimension=0, tiled=True).astype(jnp.float32),
        lax.psum_scatter(mixer_totals[2].astype(jnp.bfloat16), "dp", scatter_dimension=1, tiled=True).astype(jnp.float32),
        lax.psum_scatter(mixer_totals[3].astype(jnp.bfloat16), "dp", scatter_dimension=1, tiled=True).astype(jnp.float32),
        lax.psum_scatter(mixer_totals[4].astype(jnp.bfloat16), "dp", scatter_dimension=1, tiled=True).astype(jnp.float32),
        lax.psum_scatter(mixer_totals[5].astype(jnp.bfloat16), "dp", scatter_dimension=1, tiled=True).astype(jnp.float32),
        lax.psum_scatter(mixer_totals[6].astype(jnp.bfloat16), "dp", scatter_dimension=1, tiled=True).astype(jnp.float32),
        lax.psum_scatter(mixer_totals[7].astype(jnp.bfloat16), "dp", scatter_dimension=2, tiled=True).astype(jnp.float32),
        lax.psum_scatter(mixer_totals[8].astype(jnp.bfloat16), "dp", scatter_dimension=1, tiled=True).astype(jnp.float32),
        lax.psum_scatter(mixer_totals[9].astype(jnp.bfloat16), "dp", scatter_dimension=1, tiled=True).astype(jnp.float32),
        lax.psum_scatter(feed_totals[0].astype(jnp.bfloat16), "dp", scatter_dimension=0, tiled=True).astype(jnp.float32),
        lax.psum_scatter(feed_totals[1].astype(jnp.bfloat16), "dp", scatter_dimension=0, tiled=True).astype(jnp.float32),
        lax.psum_scatter(feed_totals[2].astype(jnp.bfloat16), "dp", scatter_dimension=1, tiled=True).astype(jnp.float32),
        lax.psum_scatter(mixer_totals[10].astype(jnp.bfloat16), "dp", scatter_dimension=0, tiled=True).astype(jnp.float32),
        lax.psum_scatter(feed_totals[3].astype(jnp.bfloat16), "dp", scatter_dimension=0, tiled=True).astype(jnp.float32),
    )
    gain_totals = lax.psum((reduced[13], reduced[14]), "tensor")
    return (
        (hidden_out, input_grad)
        + tuple((member[None] for member in reduced[:13]))
        + (gain_totals[0][None], gain_totals[1][None])
    )


def solution(mesh):
    placed = (
        P(None, ("dp", "tensor"), None),
        P(None, ("dp", "tensor"), None),
        P(),
        P(),
        P("section", "dp", "tensor"),
        P("section", "dp", "tensor"),
        P("section", "tensor", "dp", None),
        P("section", "tensor", "dp", None),
        P("section", "tensor", "dp"),
        P("section", "tensor", "dp"),
        P("section", "tensor", "dp"),
        P("section", None, "tensor", "dp"),
        P("section", "tensor", "dp"),
        P("section", "tensor", "dp"),
        P("section", "dp", "tensor"),
        P("section", "dp", "tensor"),
        P("section", "tensor", "dp"),
        P("section", "dp"),
        P("section", "dp"),
    )
    return jax.shard_map(
        shards,
        mesh=mesh,
        in_specs=placed,
        out_specs=(
            P("section", None, ("dp", "tensor"), None),
            P("section", None, ("dp", "tensor"), None),
            P("section", "dp", "tensor"),
            P("section", "dp", "tensor"),
            P("section", "tensor", "dp", None),
            P("section", "tensor", "dp", None),
            P("section", "tensor", "dp"),
            P("section", "tensor", "dp"),
            P("section", "tensor", "dp"),
            P("section", None, "tensor", "dp"),
            P("section", "tensor", "dp"),
            P("section", "tensor", "dp"),
            P("section", "dp", "tensor"),
            P("section", "dp", "tensor"),
            P("section", "tensor", "dp"),
            P("section", "dp"),
            P("section", "dp"),
        ),
        check_vma=False,
    )
```

```python
import jax
import jax.numpy as jnp
from jax import lax
from jax.experimental import pallas as pl
from jax.experimental.pallas import tpu as pltpu
from jax.sharding import PartitionSpec as P

MESH = pl.DeviceIdType.MESH
F32 = jnp.float32
BF16 = jnp.bfloat16
EPS = 1e-06
FLOOR = 0.01
PIECES = 20
PW = 512
TILE = 256
HALF = 144
ALL = 288
D = 1536
QUARTER = 384
VMEM_LIMIT = 62 * 2**20


def nn(a, b):
    return lax.dot_general(a, b, (((1,), (0,)), ((), ())), preferred_element_type=F32)


def nt(a, b):
    return lax.dot_general(a, b, (((1,), (1,)), ((), ())), preferred_element_type=F32)


def tn(a, b):
    return lax.dot_general(a, b, (((0,), (0,)), ((), ())), preferred_element_type=F32)


def gelu_parts(v):
    k = 0.7978845608028654
    th = jnp.tanh(k * (v + 0.044715 * v * v * v))
    half = 0.5 * (1.0 + th)
    slope = half + 0.5 * v * (1.0 - th * th) * (k * (1.0 + 0.134145 * v * v))
    return v * half, slope


def gelu(v):
    k = 0.7978845608028654
    return 0.5 * v * (1.0 + jnp.tanh(k * (v + 0.044715 * v * v * v)))


def sigmoid(v):
    return 1.0 / (1.0 + jnp.exp(-v))


def softplus(v):
    return jnp.maximum(v, 0.0) + jnp.log(1.0 + jnp.exp(-jnp.abs(v)))


def to_natural(v):
    return jnp.concatenate([v[0:72], v[144:216], v[72:144], v[216:288]], axis=0)


def to_exchange(v):
    return jnp.concatenate([v[0:72], v[144:216], v[72:144], v[216:288]], axis=0)


def down(v, k):
    return pltpu.roll(v, k, 0) if k else v


def up(v, k):
    return pltpu.roll(v, ALL - k, 0) if k else v


def scan_down(a, b):
    for s in (1, 2, 4, 8, 16, 32, 64):
        b = a * down(b, s) + b
        if s < 64:
            a = a * down(a, s)
    return b


def scan_up(a, b):
    for s in (1, 2, 4, 8, 16, 32, 64):
        b = a * up(b, s) + b
        if s < 64:
            a = a * up(a, s)
    return b


def iota(shape, dim):
    return lax.broadcasted_iota(jnp.int32, shape, dim)


def onehot(cond):
    return jnp.where(cond, 1.0, 0.0).astype(BF16)


class Ring:
    def __init__(self):
        dp = lax.axis_index("dp")
        c, z, x = dp % 2, (dp // 2) % 4, dp // 8
        self.dp, self.c, self.z, self.x = dp, c, z, x

        def at(dx, dz):
            return ((x + dx) % 4) * 8 + ((z + dz) % 4) * 2 + c

        self.ap, self.am = at(1 - c, c), at(3 * (1 - c), 3 * c)
        self.bp, self.bm = at(c, 1 - c), at(3 * c, 3 * (1 - c))
        self.sib = dp + 1 - 2 * c

    def by_colour(self, fn):
        @pl.when(self.c == 0)
        def _():
            fn(0)

        @pl.when(self.c == 1)
        def _():
            fn(1)


def by_parity(k, fn):
    @pl.when(k % 2 == 0)
    def _():
        fn(0)

    @pl.when(k % 2 == 1)
    def _():
        fn(1)


def go(src, dst, dev, ssem, rsem):
    return pltpu.make_async_remote_copy(
        src_ref=src, dst_ref=dst, send_sem=ssem, recv_sem=rsem, device_id=dev, device_id_type=MESH
    )


def gather_weights(ring, g_ref, sems):
    s1s, s1r, s2s, s2r, s3s, s3r = sems
    c, x, z = ring.c, ring.x, ring.z
    K = PIECES

    def send(r, dev, ssem, rsem):
        return go(r, r, {"dp": dev}, ssem, rsem)

    def one(k, j):
        return g_ref.at[k, (x + j * (1 - c)) % 4, (z + j * c) % 4, c]

    def p1(k, j, recv):
        if j == 0:
            return send(one(k, 3 if recv else 0), ring.ap, s1s.at[k, 0], s1r.at[k, 0])
        return send(one(k, 1 if recv else 0), ring.am, s1s.at[k, 1], s1r.at[k, 1])

    def p1f(k, par, recv):
        if par == 0:
            return send(one(k, 2 if recv else 3), ring.ap, s1s.at[k, 2], s1r.at[k, 2])
        return send(one(k, 2 if recv else 1), ring.am, s1s.at[k, 2], s1r.at[k, 2])

    def row(k, j, col):
        if col == 0:
            return g_ref.at[k, :, (z + j) % 4, 0]
        return g_ref.at[k, (x + j) % 4, :, 1]

    def p2(k, j, recv, col):
        if j == 0:
            return send(row(k, 3 if recv else 0, col), ring.bp, s2s.at[k, 0], s2r.at[k, 0])
        return send(row(k, 1 if recv else 0, col), ring.bm, s2s.at[k, 1], s2r.at[k, 1])

    def p2f(k, par, recv, col):
        if par == 0:
            return send(row(k, 2 if recv else 3, col), ring.bp, s2s.at[k, 2], s2r.at[k, 2])
        return send(row(k, 2 if recv else 1, col), ring.bm, s2s.at[k, 2], s2r.at[k, 2])

    def sb(k, j, col):
        return send(row(k, j, col), ring.sib, s3s.at[k, j], s3r.at[k, j])

    def step(t, carry):
        @pl.when(t < K)
        def _():
            p1(t, 0, False).start()
            p1(t, 1, False).start()

        @pl.when(jnp.logical_and(t >= 1, t - 1 < K))
        def _():
            k = t - 1

            def f(par):
                p1(k, par, True).wait_recv()
                p1f(k, par, False).start()
                p1(k, 1 - par, True).wait_recv()

            by_parity(k, f)

        @pl.when(jnp.logical_and(t >= 2, t - 2 < K))
        def _():
            k = t - 2
            by_parity(k, lambda par: p1f(k, par, True).wait_recv())

            def f(col):
                p2(k, 0, False, col).start()
                p2(k, 1, False, col).start()
                sb(k, 0, col).start()

            ring.by_colour(f)

        @pl.when(jnp.logical_and(t >= 3, t - 3 < K))
        def _():
            k = t - 3

            def f(col):
                def h(par):
                    p2(k, par, True, col).wait_recv()
                    p2f(k, par, False, col).start()
                    p2(k, 1 - par, True, col).wait_recv()

                by_parity(k, h)
                sb(k, 1, col).start()
                sb(k, 3, col).start()

            ring.by_colour(f)

        @pl.when(t >= 4)
        def _():
            k = t - 4

            def f(col):
                by_parity(k, lambda par: p2f(k, par, True, col).wait_recv())
                sb(k, 2, col).start()

            ring.by_colour(f)

        return carry

    lax.fori_loop(0, K + 4, step, 0)

    def finish(k, carry):
        p1(k, 0, False).wait_send()
        p1(k, 1, False).wait_send()
        by_parity(k, lambda par: p1f(k, par, False).wait_send())

        def f(col):
            p2(k, 0, False, col).wait_send()
            p2(k, 1, False, col).wait_send()
            by_parity(k, lambda par: p2f(k, par, False, col).wait_send())
            for j in range(4):
                sb(k, j, col).wait_send()
                send(row(k, j, 1 - col), ring.sib, s3s.at[k, j], s3r.at[k, j]).wait_recv()

        ring.by_colour(f)
        return carry

    lax.fori_loop(0, K, finish, 0)


def chain_kernel(
    shard_ref, xin_ref, ein_ref, mask_ref,
    res_out, grad_out, left_out, right_out, small_out,
    g_ref, xb, left, right, pf, cv, rg, ig, st, mid, own, sb, rb, gmid, rw, vec, vgrad, gains, gsum, gpart, sgrad, acc,
    lsem, psem_s, psem_r, *gsems,
):
    sec = lax.axis_index("section")
    t = lax.axis_index("tensor")
    ring = Ring()
    barrier = pltpu.get_barrier_semaphore()
    others = [{"dp": d} for d in (ring.ap, ring.am, ring.bp, ring.bm, ring.sib)] + [{"tensor": 1 - t}, {"section": 1 - sec}]
    for dev in others:
        pl.semaphore_signal(barrier, inc=1, device_id=dev, device_id_type=MESH)
    load = pltpu.make_async_copy(shard_ref, g_ref.at[:, ring.x, ring.z, ring.c], lsem.at[0])
    load.start()
    pl.semaphore_wait(barrier, 7)
    load.wait()

    my = pl.ds(pl.multiple_of(t * HALF, 16), HALF)
    his = pl.ds(pl.multiple_of((1 - t) * HALF, 16), HALF)

    def pair(src, dst, i):
        return go(src, dst, {"tensor": 1 - t}, psem_s.at[i], psem_r.at[i])

    def share(li, i):
        return pair(left.at[li, my], left.at[li, my], i)

    def shared(li, i):
        return pair(left.at[li, his], left.at[li, his], i)

    def hand(src, dst, i):
        return go(src, dst, {"section": 1 - sec}, psem_s.at[i], psem_r.at[i])

    def back_piece(x):
        return hand(sb.at[x], left.at[3, my, pl.ds(x * QUARTER, QUARTER)], 22 + x)

    @pl.when(sec == 1)
    def _():
        left[3, my, :] = ein_ref[...]
        share(3, 10).start()

    gather_weights(ring, g_ref, gsems)

    def wt(T):
        k, off = T // 2, pl.multiple_of((T % 2) * TILE, TILE)
        return g_ref[k, :, :, :, :, pl.ds(off, TILE)].reshape(D, TILE)

    def wq(T, x):
        k, off = T // 2, pl.multiple_of((T % 2) * TILE, TILE)
        return g_ref[k, x, :, :, :, pl.ds(off, TILE)].reshape(QUARTER, TILE)

    small = wt(0)

    def unpack(j, carry):
        ci, r = iota((128, D), 0), iota((128, D), 1)
        sel = onehot(r == (ci // 4) * 48 + j * 4 + ci % 4)
        rw[j] = nn(sel, small).astype(BF16)
        return carry

    lax.fori_loop(0, 8, unpack, 0)
    dpi, r = iota((32, D), 0), iota((32, D), 1)
    t32 = nn(onehot(r == dpi * 48 + 32), small).astype(BF16)
    d1 = onehot(iota((32, 128), 1) // 4 == iota((32, 128), 0))
    e1 = tn(t32, d1)
    e1 = jnp.where(iota((256, 128), 0) % 4 == iota((256, 128), 1) % 4, e1, 0.0).astype(BF16)
    v1 = nn(onehot(iota((64, 256), 1) // 4 == iota((64, 256), 0)), e1)
    for i in range(64):
        vec[i] = v1[i:i + 1, :]
    t33 = nn(onehot(r == dpi * 48 + 33), small).astype(BF16)
    d2 = onehot(jnp.logical_and(r >= dpi * 48, r < dpi * 48 + 48))
    e2 = tn(t33[:, 0:128], d2)
    within = iota((128, D), 1) % 48
    q = iota((128, D), 0)
    gains[0] = jnp.sum(jnp.where(q == within, e2, 0.0), axis=0, keepdims=True)
    gains[1] = jnp.sum(jnp.where(q == within + 48, e2, 0.0), axis=0, keepdims=True)

    @pl.when(sec == 0)
    def _():
        xb[...] = xin_ref[...]

    @pl.when(sec == 1)
    def _():
        hand(xb, xb, 21).wait_recv()

    def rows16(i):
        return pl.ds(pl.multiple_of(i * 16, 16), 16)

    def myrows16(i):
        return pl.ds(pl.multiple_of(t * HALF + i * 16, 16), 16)

    def scale_of(v):
        return lax.rsqrt(jnp.mean(v * v, axis=1, keepdims=True) + EPS)

    def norm_one(i, carry):
        v = xb[rows16(i), :].astype(F32)
        left[0, myrows16(i), :] = (v * scale_of(v) * gains[0]).astype(BF16)
        return carry

    lax.fori_loop(0, 9, norm_one, 0)
    share(0, 0).start()

    def into_branches(rows):
        def body(i, carry):
            pf[i, rows, :] = nn(left[0, rows, :], wt(1 + i))
            return carry
        lax.fori_loop(0, 8, body, 0)

    into_branches(my)
    shared(0, 0).wait_recv()
    into_branches(his)

    def vrow(a, j):
        return vec[a * 8 + j]

    def mixer(i, carry):
        for h in range(2):
            j = i * 2 + h
            lanes = slice(h * 128, h * 128 + 128)
            feature = to_natural(pf[4 + i, :, lanes])
            filtered = vrow(7, j)
            for k in range(4):
                filtered = filtered + vrow(3 + k, j) * down(feature, k) * mask_ref[k]
            low = filtered.astype(BF16)
            cv[j] = low
            conv = low.astype(F32)
            pre = nn(low, rw[j])
            rate = sigmoid(pre[:, 0:128] + vrow(0, j))
            inp = sigmoid(pre[:, 128:256] + vrow(1, j))
            rg[j] = rate
            ig[j] = inp
            decay = jnp.exp(-8.0 * rate * softplus(-vrow(2, j)))
            scale_in = jnp.sqrt(jnp.maximum(1.0 - decay * decay, FLOOR))
            state = scan_down(decay * mask_ref[1], scale_in * inp * conv)
            st[j] = state
            right[8 + i, :, lanes] = (to_exchange(state) * gelu(pf[i, :, lanes])).astype(BF16)
        return carry

    lax.fori_loop(0, 4, mixer, 0)

    def reduce_out(terms, base, turn):
        def body(x, carry):
            total = None
            for ri, T in terms:
                part = nt(right[ri], wq(T, x))
                total = part if total is None else total + part
            acc[...] = total
            sb[x] = acc[his, :].astype(BF16)
            pair(sb.at[x], rb.at[turn, x], base + x).start()
            own[x] = acc[my, :]
            return carry

        lax.fori_loop(0, 4, body, 0)
        for x in range(4):
            pair(sb.at[x], rb.at[turn, x], base + x).wait()

    def summed(i, turn):
        rows = rows16(i)
        return jnp.concatenate([own[x, rows, :] + rb[turn, x, rows, :].astype(F32) for x in range(4)], axis=1)

    reduce_out([(8 + i, 9 + i) for i in range(4)], 1, 0)

    def norm_two(i, carry):
        v = xb[rows16(i), :].astype(F32) + summed(i, 0)
        mid[rows16(i), :] = v
        left[2, myrows16(i), :] = (v * scale_of(v) * gains[1]).astype(BF16)
        return carry

    lax.fori_loop(0, 9, norm_two, 0)
    share(2, 5).start()

    def feed(rows):
        def body(i, carry):
            lhs = left[2, rows, :]
            pg = nn(lhs, wt(13 + i))
            pu = nn(lhs, wt(22 + i))
            right[12 + i, rows, :] = pg.astype(BF16)
            right[21 + i, rows, :] = pu.astype(BF16)
            right[30 + i, rows, :] = (gelu(pg) * pu).astype(BF16)
            return carry
        lax.fori_loop(0, 9, body, 0)

    feed(my)
    shared(2, 5).wait_recv()
    feed(his)
    reduce_out([(30 + i, 31 + i) for i in range(9)], 6, 1)

    def finish_forward(i, carry):
        v = mid[rows16(i), :] + summed(i, 1)
        res_out[rows16(i), :] = v.astype(BF16)
        return carry

    lax.fori_loop(0, 9, finish_forward, 0)

    @pl.when(sec == 0)
    def _():
        hand(res_out, xb, 21).start()
        for x in range(4):
            back_piece(x).wait_recv()
        share(3, 10).start()

    shared(3, 10).wait_recv()

    def feed_back(i, carry):
        gh = nn(left[3], wt(31 + i))
        pg = right[12 + i].astype(F32)
        pu = right[21 + i].astype(F32)
        act, slope = gelu_parts(pg)
        right[12 + i] = (gh * pu * slope).astype(BF16)
        right[21 + i] = (gh * act).astype(BF16)
        return carry

    lax.fori_loop(0, 9, feed_back, 0)
    reduce_out([(12 + i, 13 + i) for i in range(18)], 11, 0)

    def eight(v):
        return v[0:8] + v[8:16]

    def middle_back(i, carry):
        ng = summed(i, 0)
        m = mid[rows16(i), :]
        sc = scale_of(m)
        u = ng * gains[1]
        gm = left[3, myrows16(i), :].astype(F32) + sc * u - m * (sc * sc * sc) * jnp.mean(u * m, axis=1, keepdims=True)
        gmid[rows16(i), :] = gm
        left[1, myrows16(i), :] = gm.astype(BF16)
        return carry + eight(ng * m * sc)

    gpart[1] = lax.fori_loop(0, 9, middle_back, jnp.zeros((8, D), F32))
    share(1, 15).start()
    shared(1, 15).wait_recv()

    def mixer_back(i, carry):
        gmix = nn(left[1], wt(9 + i))
        for h in range(2):
            j = i * 2 + h
            lanes = slice(h * 128, h * 128 + 128)
            gm = gmix[:, lanes]
            act, slope = gelu_parts(pf[i, :, lanes])
            state = st[j]
            right[i, :, lanes] = (gm * to_exchange(state) * slope).astype(BF16)
            grad_state = to_natural(gm * act)
            rate, inp = rg[j], ig[j]
            conv = cv[j].astype(F32)
            forget = softplus(-vrow(2, j))
            decay = jnp.exp(-8.0 * rate * forget)
            spare = 1.0 - decay * decay
            scale_in = jnp.sqrt(jnp.maximum(spare, FLOOR))
            m1 = mask_ref[1]
            drive = scan_up(up(decay * m1, 1), grad_state)
            grad_spare = jnp.where(spare > FLOOR, 0.5 * (drive * inp * conv) / scale_in, 0.0)
            grad_decay = drive * down(state, 1) * m1 - 2.0 * decay * grad_spare
            grad_log = grad_decay * decay
            rate_low = (grad_log * (-8.0 * forget) * rate * (1.0 - rate)).astype(BF16)
            driven = drive * scale_in
            input_low = (driven * conv * inp * (1.0 - inp)).astype(BF16)
            both = jnp.concatenate([rate_low, input_low], axis=1)
            back = nt(both, rw[j])
            vgrad[0 * 8 + j] = jnp.sum(rate_low.astype(F32), axis=0, keepdims=True)
            vgrad[1 * 8 + j] = jnp.sum(input_low.astype(F32), axis=0, keepdims=True)
            grad_forget = jnp.sum(grad_log * (-8.0 * rate), axis=0, keepdims=True)
            vgrad[2 * 8 + j] = -grad_forget * sigmoid(-vrow(2, j))
            sgrad[j] = tn(cv[j], both).astype(BF16)
            grad_conv = driven * inp + back
            feature = to_natural(pf[4 + i, :, lanes])
            grad_feature = None
            for k in range(4):
                masked = grad_conv * mask_ref[k] if k else grad_conv
                vgrad[(3 + k) * 8 + j] = jnp.sum(masked * down(feature, k), axis=0, keepdims=True)
                term = up(masked, k) * vrow(3 + k, j)
                grad_feature = term if grad_feature is None else grad_feature + term
            vgrad[7 * 8 + j] = jnp.sum(grad_conv, axis=0, keepdims=True)
            right[4 + i, :, lanes] = to_exchange(grad_feature).astype(BF16)
        return carry

    lax.fori_loop(0, 4, mixer_back, 0)
    reduce_out([(i, 1 + i) for i in range(8)], 16, 1)

    def first_back(i, carry):
        fg = summed(i, 1)
        v = xb[rows16(i), :].astype(F32)
        sc = scale_of(v)
        u = fg * gains[0]
        gv = gmid[rows16(i), :] + sc * u - v * (sc * sc * sc) * jnp.mean(u * v, axis=1, keepdims=True)
        mid[rows16(i), :] = gv
        for x in range(4):
            sb[x, rows16(i), :] = gv[:, x * QUARTER:(x + 1) * QUARTER].astype(BF16)
        return carry + eight(fg * v * sc)

    gpart[0] = lax.fori_loop(0, 9, first_back, jnp.zeros((8, D), F32))

    @pl.when(sec == 1)
    def _():
        for x in range(4):
            back_piece(x).start()

    pair(gpart, gsum, 20).start()
    grad_copy = pltpu.make_async_copy(mid, grad_out, lsem.at[1])
    left_copy = pltpu.make_async_copy(left, left_out, lsem.at[2])
    right_copy = pltpu.make_async_copy(right, right_out, lsem.at[3])
    grad_copy.start()
    left_copy.start()
    right_copy.start()

    v2 = jnp.concatenate([vgrad[i] for i in range(64)], axis=0).astype(BF16)
    e2 = nn(onehot(iota((256, 64), 0) // 4 == iota((256, 64), 1)), v2)
    e2 = jnp.where(iota((256, 128), 0) % 4 == iota((256, 128), 1) % 4, e2, 0.0).astype(BF16)
    t32 = nt(d1, e2).astype(BF16)
    pair(gpart, gsum, 20).wait()
    n1 = jnp.sum(gpart[0] + gsum[0], axis=0, keepdims=True)
    n2 = jnp.sum(gpart[1] + gsum[1], axis=0, keepdims=True)
    spread = jnp.where(q == within, n1, jnp.where(q == within + 48, n2, 0.0)).astype(BF16)
    t33 = nt(d2, spread).astype(BF16)
    t33 = jnp.concatenate([t33, jnp.zeros((32, 128), BF16)], axis=1)

    def pack(x, carry):
        r = iota((QUARTER, 128), 0) + x * QUARTER
        ci = iota((QUARTER, 128), 1)
        total = None
        for j in range(8):
            sel = onehot(r == (ci // 4) * 48 + j * 4 + ci % 4)
            part = nn(sel, sgrad[j])
            total = part if total is None else total + part
        r = iota((QUARTER, 32), 0) + x * QUARTER
        dpi = iota((QUARTER, 32), 1)
        total = total + nn(onehot(r == dpi * 48 + 32), t32) + nn(onehot(r == dpi * 48 + 33), t33)
        small_out[pl.ds(pl.multiple_of(x * QUARTER, 16), QUARTER), :] = total.astype(BF16)
        return carry

    lax.fori_loop(0, 4, pack, 0)

    for li, i in ((0, 0), (2, 5), (3, 10), (1, 15)):
        share(li, i).wait_send()

    @pl.when(sec == 0)
    def _():
        hand(res_out, xb, 21).wait_send()

    @pl.when(sec == 1)
    def _():
        for x in range(4):
            back_piece(x).wait_send()

    grad_copy.wait()
    left_copy.wait()
    right_copy.wait()


def chain(shard, xin, ein, masks):
    K = PIECES
    dma = pltpu.SemaphoreType.DMA
    vmem = pl.BlockSpec(memory_space=pltpu.VMEM)
    hbm = pl.BlockSpec(memory_space=pl.ANY)
    sds = jax.ShapeDtypeStruct
    return pl.pallas_call(
        chain_kernel,
        name="chain",
        out_shape=(
            sds((HALF, D), BF16), sds((HALF, D), F32), sds((4, ALL, D), BF16),
            sds((39, ALL, TILE), BF16), sds((D, TILE), BF16),
        ),
        in_specs=[hbm, vmem, vmem, vmem],
        out_specs=(vmem, hbm, hbm, hbm, vmem),
        scratch_shapes=[
            pltpu.VMEM((K, 4, 4, 2, 48, PW), BF16),
            pltpu.VMEM((HALF, D), BF16),
            pltpu.VMEM((4, ALL, D), BF16),
            pltpu.VMEM((39, ALL, TILE), BF16),
            pltpu.VMEM((8, ALL, TILE), F32),
            pltpu.VMEM((8, ALL, 128), BF16),
            pltpu.VMEM((8, ALL, 128), F32),
            pltpu.VMEM((8, ALL, 128), F32),
            pltpu.VMEM((8, ALL, 128), F32),
            pltpu.VMEM((HALF, D), F32),
            pltpu.VMEM((4, HALF, QUARTER), F32),
            pltpu.VMEM((4, HALF, QUARTER), BF16),
            pltpu.VMEM((2, 4, HALF, QUARTER), BF16),
            pltpu.VMEM((HALF, D), F32),
            pltpu.VMEM((8, 128, 256), BF16),
            pltpu.VMEM((64, 1, 128), F32),
            pltpu.VMEM((64, 1, 128), F32),
            pltpu.VMEM((2, 1, D), F32),
            pltpu.VMEM((2, 8, D), F32),
            pltpu.VMEM((2, 8, D), F32),
            pltpu.VMEM((8, 128, 256), BF16),
            pltpu.VMEM((ALL, QUARTER), F32),
            dma((4,)), dma((26,)), dma((26,)),
            dma((K, 3)), dma((K, 3)), dma((K, 3)), dma((K, 3)), dma((K, 4)), dma((K, 4)),
        ],
        compiler_params=pltpu.CompilerParams(
            collective_id=1, has_side_effects=True, vmem_limit_bytes=VMEM_LIMIT
        ),
    )(shard, xin, ein, masks)


def document_masks(doc_lengths):
    ends = jnp.cumsum(doc_lengths, axis=-1, dtype=jnp.int32)
    position = jnp.arange(HALF, dtype=jnp.int32)
    ident = jnp.sum((position[None, :, None] >= ends[:, None, :]).astype(jnp.int32), axis=-1, dtype=jnp.int32)
    masks = []
    for offset in range(4):
        before = jnp.pad(ident, ((0, 0), (offset, 0)), constant_values=-1)[:, :HALF]
        masks.append((before == ident).astype(F32).reshape(ALL, 1))
    return jnp.broadcast_to(jnp.stack(masks), (4, ALL, 128))


def pack_shard(gelu_weight, lru_weight, rate_weight, input_weight, rate_bias, input_bias, decay_param,
               filter_taps, filter_bias, out_weight, gate_weight, up_weight, down_weight, norm_first, norm_second):
    vectors = jnp.concatenate([v[0].reshape(-1) for v in (rate_bias, input_bias, decay_param, filter_taps, filter_bias)]).reshape(1, 256)
    gains = jnp.concatenate([norm_first[0], norm_second[0], jnp.zeros((160,), BF16)]).reshape(1, 256)
    gates = jnp.concatenate([rate_weight[0].reshape(32, 128), input_weight[0].reshape(32, 128)], axis=1)
    small = jnp.concatenate([gates, vectors, gains, jnp.zeros((14, 256), BF16)], axis=0)
    shard = jnp.concatenate(
        [small, gelu_weight[0], lru_weight[0], out_weight[0].T, gate_weight[0], up_weight[0], down_weight[0].T], axis=1
    )
    return shard.reshape(48, PIECES, PW).transpose(1, 0, 2)


def reduce_kernel(
    left_ref, right_ref, small_ref, out_ref,
    leftt, pp, r0, hh, tt, h2, uu, sbs, sbr, s1s, s1r, s2s, s2r,
):
    ring = Ring()
    c, x, z = ring.c, ring.x, ring.z
    K = PIECES
    barrier = pltpu.get_barrier_semaphore()
    for dev in (ring.ap, ring.am, ring.bp, ring.bm, ring.sib):
        pl.semaphore_signal(barrier, inc=1, device_id={"dp": dev}, device_id_type=MESH)

    def send(src, dst, dev, ssem, rsem):
        return go(src, dst, {"dp": dev}, ssem, rsem)

    def turn_left(li):
        def body(i, carry):
            cols = pl.ds(pl.multiple_of(i * 128, 128), 128)
            leftt[li, cols, :] = left_ref[li, :, cols].T
            return carry
        lax.fori_loop(0, 12, body, 0)

    def one(k, j):
        return k, (x + j * (1 - c)) % 4, (z + j * c) % 4

    def row(k, j, col):
        if col == 0:
            return k, slice(None), (z + j) % 4
        return k, (x + j) % 4

    def sib(k, col):
        return send(pp.at[k % 2, :, :, 1 - col], r0.at[k], ring.sib, sbs.at[k], sbr.at[k])

    def p1(k, i, j, dev, col):
        dst = hh.at[k] if i == 0 else tt.at[k, i - 1]
        return send(r0.at[row(k, j, col)], dst, dev, s1s.at[k, i], s1r.at[k, i])

    def p2(k, i, j, dev):
        dst = h2.at[k] if i == 0 else uu.at[k, i - 1]
        return send(r0.at[one(k, j)], dst, dev, s2s.at[k, i], s2r.at[k, i])

    def add(a, b):
        return a.astype(F32) + b.astype(F32)

    def step(t, carry):
        for li, when in ((0, 0), (1, 2), (2, 4), (3, 8)):
            @pl.when(t == when)
            def _(li=li):
                turn_left(li)

        @pl.when(t == 0)
        def _():
            pl.semaphore_wait(barrier, 5)

        @pl.when(t < K)
        def _():
            k = t

            @pl.when(k >= 2)
            def _():
                ring.by_colour(lambda col: sib(k - 2, col).wait_send())

            for h in range(2):
                T = 2 * k + h
                lanes = slice(h * TILE, h * TILE + TILE)
                li = (T >= 9).astype(jnp.int32) + (T >= 13).astype(jnp.int32) + (T >= 31).astype(jnp.int32)
                ri = jnp.maximum(T - 1, 0)

                def body(xx, carry):
                    rows = pl.ds(pl.multiple_of(xx * QUARTER, 16), QUARTER)
                    part = nn(leftt[li, rows, :], right_ref[ri]).astype(BF16)
                    pp[k % 2, xx, :, :, :, lanes] = part.reshape(4, 2, 48, TILE)
                    return carry

                lax.fori_loop(0, 4, body, 0)

            @pl.when(k == 0)
            def _():
                def body(xx, carry):
                    rows = pl.ds(pl.multiple_of(xx * QUARTER, 16), QUARTER)
                    pp[0, xx, :, :, :, 0:TILE] = small_ref[rows, :].reshape(4, 2, 48, TILE)
                    return carry
                lax.fori_loop(0, 4, body, 0)

            ring.by_colour(lambda col: sib(k, col).start())

        @pl.when(jnp.logical_and(t >= 1, t - 1 < K))
        def _():
            k = t - 1

            def f(col):
                sib(k, col).wait_recv()

                def body(xx, carry):
                    r0[k, xx] = add(r0[k, xx], pp[k % 2, xx, :, col]).astype(BF16)
                    return carry

                lax.fori_loop(0, 4, body, 0)

                def h(par):
                    if par == 0:
                        p1(k, 0, 2, ring.bp, col).start()
                        p1(k, 2, 3, ring.bm, col).start()
                    else:
                        p1(k, 0, 2, ring.bm, col).start()
                        p1(k, 1, 1, ring.bp, col).start()

                by_parity(k, h)

            ring.by_colour(f)

        @pl.when(jnp.logical_and(t >= 2, t - 2 < K))
        def _():
            k = t - 2

            def f(col):
                def h(par):
                    j = 1 if par == 0 else 3
                    p1(k, 0, 2, ring.bp, col).wait_recv()
                    r0[row(k, j, col)] = add(r0[row(k, j, col)], hh[k]).astype(BF16)
                    if par == 0:
                        p1(k, 1, 1, ring.bp, col).start()
                    else:
                        p1(k, 2, 3, ring.bm, col).start()

                by_parity(k, h)

            ring.by_colour(f)

        @pl.when(jnp.logical_and(t >= 3, t - 3 < K))
        def _():
            k = t - 3

            def f(col):
                p1(k, 1, 1, ring.bp, col).wait_recv()
                p1(k, 2, 3, ring.bm, col).wait_recv()
                mine = row(k, 0, col)
                r0[mine] = (add(r0[mine], tt[k, 0]) + tt[k, 1].astype(F32)).astype(BF16)

            ring.by_colour(f)

            def h(par):
                if par == 0:
                    p2(k, 0, 2, ring.ap).start()
                    p2(k, 2, 3, ring.am).start()
                else:
                    p2(k, 0, 2, ring.am).start()
                    p2(k, 1, 1, ring.ap).start()

            by_parity(k, h)

        @pl.when(jnp.logical_and(t >= 4, t - 4 < K))
        def _():
            k = t - 4

            def h(par):
                j = 1 if par == 0 else 3
                p2(k, 0, 2, ring.ap).wait_recv()
                r0[one(k, j)] = add(r0[one(k, j)], h2[k]).astype(BF16)
                if par == 0:
                    p2(k, 1, 1, ring.ap).start()
                else:
                    p2(k, 2, 3, ring.am).start()

            by_parity(k, h)

        @pl.when(t >= 5)
        def _():
            k = t - 5
            p2(k, 1, 1, ring.ap).wait_recv()
            p2(k, 2, 3, ring.am).wait_recv()
            out_ref[:, pl.ds(pl.multiple_of(k * PW, PW), PW)] = add(r0[one(k, 0)], uu[k, 0]) + uu[k, 1].astype(F32)

        return carry

    lax.fori_loop(0, K + 5, step, 0)

    def finish(k, carry):
        def f(col):
            @pl.when(k >= K - 2)
            def _():
                sib(k, col).wait_send()
            for i in range(3):
                p1(k, i, 1, ring.bp, col).wait_send()

        ring.by_colour(f)
        for i in range(3):
            p2(k, i, 1, ring.ap).wait_send()
        return carry

    lax.fori_loop(0, K, finish, 0)


def reduce_weights(left, right, small):
    K = PIECES
    dma = pltpu.SemaphoreType.DMA
    vmem = pl.BlockSpec(memory_space=pltpu.VMEM)
    return pl.pallas_call(
        reduce_kernel,
        name="reduce",
        out_shape=jax.ShapeDtypeStruct((48, PIECES * PW), F32),
        in_specs=[vmem, vmem, vmem],
        out_specs=vmem,
        scratch_shapes=[
            pltpu.VMEM((4, D, ALL), BF16),
            pltpu.VMEM((2, 4, 4, 2, 48, PW), BF16),
            pltpu.VMEM((K, 4, 4, 48, PW), BF16),
            pltpu.VMEM((K, 4, 48, PW), BF16),
            pltpu.VMEM((K, 2, 4, 48, PW), BF16),
            pltpu.VMEM((K, 48, PW), BF16),
            pltpu.VMEM((K, 2, 48, PW), BF16),
            dma((K,)), dma((K,)), dma((K, 3)), dma((K, 3)), dma((K, 3)), dma((K, 3)),
        ],
        compiler_params=pltpu.CompilerParams(
            collective_id=2, has_side_effects=True, vmem_limit_bytes=VMEM_LIMIT
        ),
    )(left, right, small)


def shards(
    inputs, out_grad, lengths, order, *weights
):
    group = lax.axis_index("dp")
    masks = document_masks(lax.dynamic_index_in_dim(lengths, group, 1, keepdims=False))
    res, grad, left, right, small = chain(
        pack_shard(*weights), inputs.reshape(HALF, D), out_grad.reshape(HALF, D), masks
    )
    slots = jnp.arange(32, dtype=jnp.int32)
    source = jnp.sum(jnp.where(order == group, slots[None, :], 0), axis=1, dtype=jnp.int32)
    every = lax.all_gather(res, "dp", axis=0, tiled=False).reshape(32, 2, 72, D)
    hidden = jnp.stack(
        [lax.dynamic_index_in_dim(every[:, m], source[m], 0, keepdims=False) for m in range(2)]
    ).astype(F32)[None]
    input_grad = grad.reshape(1, 2, 72, D)
    total = reduce_weights(left, right, small)
    vec = total[32, 0:256].reshape(8, 8, 4)
    col = lambda a, n: total[:, a:a + n]
    return (
        hidden, input_grad,
        col(256, 1024)[None], col(1280, 1024)[None],
        total[0:32, 0:128].reshape(1, 8, 4, 128), total[0:32, 128:256].reshape(1, 8, 4, 128),
        vec[0][None], vec[1][None], vec[2][None], vec[3:7][None], vec[7][None],
        col(2304, 1024).T[None], col(3328, 2304)[None], col(5632, 2304)[None], col(7936, 2304).T[None],
        total[33, 0:48][None], total[33, 48:96][None],
    )


def solution(mesh):
    rows = P(None, ("dp", "tensor"), None)
    tall = P("section", "dp", "tensor")
    wide = P("section", "tensor", "dp")
    block = P("section", "tensor", "dp", None)
    taps = P("section", None, "tensor", "dp")
    gain = P("section", "dp")
    params = (tall, tall, block, block, wide, wide, wide, taps, wide, wide, tall, tall, wide, gain, gain)
    out_rows = P("section", None, ("dp", "tensor"), None)
    return jax.shard_map(
        shards,
        mesh=mesh,
        in_specs=(rows, rows, P(), P()) + params,
        out_specs=(out_rows, out_rows) + params,
        check_vma=False,
    )
```

```python
import jax
import jax.numpy as jnp
from jax import lax
from jax.experimental import pallas as pl
from jax.experimental.pallas import tpu as pltpu
from jax.sharding import PartitionSpec as P

MESH = pl.DeviceIdType.MESH
F32 = jnp.float32
BF16 = jnp.bfloat16
EPS = 1e-06
FLOOR = 0.01
PIECES = 20
PW = 512
TILE = 256
HALF = 144
ALL = 288
D = 1536
QUARTER = 384
VMEM_LIMIT = 63 * 2**20


def nn(a, b):
    return lax.dot_general(a, b, (((1,), (0,)), ((), ())), preferred_element_type=F32)


def nt(a, b):
    return lax.dot_general(a, b, (((1,), (1,)), ((), ())), preferred_element_type=F32)


def tn(a, b):
    return lax.dot_general(a, b, (((0,), (0,)), ((), ())), preferred_element_type=F32)


def gelu_parts(v):
    k = 0.7978845608028654
    th = jnp.tanh(k * (v + 0.044715 * v * v * v))
    half = 0.5 * (1.0 + th)
    slope = half + 0.5 * v * (1.0 - th * th) * (k * (1.0 + 0.134145 * v * v))
    return v * half, slope


def gelu(v):
    k = 0.7978845608028654
    return 0.5 * v * (1.0 + jnp.tanh(k * (v + 0.044715 * v * v * v)))


def sigmoid(v):
    return 1.0 / (1.0 + jnp.exp(-v))


def softplus(v):
    return jnp.maximum(v, 0.0) + jnp.log(1.0 + jnp.exp(-jnp.abs(v)))


def to_natural(v):
    return jnp.concatenate([v[0:72], v[144:216], v[72:144], v[216:288]], axis=0)


def to_exchange(v):
    return jnp.concatenate([v[0:72], v[144:216], v[72:144], v[216:288]], axis=0)


def down(v, k):
    return pltpu.roll(v, k, 0) if k else v


def up(v, k):
    return pltpu.roll(v, ALL - k, 0) if k else v


def scan_down(a, b):
    for s in (1, 2, 4, 8, 16, 32, 64):
        b = a * down(b, s) + b
        if s < 64:
            a = a * down(a, s)
    return b


def scan_up(a, b):
    for s in (1, 2, 4, 8, 16, 32, 64):
        b = a * up(b, s) + b
        if s < 64:
            a = a * up(a, s)
    return b


def iota(shape, dim):
    return lax.broadcasted_iota(jnp.int32, shape, dim)


def onehot(cond):
    return jnp.where(cond, 1.0, 0.0).astype(BF16)


class Ring:
    def __init__(self):
        dp = lax.axis_index("dp")
        c, z, x = dp % 2, (dp // 2) % 4, dp // 8
        self.dp, self.c, self.z, self.x = dp, c, z, x

        def at(dx, dz):
            return ((x + dx) % 4) * 8 + ((z + dz) % 4) * 2 + c

        self.ap, self.am = at(1 - c, c), at(3 * (1 - c), 3 * c)
        self.bp, self.bm = at(c, 1 - c), at(3 * c, 3 * (1 - c))
        self.sib = dp + 1 - 2 * c

    def by_colour(self, fn):
        @pl.when(self.c == 0)
        def _():
            fn(0)

        @pl.when(self.c == 1)
        def _():
            fn(1)


def by_parity(k, fn):
    @pl.when(k % 2 == 0)
    def _():
        fn(0)

    @pl.when(k % 2 == 1)
    def _():
        fn(1)


def go(src, dst, dev, ssem, rsem):
    return pltpu.make_async_remote_copy(
        src_ref=src, dst_ref=dst, send_sem=ssem, recv_sem=rsem, device_id=dev, device_id_type=MESH
    )


def gather_steps(ring, g_ref, sems):
    s1s, s1r, s2s, s2r, s3s, s3r = sems
    c, x, z = ring.c, ring.x, ring.z
    K = PIECES

    def send(r, dev, ssem, rsem):
        return go(r, r, {"dp": dev}, ssem, rsem)

    def one(k, j):
        return g_ref.at[k, (x + j * (1 - c)) % 4, (z + j * c) % 4, c]

    def p1(k, j, recv):
        if j == 0:
            return send(one(k, 3 if recv else 0), ring.ap, s1s.at[k, 0], s1r.at[k, 0])
        return send(one(k, 1 if recv else 0), ring.am, s1s.at[k, 1], s1r.at[k, 1])

    def p1f(k, par, recv):
        if par == 0:
            return send(one(k, 2 if recv else 3), ring.ap, s1s.at[k, 2], s1r.at[k, 2])
        return send(one(k, 2 if recv else 1), ring.am, s1s.at[k, 2], s1r.at[k, 2])

    def row(k, j, col):
        if col == 0:
            return g_ref.at[k, :, (z + j) % 4, 0]
        return g_ref.at[k, (x + j) % 4, :, 1]

    def p2(k, j, recv, col):
        if j == 0:
            return send(row(k, 3 if recv else 0, col), ring.bp, s2s.at[k, 0], s2r.at[k, 0])
        return send(row(k, 1 if recv else 0, col), ring.bm, s2s.at[k, 1], s2r.at[k, 1])

    def p2f(k, par, recv, col):
        if par == 0:
            return send(row(k, 2 if recv else 3, col), ring.bp, s2s.at[k, 2], s2r.at[k, 2])
        return send(row(k, 2 if recv else 1, col), ring.bm, s2s.at[k, 2], s2r.at[k, 2])

    def sb(k, j, col):
        return send(row(k, j, col), ring.sib, s3s.at[k, j], s3r.at[k, j])

    def step(t):
        @pl.when(t < K)
        def _():
            p1(t, 0, False).start()
            p1(t, 1, False).start()

        @pl.when(jnp.logical_and(t >= 1, t - 1 < K))
        def _():
            k = t - 1

            def f(par):
                p1(k, par, True).wait_recv()
                p1f(k, par, False).start()
                p1(k, 1 - par, True).wait_recv()

            by_parity(k, f)

        @pl.when(jnp.logical_and(t >= 2, t - 2 < K))
        def _():
            k = t - 2
            by_parity(k, lambda par: p1f(k, par, True).wait_recv())

            def f(col):
                p2(k, 0, False, col).start()
                p2(k, 1, False, col).start()
                sb(k, 0, col).start()

            ring.by_colour(f)

        @pl.when(jnp.logical_and(t >= 3, t - 3 < K))
        def _():
            k = t - 3

            def f(col):
                def h(par):
                    p2(k, par, True, col).wait_recv()
                    p2f(k, par, False, col).start()
                    p2(k, 1 - par, True, col).wait_recv()

                by_parity(k, h)
                sb(k, 1, col).start()
                sb(k, 3, col).start()

            ring.by_colour(f)

        @pl.when(t >= 4)
        def _():
            k = t - 4

            def f(col):
                by_parity(k, lambda par: p2f(k, par, True, col).wait_recv())
                sb(k, 2, col).start()

            ring.by_colour(f)

    def ready(k):
        def f(col):
            for j in range(4):
                send(row(k, j, 1 - col), ring.sib, s3s.at[k, j], s3r.at[k, j]).wait_recv()

        ring.by_colour(f)

    def finish(k, carry):
        p1(k, 0, False).wait_send()
        p1(k, 1, False).wait_send()
        by_parity(k, lambda par: p1f(k, par, False).wait_send())

        def f(col):
            p2(k, 0, False, col).wait_send()
            p2(k, 1, False, col).wait_send()
            by_parity(k, lambda par: p2f(k, par, False, col).wait_send())
            for j in range(4):
                sb(k, j, col).wait_send()

        ring.by_colour(f)
        return carry

    return step, ready, lambda: lax.fori_loop(0, K, finish, 0)


def deal_steps(ring, res, hid, sems):
    s1s, s1r, s2s, s2r, s3s, s3r, lsem = sems
    c, x, z = ring.c, ring.x, ring.z
    parts = (pl.ds(0, 80), pl.ds(80, 64))

    def send(r, dev, ssem, rsem):
        return go(r, r, {"dp": dev}, ssem, rsem)

    def one(j):
        return hid.at[(x + j * (1 - c)) % 4, (z + j * c) % 4, c]

    def row(j, col):
        if col == 0:
            return hid.at[:, (z + j) % 4, 0]
        return hid.at[(x + j) % 4, :, 1]

    def p1(i, recv):
        if i == 0:
            return send(one(3 if recv else 0), ring.ap, s1s.at[0], s1r.at[0])
        if i == 1:
            return send(one(1 if recv else 0), ring.am, s1s.at[1], s1r.at[1])
        if i == 2:
            return send(one(2 if recv else 3).at[parts[0]], ring.ap, s1s.at[2], s1r.at[2])
        return send(one(2 if recv else 1).at[parts[1]], ring.am, s1s.at[3], s1r.at[3])

    def p2(i, recv, col):
        if i == 0:
            return send(row(3 if recv else 0, col), ring.bp, s2s.at[0], s2r.at[0])
        if i == 1:
            return send(row(1 if recv else 0, col), ring.bm, s2s.at[1], s2r.at[1])
        if i == 2:
            return send(row(2 if recv else 3, col).at[:, parts[0]], ring.bp, s2s.at[2], s2r.at[2])
        return send(row(2 if recv else 1, col).at[:, parts[1]], ring.bm, s2s.at[3], s2r.at[3])

    def sb(j, col):
        return send(row(j, col), ring.sib, s3s.at[j], s3r.at[j])

    def step(t):
        if t == 0:
            local = pltpu.make_async_copy(res, one(0), lsem)
            local.start()
            local.wait()
            p1(0, False).start()
            p1(1, False).start()
        elif t == 1:
            p1(0, True).wait_recv()
            p1(2, False).start()
            p1(1, True).wait_recv()
            p1(3, False).start()
        elif t == 2:
            p1(2, True).wait_recv()
            p1(3, True).wait_recv()

            def f(col):
                p2(0, False, col).start()
                p2(1, False, col).start()
                sb(0, col).start()

            ring.by_colour(f)
        elif t == 3:
            def f(col):
                p2(0, True, col).wait_recv()
                p2(2, False, col).start()
                sb(3, col).start()
                p2(1, True, col).wait_recv()
                p2(3, False, col).start()
                sb(1, col).start()

            ring.by_colour(f)
        elif t == 4:
            def f(col):
                p2(2, True, col).wait_recv()
                p2(3, True, col).wait_recv()
                sb(2, col).start()

            ring.by_colour(f)
        else:
            for i in range(4):
                p1(i, False).wait_send()

            def f(col):
                for i in range(4):
                    p2(i, False, col).wait_send()
                    sb(i, col).wait_send()
                    send(row(i, 1 - col), ring.sib, s3s.at[i], s3r.at[i]).wait_recv()

            ring.by_colour(f)

    return step


def reduce_steps(ring, g_ref, left, right, leftt, pp, out_ref, stage, free, pack, sems):
    sbs, sbr, s1s, s1r, s2s, s2r, osem = sems
    c, x, z = ring.c, ring.x, ring.z
    K = PIECES

    def send(src, dst, dev, ssem, rsem):
        return go(src, dst, {"dp": dev}, ssem, rsem)

    def turn_left(li):
        def body(i, carry):
            cols = pl.ds(pl.multiple_of(i * 128, 128), 128)
            leftt[cols, :] = left[li, :, cols].T
            return carry
        lax.fori_loop(0, 12, body, 0)

    def one(k, j):
        return k, (x + j * (1 - c)) % 4, (z + j * c) % 4, 0

    def row(k, j, col):
        if col == 0:
            return k, slice(None), (z + j) % 4, 0
        return k, (x + j) % 4, slice(None), 0

    def sib(k, col):
        return send(pp.at[k % 2, :, :, 1 - col], g_ref.at[k, :, :, 0], ring.sib, sbs.at[k], sbr.at[k])

    def p1(k, i, j, dev, col):
        return send(g_ref.at[row(k, j, col)], g_ref.at[k, i, :, 1], dev, s1s.at[k, i], s1r.at[k, i])

    def p2(k, i, j, dev):
        return send(g_ref.at[one(k, j)], g_ref.at[k, 3, i, 1], dev, s2s.at[k, i], s2r.at[k, i])

    def add(a, b):
        return a.astype(F32) + b.astype(F32)

    def out_copy(k):
        return pltpu.make_async_copy(stage.at[k % 2], out_ref.at[k], osem.at[k % 2])

    def step(t, low, high):
        for li, when in ((3, 0), (2, 4), (1, 13), (0, 15), (3, 19)):
            if not low <= when <= high:
                continue

            @pl.when(t == when)
            def _(li=li):
                turn_left(li)

        for group, when in ((0, 0), (1, 4), (2, 13), (3, 15)):
            if not low <= when <= high:
                continue

            @pl.when(t == when)
            def _(group=group):
                pl.semaphore_wait(free.at[group], 5)

        @pl.when(t < K)
        def _():
            k = K - 1 - t

            @pl.when(t >= 2)
            def _():
                ring.by_colour(lambda col: sib(k + 2, col).wait_send())

            def body(xx, carry):
                rows = pl.ds(pl.multiple_of(xx * QUARTER, 16), QUARTER)
                part = nn(leftt[rows, :], right[k]).astype(BF16)
                pp[k % 2, xx] = part.reshape(4, 2, 48, PW)
                return carry

            lax.fori_loop(0, 4, body, 0)

            if high >= K - 1:
                pl.when(k == 0)(pack)

            ring.by_colour(lambda col: sib(k, col).start())

        @pl.when(jnp.logical_and(t >= 1, t - 1 < K))
        def _():
            k = K - t

            def f(col):
                sib(k, col).wait_recv()

                def body(xx, carry):
                    g_ref[k, xx, :, 0] = add(g_ref[k, xx, :, 0], pp[k % 2, xx, :, col]).astype(BF16)
                    return carry

                lax.fori_loop(0, 4, body, 0)

                def h(par):
                    if par == 0:
                        p1(k, 0, 2, ring.bp, col).start()
                        p1(k, 2, 3, ring.bm, col).start()
                    else:
                        p1(k, 0, 2, ring.bm, col).start()
                        p1(k, 1, 1, ring.bp, col).start()

                by_parity(k, h)

            ring.by_colour(f)

        @pl.when(jnp.logical_and(t >= 2, t - 2 < K))
        def _():
            k = K + 1 - t

            def f(col):
                def h(par):
                    j = 1 if par == 0 else 3
                    p1(k, 0, 2, ring.bp, col).wait_recv()
                    g_ref[row(k, j, col)] = add(g_ref[row(k, j, col)], g_ref[k, 0, :, 1]).astype(BF16)
                    if par == 0:
                        p1(k, 1, 1, ring.bp, col).start()
                    else:
                        p1(k, 2, 3, ring.bm, col).start()

                by_parity(k, h)

            ring.by_colour(f)

        @pl.when(jnp.logical_and(t >= 3, t - 3 < K))
        def _():
            k = K + 2 - t

            def f(col):
                p1(k, 1, 1, ring.bp, col).wait_recv()
                p1(k, 2, 3, ring.bm, col).wait_recv()
                mine = row(k, 0, col)
                g_ref[mine] = (add(g_ref[mine], g_ref[k, 1, :, 1]) + g_ref[k, 2, :, 1].astype(F32)).astype(BF16)

            ring.by_colour(f)

            def h(par):
                if par == 0:
                    p2(k, 0, 2, ring.ap).start()
                    p2(k, 2, 3, ring.am).start()
                else:
                    p2(k, 0, 2, ring.am).start()
                    p2(k, 1, 1, ring.ap).start()

            by_parity(k, h)

        @pl.when(jnp.logical_and(t >= 4, t - 4 < K))
        def _():
            k = K + 3 - t

            def h(par):
                j = 1 if par == 0 else 3
                p2(k, 0, 2, ring.ap).wait_recv()
                g_ref[one(k, j)] = add(g_ref[one(k, j)], g_ref[k, 3, 0, 1]).astype(BF16)
                if par == 0:
                    p2(k, 1, 1, ring.ap).start()
                else:
                    p2(k, 2, 3, ring.am).start()

            by_parity(k, h)

        @pl.when(t >= 5)
        def _():
            k = K + 4 - t
            p2(k, 1, 1, ring.ap).wait_recv()
            p2(k, 2, 3, ring.am).wait_recv()

            @pl.when(t >= 7)
            def _():
                out_copy(k + 2).wait()

            stage[k % 2] = add(g_ref[one(k, 0)], g_ref[k, 3, 1, 1]) + g_ref[k, 3, 2, 1].astype(F32)
            out_copy(k).start()

    def finish_one(k, carry):
        def f(col):
            @pl.when(k < 2)
            def _():
                sib(k, col).wait_send()
                out_copy(k).wait()

            for i in range(3):
                p1(k, i, 1, ring.bp, col).wait_send()

        ring.by_colour(f)
        for i in range(3):
            p2(k, i, 1, ring.ap).wait_send()
        return carry

    return step, lambda: lax.fori_loop(0, K, finish_one, 0)


def whole_kernel(
    gelu_ref, lru_ref, out_ref, gate_ref, up_ref, down_ref, small_ref, xin_ref, ein_ref, mask_ref,
    hid_out, grad_out, sums_out,
    g_ref, xb, left, right, pf, cv, rg, ig, st, mid, own, sb, rb, gmid, rw, vec, vgrad, gains, gsum, gpart, sgrad, acc,
    leftt, pp, stage, res,
    lsem, psem_s, psem_r, free, *more,
):
    sec = lax.axis_index("section")
    t = lax.axis_index("tensor")
    ring = Ring()
    barrier = pltpu.get_barrier_semaphore()
    others = [{"dp": d} for d in (ring.ap, ring.am, ring.bp, ring.bm, ring.sib)] + [{"tensor": 1 - t}, {"section": 1 - sec}]
    for dev in others:
        pl.semaphore_signal(barrier, inc=1, device_id=dev, device_id_type=MESH)
    loads = []

    def load(src, col, width, piece, lane):
        part = src.at[:, pl.ds(col, width)]
        to = g_ref.at[piece, ring.x, ring.z, ring.c, :, pl.ds(lane, width)]
        loads.append(pltpu.make_async_copy(part, to, lsem.at[len(loads)]))

    load(down_ref, 2048, 256, 0, 0)
    load(small_ref, 0, 256, 0, 256)
    for i in range(2):
        load(gelu_ref, i * 512, 512, 1 + i, 0)
        load(lru_ref, i * 512, 512, 3 + i, 0)
        load(out_ref, i * 512, 512, 5 + i, 0)
    for i in range(9):
        load(gate_ref, i * 256, 256, 7 + i, 0)
        load(up_ref, i * 256, 256, 7 + i, 256)
    for i in range(4):
        load(down_ref, i * 512, 512, 16 + i, 0)
    for copy in loads:
        copy.start()
    my = pl.ds(pl.multiple_of(t * HALF, 16), HALF)
    his = pl.ds(pl.multiple_of((1 - t) * HALF, 16), HALF)
    xcopy = pltpu.make_async_copy(xin_ref, xb, lsem.at[30])
    ecopy = pltpu.make_async_copy(ein_ref, left.at[3, my], lsem.at[31])

    @pl.when(sec == 0)
    def _():
        xcopy.start()

    @pl.when(sec == 1)
    def _():
        ecopy.start()

    pl.semaphore_wait(barrier, 7)
    for copy in loads:
        copy.wait()

    def pair(src, dst, i):
        return go(src, dst, {"tensor": 1 - t}, psem_s.at[i], psem_r.at[i])

    def share(li, i):
        return pair(left.at[li, my], left.at[li, my], i)

    def shared(li, i):
        return pair(left.at[li, his], left.at[li, his], i)

    def hand(src, dst, i):
        return go(src, dst, {"section": 1 - sec}, psem_s.at[i], psem_r.at[i])

    def back_piece(x):
        return hand(sb.at[x], left.at[3, my, pl.ds(x * QUARTER, QUARTER)], 22 + x)

    ag_step, ag_ready, ag_finish = gather_steps(ring, g_ref, more[0:6])
    deal = deal_steps(ring, res, hid_out, more[6:13])

    @pl.when(sec == 0)
    def _():
        def body(i, carry):
            ag_step(i)
            return carry
        lax.fori_loop(0, 5, body, 0)
        ag_ready(0)
        xcopy.wait()

    @pl.when(sec == 1)
    def _():
        ecopy.wait()
        share(3, 10).start()

        def body(i, carry):
            ag_step(i)
            return carry

        lax.fori_loop(0, PIECES + 4, body, 0)

        def await_piece(i, carry):
            ag_ready(i)
            return carry

        lax.fori_loop(0, PIECES, await_piece, 0)

    def beside(step, piece=None):
        @pl.when(sec == 0)
        def _():
            ag_step(step)
            if piece is not None:
                ag_ready(piece)

    def wt(piece, lane):
        return g_ref[piece, :, :, :, :, pl.ds(pl.multiple_of(lane, TILE), TILE)].reshape(D, TILE)

    def wc(piece):
        return g_ref[piece].reshape(D, PW)

    def wq(piece, x, width=PW):
        return g_ref[piece, x, :, :, :, 0:width].reshape(QUARTER, width)

    right[0] = jnp.zeros((ALL, PW), BF16)
    small = wt(0, TILE)

    def unpack(j, carry):
        ci, r = iota((128, D), 0), iota((128, D), 1)
        sel = onehot(r == (ci // 4) * 48 + j * 4 + ci % 4)
        rw[j] = nn(sel, small).astype(BF16)
        return carry

    lax.fori_loop(0, 8, unpack, 0)
    dpi, r = iota((32, D), 0), iota((32, D), 1)
    t32 = nn(onehot(r == dpi * 48 + 32), small).astype(BF16)
    d1 = onehot(iota((32, 128), 1) // 4 == iota((32, 128), 0))
    e1 = tn(t32, d1)
    e1 = jnp.where(iota((256, 128), 0) % 4 == iota((256, 128), 1) % 4, e1, 0.0).astype(BF16)
    v1 = nn(onehot(iota((64, 256), 1) // 4 == iota((64, 256), 0)), e1)
    for i in range(64):
        vec[i] = v1[i:i + 1, :]
    t33 = nn(onehot(r == dpi * 48 + 33), small).astype(BF16)
    d2 = onehot(jnp.logical_and(r >= dpi * 48, r < dpi * 48 + 48))
    e2 = tn(t33[:, 0:128], d2)
    within = iota((128, D), 1) % 48
    q = iota((128, D), 0)
    gains[0] = jnp.sum(jnp.where(q == within, e2, 0.0), axis=0, keepdims=True)
    gains[1] = jnp.sum(jnp.where(q == within + 48, e2, 0.0), axis=0, keepdims=True)

    @pl.when(sec == 1)
    def _():
        hand(xb, xb, 21).wait_recv()

    def rows16(i):
        return pl.ds(pl.multiple_of(i * 16, 16), 16)

    def myrows16(i):
        return pl.ds(pl.multiple_of(t * HALF + i * 16, 16), 16)

    def scale_of(v):
        return lax.rsqrt(jnp.mean(v * v, axis=1, keepdims=True) + EPS)

    def norm_one(i, carry):
        v = xb[rows16(i), :].astype(F32)
        left[0, myrows16(i), :] = (v * scale_of(v) * gains[0]).astype(BF16)
        return carry

    lax.fori_loop(0, 9, norm_one, 0)
    share(0, 0).start()

    def into_branches(rows, first):
        def body(i, carry):
            if first:
                beside(5 + i, 1 + i)
            else:
                pl.when(i < 2)(lambda: beside(9 + i, 5 + i))
            pf[i, rows, :] = nn(left[0, rows, :], wc(1 + i))
            return carry
        lax.fori_loop(0, 4, body, 0)

    into_branches(my, True)
    shared(0, 0).wait_recv()
    into_branches(his, False)

    def vrow(a, j):
        return vec[a * 8 + j]

    def lanes_of(i, h):
        return pl.ds(pl.multiple_of((i % 2) * 256 + h * 128, 128), 128)

    def mixer(i, carry):
        beside(11 + i, 7 + i)
        for h in range(2):
            j = i * 2 + h
            lanes = lanes_of(i, h)
            feature = to_natural(pf[2 + i // 2, :, lanes])
            filtered = vrow(7, j)
            for k in range(4):
                filtered = filtered + vrow(3 + k, j) * (down(feature, k) * mask_ref[k - 1] if k else feature)
            low = filtered.astype(BF16)
            cv[j] = low
            conv = low.astype(F32)
            pre = nn(low, rw[j])
            rate = sigmoid(pre[:, 0:128] + vrow(0, j))
            inp = sigmoid(pre[:, 128:256] + vrow(1, j))
            rg[j] = rate
            ig[j] = inp
            decay = jnp.exp(-8.0 * rate * softplus(-vrow(2, j)))
            scale_in = jnp.sqrt(jnp.maximum(1.0 - decay * decay, FLOOR))
            state = scan_down(decay * mask_ref[0], scale_in * inp * conv)
            st[j] = state
            right[5 + i // 2, :, lanes] = (to_exchange(state) * gelu(pf[i // 2, :, lanes])).astype(BF16)
        return carry

    lax.fori_loop(0, 4, mixer, 0)

    def reduce_out(pieces, base, turn, also):
        def body(x, carry):
            total = None
            for piece in pieces:
                width = PW if piece else TILE
                part = nt(right[piece, :, 0:width], wq(piece, x, width))
                total = part if total is None else total + part
            acc[...] = total
            sb[x] = acc[his, :].astype(BF16)
            pair(sb.at[x], rb.at[turn, x], base + x).start()
            own[x] = acc[my, :]
            also(x)
            return carry

        lax.fori_loop(0, 4, body, 0)

    def reduce_wait(base, turn):
        for x in range(4):
            pair(sb.at[x], rb.at[turn, x], base + x).wait()

    def summed(i, turn):
        rows = rows16(i)
        return jnp.concatenate([own[x, rows, :] + rb[turn, x, rows, :].astype(F32) for x in range(4)], axis=1)

    reduce_out((5, 6), 1, 0, lambda x: beside(15 + x, 11 + x))
    reduce_wait(1, 0)

    def norm_two(i, carry):
        v = xb[rows16(i), :].astype(F32) + summed(i, 0)
        mid[rows16(i), :] = v
        left[2, myrows16(i), :] = (v * scale_of(v) * gains[1]).astype(BF16)
        return carry

    lax.fori_loop(0, 9, norm_two, 0)
    share(2, 5).start()

    def hidden_at(i):
        return (16 + i // 2) % PIECES, pl.multiple_of((i % 2) * TILE, TILE)

    def feed(rows, first):
        def body(i, carry):
            if first:
                pl.when(i < 5)(lambda: beside(19 + i, 15 + i))
            both = nn(left[2, rows, :], wc(7 + i))
            pg, pu = both[:, 0:TILE], both[:, TILE:PW]
            right[7 + i, rows, :] = both.astype(BF16)
            piece, lane = hidden_at(i)
            right[piece, rows, pl.ds(lane, TILE)] = (gelu(pg) * pu).astype(BF16)
            return carry
        lax.fori_loop(0, 9, body, 0)

    feed(my, True)
    shared(2, 5).wait_recv()
    feed(his, False)
    reduce_out((16, 17, 18, 19, 0), 6, 1, lambda x: None)
    reduce_wait(6, 1)

    def finish_forward(i, carry):
        v = mid[rows16(i), :] + summed(i, 1)
        res[rows16(i), :] = v.astype(BF16)
        return carry

    lax.fori_loop(0, 9, finish_forward, 0)

    @pl.when(sec == 0)
    def _():
        hand(res, xb, 21).start()
        for i in range(5):
            deal(i)
        for x in range(4):
            back_piece(x).wait_recv()
        share(3, 10).start()

    def deal_beside(i):
        @pl.when(sec == 1)
        def _():
            deal(i)

    deal_beside(0)
    ag_finish()
    shared(3, 10).wait_recv()

    def feed_back(i, carry):
        piece, lane = hidden_at(i)
        gh = nn(left[3], wt(piece, lane))
        pg = right[7 + i, :, 0:TILE].astype(F32)
        pu = right[7 + i, :, TILE:PW].astype(F32)
        act, slope = gelu_parts(pg)
        right[7 + i, :, 0:TILE] = (gh * pu * slope).astype(BF16)
        right[7 + i, :, TILE:PW] = (gh * act).astype(BF16)
        return carry

    lax.fori_loop(0, 9, feed_back, 0)
    around = (ring.ap, ring.am, ring.bp, ring.bm, ring.sib)

    def release(group):
        for dev in around:
            pl.semaphore_signal(free.at[group], inc=1, device_id={"dp": dev}, device_id_type=MESH)

    rs_step, rs_finish = reduce_steps(ring, g_ref, left, right, leftt, pp, sums_out, stage, free, lambda: pack_small(), more[13:20])

    def sum_beside(i, low, high):
        @pl.when(sec == 0)
        def _():
            rs_step(i, low, high)

    release(0)
    deal_beside(1)
    reduce_out(tuple(range(7, 16)), 11, 0, lambda x: sum_beside(x, 0, 3))
    release(1)
    reduce_wait(11, 0)

    def eight(v):
        return v[0:8] + v[8:16]

    def middle_back(i, carry):
        ng = summed(i, 0)
        m = mid[rows16(i), :]
        sc = scale_of(m)
        u = ng * gains[1]
        gm = left[3, myrows16(i), :].astype(F32) + sc * u - m * (sc * sc * sc) * jnp.mean(u * m, axis=1, keepdims=True)
        gmid[rows16(i), :] = gm
        left[1, myrows16(i), :] = gm.astype(BF16)
        return carry + eight(ng * m * sc)

    gpart[1] = lax.fori_loop(0, 9, middle_back, jnp.zeros((8, D), F32))
    share(1, 15).start()
    deal_beside(2)
    sum_beside(4, 4, 4)
    shared(1, 15).wait_recv()

    def mixer_back(i, carry):
        gmix = nn(left[1], wt(5 + i // 2, (i % 2) * TILE))
        sum_beside(5 + i, 5, 8)
        for h in range(2):
            j = i * 2 + h
            lanes = lanes_of(i, h)
            gm = gmix[:, h * 128:h * 128 + 128]
            act, slope = gelu_parts(pf[i // 2, :, lanes])
            state = st[j]
            right[1 + i // 2, :, lanes] = (gm * to_exchange(state) * slope).astype(BF16)
            grad_state = to_natural(gm * act)
            rate, inp = rg[j], ig[j]
            conv = cv[j].astype(F32)
            forget = softplus(-vrow(2, j))
            decay = jnp.exp(-8.0 * rate * forget)
            spare = 1.0 - decay * decay
            scale_in = jnp.sqrt(jnp.maximum(spare, FLOOR))
            m1 = mask_ref[0]
            drive = scan_up(up(decay * m1, 1), grad_state)
            grad_spare = jnp.where(spare > FLOOR, 0.5 * (drive * inp * conv) / scale_in, 0.0)
            grad_decay = drive * down(state, 1) * m1 - 2.0 * decay * grad_spare
            grad_log = grad_decay * decay
            rate_low = (grad_log * (-8.0 * forget) * rate * (1.0 - rate)).astype(BF16)
            driven = drive * scale_in
            input_low = (driven * conv * inp * (1.0 - inp)).astype(BF16)
            both = jnp.concatenate([rate_low, input_low], axis=1)
            back = nt(both, rw[j])
            vgrad[0 * 8 + j] = jnp.sum(rate_low.astype(F32), axis=0, keepdims=True)
            vgrad[1 * 8 + j] = jnp.sum(input_low.astype(F32), axis=0, keepdims=True)
            grad_forget = jnp.sum(grad_log * (-8.0 * rate), axis=0, keepdims=True)
            vgrad[2 * 8 + j] = -grad_forget * sigmoid(-vrow(2, j))
            sgrad[j] = tn(cv[j], both).astype(BF16)
            grad_conv = driven * inp + back
            feature = to_natural(pf[2 + i // 2, :, lanes])
            grad_feature = None
            for k in range(4):
                masked = grad_conv * mask_ref[k - 1] if k else grad_conv
                vgrad[(3 + k) * 8 + j] = jnp.sum(masked * down(feature, k), axis=0, keepdims=True)
                term = up(masked, k) * vrow(3 + k, j)
                grad_feature = term if grad_feature is None else grad_feature + term
            vgrad[7 * 8 + j] = jnp.sum(grad_conv, axis=0, keepdims=True)
            right[3 + i // 2, :, lanes] = to_exchange(grad_feature).astype(BF16)
        return carry

    lax.fori_loop(0, 4, mixer_back, 0)
    release(2)
    deal_beside(3)
    reduce_out((1, 2, 3, 4), 16, 1, lambda x: sum_beside(9 + x, 9, 12))
    release(3)
    reduce_wait(16, 1)

    def first_back(i, carry):
        fg = summed(i, 1)
        v = xb[rows16(i), :].astype(F32)
        sc = scale_of(v)
        u = fg * gains[0]
        gv = gmid[rows16(i), :] + sc * u - v * (sc * sc * sc) * jnp.mean(u * v, axis=1, keepdims=True)
        mid[rows16(i), :] = gv
        for x in range(4):
            sb[x, rows16(i), :] = gv[:, x * QUARTER:(x + 1) * QUARTER].astype(BF16)
        return carry + eight(fg * v * sc)

    gpart[0] = lax.fori_loop(0, 9, first_back, jnp.zeros((8, D), F32))

    @pl.when(sec == 1)
    def _():
        for x in range(4):
            back_piece(x).start()

    pair(gpart, gsum, 20).start()
    grad_copy = pltpu.make_async_copy(mid, grad_out, lsem.at[0])
    grad_copy.start()
    deal_beside(4)

    v2 = jnp.concatenate([vgrad[i] for i in range(64)], axis=0).astype(BF16)
    e2 = nn(onehot(iota((256, 64), 0) // 4 == iota((256, 64), 1)), v2)
    e2 = jnp.where(iota((256, 128), 0) % 4 == iota((256, 128), 1) % 4, e2, 0.0).astype(BF16)
    t32 = nt(d1, e2).astype(BF16)
    pair(gpart, gsum, 20).wait()
    n1 = jnp.sum(gpart[0] + gsum[0], axis=0, keepdims=True)
    n2 = jnp.sum(gpart[1] + gsum[1], axis=0, keepdims=True)
    spread = jnp.where(q == within, n1, jnp.where(q == within + 48, n2, 0.0)).astype(BF16)
    t33 = nt(d2, spread).astype(BF16)
    t33 = jnp.concatenate([t33, jnp.zeros((32, 128), BF16)], axis=1)

    def pack_part(x, carry):
        r = iota((QUARTER, 128), 0) + x * QUARTER
        ci = iota((QUARTER, 128), 1)
        total = None
        for j in range(8):
            sel = onehot(r == (ci // 4) * 48 + j * 4 + ci % 4)
            part = nn(sel, sgrad[j])
            total = part if total is None else total + part
        r = iota((QUARTER, 32), 0) + x * QUARTER
        dpi = iota((QUARTER, 32), 1)
        total = total + nn(onehot(r == dpi * 48 + 32), t32) + nn(onehot(r == dpi * 48 + 33), t33)
        pp[0, x, :, :, :, TILE:PW] = total.astype(BF16).reshape(4, 2, 48, TILE)
        return carry

    def pack_small():
        lax.fori_loop(0, 4, pack_part, 0)

    def last(i, carry):
        rs_step(i, 0, PIECES + 4)
        return carry

    lax.fori_loop(jnp.where(sec == 0, 13, 0), PIECES + 5, last, 0)
    rs_finish()
    deal(5)
    for li, i in ((0, 0), (2, 5), (3, 10), (1, 15)):
        share(li, i).wait_send()

    @pl.when(sec == 0)
    def _():
        hand(res, xb, 21).wait_send()

    @pl.when(sec == 1)
    def _():
        for x in range(4):
            back_piece(x).wait_send()

    grad_copy.wait()


def whole(gelu, lru, out, gate, up_, down_, small, xin, ein, masks):
    K = PIECES
    dma = pltpu.SemaphoreType.DMA
    vmem = pl.BlockSpec(memory_space=pltpu.VMEM)
    hbm = pl.BlockSpec(memory_space=pl.ANY)
    sds = jax.ShapeDtypeStruct
    return pl.pallas_call(
        whole_kernel,
        name="whole",
        out_shape=(sds((4, 4, 2, HALF, D), BF16), sds((HALF, D), F32), sds((K, 48, PW), F32)),
        in_specs=[hbm] * 9 + [vmem],
        out_specs=(hbm, hbm, hbm),
        scratch_shapes=[
            pltpu.VMEM((K, 4, 4, 2, 48, PW), BF16),
            pltpu.VMEM((HALF, D), BF16),
            pltpu.VMEM((4, ALL, D), BF16),
            pltpu.VMEM((K, ALL, PW), BF16),
            pltpu.VMEM((4, ALL, PW), F32),
            pltpu.VMEM((8, ALL, 128), BF16),
            pltpu.VMEM((8, ALL, 128), F32),
            pltpu.VMEM((8, ALL, 128), F32),
            pltpu.VMEM((8, ALL, 128), F32),
            pltpu.VMEM((HALF, D), F32),
            pltpu.VMEM((4, HALF, QUARTER), F32),
            pltpu.VMEM((4, HALF, QUARTER), BF16),
            pltpu.VMEM((2, 4, HALF, QUARTER), BF16),
            pltpu.VMEM((HALF, D), F32),
            pltpu.VMEM((8, 128, 256), BF16),
            pltpu.VMEM((64, 1, 128), F32),
            pltpu.VMEM((64, 1, 128), F32),
            pltpu.VMEM((2, 1, D), F32),
            pltpu.VMEM((2, 8, D), F32),
            pltpu.VMEM((2, 8, D), F32),
            pltpu.VMEM((8, 128, 256), BF16),
            pltpu.VMEM((ALL, QUARTER), F32),
            pltpu.VMEM((D, ALL), BF16),
            pltpu.VMEM((2, 4, 4, 2, 48, PW), BF16),
            pltpu.VMEM((2, 48, PW), F32),
            pltpu.VMEM((HALF, D), BF16),
            dma((32,)), dma((26,)), dma((26,)), pltpu.SemaphoreType.REGULAR((4,)),
            dma((K, 3)), dma((K, 3)), dma((K, 3)), dma((K, 3)), dma((K, 4)), dma((K, 4)),
            dma((4,)), dma((4,)), dma((4,)), dma((4,)), dma((4,)), dma((4,)), dma(()),
            dma((K,)), dma((K,)), dma((K, 3)), dma((K, 3)), dma((K, 3)), dma((K, 3)), dma((2,)),
        ],
        compiler_params=pltpu.CompilerParams(
            collective_id=1, has_side_effects=True, vmem_limit_bytes=VMEM_LIMIT
        ),
    )(gelu, lru, out, gate, up_, down_, small, xin, ein, masks)


def document_masks(doc_lengths):
    ends = jnp.cumsum(doc_lengths, axis=-1, dtype=jnp.int32)
    position = jnp.arange(HALF, dtype=jnp.int32)
    ident = jnp.sum((position[None, :, None] >= ends[:, None, :]).astype(jnp.int32), axis=-1, dtype=jnp.int32)
    masks = []
    for offset in range(1, 4):
        before = jnp.pad(ident, ((0, 0), (offset, 0)), constant_values=-1)[:, :HALF]
        masks.append((before == ident).astype(F32).reshape(ALL, 1))
    return jnp.broadcast_to(jnp.stack(masks), (3, ALL, 128))


def pack_small_shard(rate_weight, input_weight, rate_bias, input_bias, decay_param, filter_taps, filter_bias, norm_first, norm_second):
    vectors = jnp.concatenate([v[0].reshape(-1) for v in (rate_bias, input_bias, decay_param, filter_taps, filter_bias)]).reshape(1, 256)
    gains = jnp.concatenate([norm_first[0], norm_second[0], jnp.zeros((160,), BF16)]).reshape(1, 256)
    gates = jnp.concatenate([rate_weight[0].reshape(32, 128), input_weight[0].reshape(32, 128)], axis=1)
    return jnp.concatenate([gates, vectors, gains, jnp.zeros((14, 256), BF16)], axis=0)


def shards(
    inputs, out_grad, lengths, order, gelu_weight, lru_weight, rate_weight, input_weight, rate_bias, input_bias,
    decay_param, filter_taps, filter_bias, out_weight, gate_weight, up_weight, down_weight, norm_first, norm_second
):
    group = lax.axis_index("dp")
    masks = document_masks(lax.dynamic_index_in_dim(lengths, group, 1, keepdims=False))
    small = pack_small_shard(rate_weight, input_weight, rate_bias, input_bias, decay_param, filter_taps, filter_bias, norm_first, norm_second)
    every, grad, sums = whole(
        gelu_weight[0], lru_weight[0], out_weight[0].T, gate_weight[0], up_weight[0], down_weight[0].T, small,
        inputs.reshape(HALF, D), out_grad.reshape(HALF, D), masks
    )
    slots = jnp.arange(32, dtype=jnp.int32)
    source = jnp.sum(jnp.where(order == group, slots[None, :], 0), axis=1, dtype=jnp.int32)
    every = every.reshape(32, 2, 72, D)
    hidden = jnp.stack(
        [lax.dynamic_index_in_dim(every[:, m], source[m], 0, keepdims=False) for m in range(2)]
    ).astype(F32)[None]
    input_grad = grad.reshape(1, 2, 72, D)

    def side(pieces):
        return jnp.concatenate(pieces, axis=1)

    tiny = sums[0, :, TILE:]
    vec = tiny[32].reshape(8, 8, 4)
    down_grad = side([sums[16], sums[17], sums[18], sums[19], sums[0, :, :TILE]])
    return (
        hidden, input_grad,
        side([sums[1], sums[2]])[None], side([sums[3], sums[4]])[None],
        tiny[0:32, 0:128].reshape(1, 8, 4, 128), tiny[0:32, 128:256].reshape(1, 8, 4, 128),
        vec[0][None], vec[1][None], vec[2][None], vec[3:7][None], vec[7][None],
        side([sums[5], sums[6]]).T[None],
        side([sums[7 + i, :, :TILE] for i in range(9)])[None], side([sums[7 + i, :, TILE:] for i in range(9)])[None],
        down_grad.T[None], tiny[33, 0:48][None], tiny[33, 48:96][None],
    )


def solution(mesh):
    rows = P(None, ("dp", "tensor"), None)
    tall = P("section", "dp", "tensor")
    wide = P("section", "tensor", "dp")
    block = P("section", "tensor", "dp", None)
    taps = P("section", None, "tensor", "dp")
    gain = P("section", "dp")
    params = (tall, tall, block, block, wide, wide, wide, taps, wide, wide, tall, tall, wide, gain, gain)
    out_rows = P("section", None, ("dp", "tensor"), None)
    return jax.shard_map(
        shards,
        mesh=mesh,
        in_specs=(rows, rows, P(), P()) + params,
        out_specs=(out_rows, out_rows) + params,
        check_vma=False,
    )
```

```python
import jax
import jax.numpy as jnp
from jax import lax
from jax.experimental import pallas as pl
from jax.experimental.pallas import tpu as pltpu
from jax.sharding import PartitionSpec as P

MESH = pl.DeviceIdType.MESH
F32 = jnp.float32
BF16 = jnp.bfloat16
EPS = 1e-06
FLOOR = 0.01
PIECES = 20
PW = 512
TILE = 256
HALF = 144
ALL = 288
D = 1536
QUARTER = 384
LAG = 2
VMEM_LIMIT = 63 * 2**20


def nn(a, b):
    return lax.dot_general(a, b, (((1,), (0,)), ((), ())), preferred_element_type=F32)


def nt(a, b):
    return lax.dot_general(a, b, (((1,), (1,)), ((), ())), preferred_element_type=F32)


def tn(a, b):
    return lax.dot_general(a, b, (((0,), (0,)), ((), ())), preferred_element_type=F32)


def gelu_parts(v):
    k = 0.7978845608028654
    th = jnp.tanh(k * (v + 0.044715 * v * v * v))
    half = 0.5 * (1.0 + th)
    slope = half + 0.5 * v * (1.0 - th * th) * (k * (1.0 + 0.134145 * v * v))
    return v * half, slope


def gelu(v):
    k = 0.7978845608028654
    return 0.5 * v * (1.0 + jnp.tanh(k * (v + 0.044715 * v * v * v)))


def sigmoid(v):
    return 1.0 / (1.0 + jnp.exp(-v))


def softplus(v):
    return jnp.maximum(v, 0.0) + jnp.log(1.0 + jnp.exp(-jnp.abs(v)))


def to_natural(v):
    return jnp.concatenate([v[0:72], v[144:216], v[72:144], v[216:288]], axis=0)


def to_exchange(v):
    return jnp.concatenate([v[0:72], v[144:216], v[72:144], v[216:288]], axis=0)


def down(v, k):
    return pltpu.roll(v, k, 0) if k else v


def up(v, k):
    return pltpu.roll(v, ALL - k, 0) if k else v


def scan_down(a, b):
    for s in (1, 2, 4, 8, 16, 32, 64):
        b = a * down(b, s) + b
        if s < 64:
            a = a * down(a, s)
    return b


def scan_up(a, b):
    for s in (1, 2, 4, 8, 16, 32, 64):
        b = a * up(b, s) + b
        if s < 64:
            a = a * up(a, s)
    return b


def iota(shape, dim):
    return lax.broadcasted_iota(jnp.int32, shape, dim)


def onehot(cond):
    return jnp.where(cond, 1.0, 0.0).astype(BF16)


class Ring:
    def __init__(self):
        dp = lax.axis_index("dp")
        c, z, x = dp % 2, (dp // 2) % 4, dp // 8
        self.dp, self.c, self.z, self.x = dp, c, z, x

        def at(dx, dz):
            return ((x + dx) % 4) * 8 + ((z + dz) % 4) * 2 + c

        self.ap, self.am = at(1 - c, c), at(3 * (1 - c), 3 * c)
        self.bp, self.bm = at(c, 1 - c), at(3 * c, 3 * (1 - c))
        self.sib = dp + 1 - 2 * c

    def by_colour(self, fn):
        @pl.when(self.c == 0)
        def _():
            fn(0)

        @pl.when(self.c == 1)
        def _():
            fn(1)


def by_parity(k, fn):
    @pl.when(k % 2 == 0)
    def _():
        fn(0)

    @pl.when(k % 2 == 1)
    def _():
        fn(1)


def go(src, dst, dev, ssem, rsem):
    return pltpu.make_async_remote_copy(
        src_ref=src, dst_ref=dst, send_sem=ssem, recv_sem=rsem, device_id=dev, device_id_type=MESH
    )


def gather_steps(ring, g_ref, sems):
    s1s, s1r, s2s, s2r, s3s, s3r = sems
    c, x, z = ring.c, ring.x, ring.z
    K = PIECES

    def send(r, dev, ssem, rsem):
        return go(r, r, {"dp": dev}, ssem, rsem)

    def one(k, j):
        return g_ref.at[k, (x + j * (1 - c)) % 4, (z + j * c) % 4, c]

    def p1(k, j, recv):
        if j == 0:
            return send(one(k, 3 if recv else 0), ring.ap, s1s.at[k, 0], s1r.at[k, 0])
        return send(one(k, 1 if recv else 0), ring.am, s1s.at[k, 1], s1r.at[k, 1])

    def p1f(k, par, recv):
        if par == 0:
            return send(one(k, 2 if recv else 3), ring.ap, s1s.at[k, 2], s1r.at[k, 2])
        return send(one(k, 2 if recv else 1), ring.am, s1s.at[k, 2], s1r.at[k, 2])

    def row(k, j, col):
        if col == 0:
            return g_ref.at[k, :, (z + j) % 4, 0]
        return g_ref.at[k, (x + j) % 4, :, 1]

    def p2(k, j, recv, col):
        if j == 0:
            return send(row(k, 3 if recv else 0, col), ring.bp, s2s.at[k, 0], s2r.at[k, 0])
        return send(row(k, 1 if recv else 0, col), ring.bm, s2s.at[k, 1], s2r.at[k, 1])

    def p2f(k, par, recv, col):
        if par == 0:
            return send(row(k, 2 if recv else 3, col), ring.bp, s2s.at[k, 2], s2r.at[k, 2])
        return send(row(k, 2 if recv else 1, col), ring.bm, s2s.at[k, 2], s2r.at[k, 2])

    def sb(k, j, col):
        return send(row(k, j, col), ring.sib, s3s.at[k, j], s3r.at[k, j])

    def step(t):
        @pl.when(t < K)
        def _():
            p1(t, 0, False).start()
            p1(t, 1, False).start()

        @pl.when(jnp.logical_and(t >= 1, t - 1 < K))
        def _():
            k = t - 1

            def f(par):
                p1(k, par, True).wait_recv()
                p1f(k, par, False).start()
                p1(k, 1 - par, True).wait_recv()

            by_parity(k, f)

        @pl.when(jnp.logical_and(t >= 2, t - 2 < K))
        def _():
            k = t - 2
            by_parity(k, lambda par: p1f(k, par, True).wait_recv())

            def f(col):
                p2(k, 0, False, col).start()
                p2(k, 1, False, col).start()
                sb(k, 0, col).start()

            ring.by_colour(f)

        @pl.when(jnp.logical_and(t >= 3, t - 3 < K))
        def _():
            k = t - 3

            def f(col):
                def h(par):
                    p2(k, par, True, col).wait_recv()
                    p2f(k, par, False, col).start()
                    p2(k, 1 - par, True, col).wait_recv()

                by_parity(k, h)
                sb(k, 1, col).start()
                sb(k, 3, col).start()

            ring.by_colour(f)

        @pl.when(t >= 4)
        def _():
            k = t - 4

            def f(col):
                by_parity(k, lambda par: p2f(k, par, True, col).wait_recv())
                sb(k, 2, col).start()

            ring.by_colour(f)

    def ready(k):
        def f(col):
            for j in range(4):
                send(row(k, j, 1 - col), ring.sib, s3s.at[k, j], s3r.at[k, j]).wait_recv()

        ring.by_colour(f)

    def finish(k, carry):
        p1(k, 0, False).wait_send()
        p1(k, 1, False).wait_send()
        by_parity(k, lambda par: p1f(k, par, False).wait_send())

        def f(col):
            p2(k, 0, False, col).wait_send()
            p2(k, 1, False, col).wait_send()
            by_parity(k, lambda par: p2f(k, par, False, col).wait_send())
            for j in range(4):
                sb(k, j, col).wait_send()

        ring.by_colour(f)
        return carry

    return step, ready, lambda: lax.fori_loop(0, K, finish, 0)


def deal_steps(ring, res, hid, sems):
    s1s, s1r, s2s, s2r, s3s, s3r, lsem = sems
    c, x, z = ring.c, ring.x, ring.z
    parts = (pl.ds(0, 80), pl.ds(80, 64))

    def send(r, dev, ssem, rsem):
        return go(r, r, {"dp": dev}, ssem, rsem)

    def one(j):
        return hid.at[(x + j * (1 - c)) % 4, (z + j * c) % 4, c]

    def row(j, col):
        if col == 0:
            return hid.at[:, (z + j) % 4, 0]
        return hid.at[(x + j) % 4, :, 1]

    def p1(i, recv):
        if i == 0:
            return send(one(3 if recv else 0), ring.ap, s1s.at[0], s1r.at[0])
        if i == 1:
            return send(one(1 if recv else 0), ring.am, s1s.at[1], s1r.at[1])
        if i == 2:
            return send(one(2 if recv else 3).at[parts[0]], ring.ap, s1s.at[2], s1r.at[2])
        return send(one(2 if recv else 1).at[parts[1]], ring.am, s1s.at[3], s1r.at[3])

    def p2(i, recv, col):
        if i == 0:
            return send(row(3 if recv else 0, col), ring.bp, s2s.at[0], s2r.at[0])
        if i == 1:
            return send(row(1 if recv else 0, col), ring.bm, s2s.at[1], s2r.at[1])
        if i == 2:
            return send(row(2 if recv else 3, col).at[:, parts[0]], ring.bp, s2s.at[2], s2r.at[2])
        return send(row(2 if recv else 1, col).at[:, parts[1]], ring.bm, s2s.at[3], s2r.at[3])

    def sb(j, col):
        return send(row(j, col), ring.sib, s3s.at[j], s3r.at[j])

    def step(t):
        if t == 0:
            local = pltpu.make_async_copy(res, one(0), lsem)
            local.start()
            local.wait()
            p1(0, False).start()
            p1(1, False).start()
        elif t == 1:
            p1(0, True).wait_recv()
            p1(2, False).start()
            p1(1, True).wait_recv()
            p1(3, False).start()
        elif t == 2:
            p1(2, True).wait_recv()
            p1(3, True).wait_recv()

            def f(col):
                p2(0, False, col).start()
                p2(1, False, col).start()
                sb(0, col).start()

            ring.by_colour(f)
        elif t == 3:
            def f(col):
                p2(0, True, col).wait_recv()
                p2(2, False, col).start()
                sb(3, col).start()
                p2(1, True, col).wait_recv()
                p2(3, False, col).start()
                sb(1, col).start()

            ring.by_colour(f)
        elif t == 4:
            def f(col):
                p2(2, True, col).wait_recv()
                p2(3, True, col).wait_recv()
                sb(2, col).start()

            ring.by_colour(f)
        else:
            for i in range(4):
                p1(i, False).wait_send()

            def f(col):
                for i in range(4):
                    p2(i, False, col).wait_send()
                    sb(i, col).wait_send()
                    send(row(i, 1 - col), ring.sib, s3s.at[i], s3r.at[i]).wait_recv()

            ring.by_colour(f)

    return step


def reduce_steps(ring, g_ref, left, right, leftt, pp, outs, stage, staget, free, pack, sems):
    sbs, sbr, s1s, s1r, s2s, s2r, osem = sems
    c, x, z = ring.c, ring.x, ring.z
    K = PIECES

    def send(src, dst, dev, ssem, rsem):
        return go(src, dst, {"dp": dev}, ssem, rsem)

    def turn_left(li):
        def body(i, carry):
            cols = pl.ds(pl.multiple_of(i * 128, 128), 128)
            leftt[cols, :] = left[li, :, cols].T
            return carry
        lax.fori_loop(0, 12, body, 0)

    def one(k, j):
        return k, (x + j * (1 - c)) % 4, (z + j * c) % 4, 0

    def row(k, j, col):
        if col == 0:
            return k, slice(None), (z + j) % 4, 0
        return k, (x + j) % 4, slice(None), 0

    def sib(k, col):
        return send(pp.at[k % 2, :, :, 1 - col], g_ref.at[k, :, :, 0], ring.sib, sbs.at[k], sbr.at[k])

    def p1(k, i, j, dev, col):
        return send(g_ref.at[row(k, j, col)], g_ref.at[k, i, :, 1], dev, s1s.at[k, i], s1r.at[k, i])

    def p2(k, i, j, dev):
        return send(g_ref.at[one(k, j)], g_ref.at[k, 3, i, 1], dev, s2s.at[k, i], s2r.at[k, i])

    def add(a, b):
        return a.astype(F32) + b.astype(F32)

    gelu_o, lru_o, out_o, gate_o, up_o, down_o, small_o = outs

    def groups(k):
        slot = k % 2

        def flat(ref, first, width=PW, lane=0, sem=0):
            to = ref.at[:, pl.ds(pl.multiple_of(first, 128), width)]
            return pltpu.make_async_copy(stage.at[slot, :, pl.ds(lane, width)], to, osem.at[slot, sem])

        def turned(ref, first, height=PW):
            to = ref.at[pl.ds(pl.multiple_of(first, 128), height)]
            return pltpu.make_async_copy(staget.at[slot, pl.ds(0, height)], to, osem.at[slot, 0])

        def between(low, high):
            return jnp.logical_and(k >= low, k <= high)

        return (
            (between(1, 2), False, lambda: (flat(gelu_o, (k - 1) * PW),)),
            (between(3, 4), False, lambda: (flat(lru_o, (k - 3) * PW),)),
            (between(5, 6), True, lambda: (turned(out_o, (k - 5) * PW),)),
            (between(7, 15), False, lambda: (flat(gate_o, (k - 7) * TILE, TILE), flat(up_o, (k - 7) * TILE, TILE, TILE, 1))),
            (between(16, 19), True, lambda: (turned(down_o, (k - 16) * PW),)),
            (k == 0, None, lambda: (turned(down_o, 4 * PW, TILE), flat(small_o, 0, TILE, TILE, 1))),
        )

    def put(k, value):
        for cond, turn, copies in groups(k):
            @pl.when(cond)
            def _(turn=turn, copies=copies):
                if turn is not False:
                    staget[k % 2] = value.T
                if turn is not True:
                    stage[k % 2] = value
                for copy in copies():
                    copy.start()

    def put_wait(k):
        for cond, _, copies in groups(k):
            @pl.when(cond)
            def _(copies=copies):
                for copy in copies():
                    copy.wait()

    def step(t, low, high):
        for li, when in ((3, 0), (2, 4), (1, 13), (0, 15), (3, 19)):
            if not low <= when <= high:
                continue

            @pl.when(t == when)
            def _(li=li):
                turn_left(li)

        for group, when in ((0, 0), (1, 4), (2, 13), (3, 15)):
            if not low <= when <= high:
                continue

            @pl.when(t == when)
            def _(group=group):
                pl.semaphore_wait(free.at[group], 5)

        @pl.when(jnp.logical_and(t >= 5 * LAG, t - 5 * LAG < K))
        def _():
            k = K - 1 - t + 5 * LAG
            p2(k, 1, 1, ring.ap).wait_recv()
            p2(k, 2, 3, ring.am).wait_recv()

            @pl.when(t >= 5 * LAG + 2)
            def _():
                put_wait(k + 2)

            put(k, add(g_ref[one(k, 0)], g_ref[k, 3, 1, 1]) + g_ref[k, 3, 2, 1].astype(F32))

        @pl.when(jnp.logical_and(t >= 4 * LAG, t - 4 * LAG < K))
        def _():
            k = K - 1 - t + 4 * LAG

            def h(par):
                j = 1 if par == 0 else 3
                p2(k, 0, 2, ring.ap).wait_recv()
                g_ref[one(k, j)] = add(g_ref[one(k, j)], g_ref[k, 3, 0, 1]).astype(BF16)
                if par == 0:
                    p2(k, 1, 1, ring.ap).start()
                else:
                    p2(k, 2, 3, ring.am).start()

            by_parity(k, h)

        @pl.when(jnp.logical_and(t >= 3 * LAG, t - 3 * LAG < K))
        def _():
            k = K - 1 - t + 3 * LAG

            def f(col):
                p1(k, 1, 1, ring.bp, col).wait_recv()
                p1(k, 2, 3, ring.bm, col).wait_recv()
                mine = row(k, 0, col)
                g_ref[mine] = (add(g_ref[mine], g_ref[k, 1, :, 1]) + g_ref[k, 2, :, 1].astype(F32)).astype(BF16)

            ring.by_colour(f)

            def h(par):
                if par == 0:
                    p2(k, 0, 2, ring.ap).start()
                    p2(k, 2, 3, ring.am).start()
                else:
                    p2(k, 0, 2, ring.am).start()
                    p2(k, 1, 1, ring.ap).start()

            by_parity(k, h)

        @pl.when(jnp.logical_and(t >= 2 * LAG, t - 2 * LAG < K))
        def _():
            k = K - 1 - t + 2 * LAG

            def f(col):
                def h(par):
                    j = 1 if par == 0 else 3
                    p1(k, 0, 2, ring.bp, col).wait_recv()
                    g_ref[row(k, j, col)] = add(g_ref[row(k, j, col)], g_ref[k, 0, :, 1]).astype(BF16)
                    if par == 0:
                        p1(k, 1, 1, ring.bp, col).start()
                    else:
                        p1(k, 2, 3, ring.bm, col).start()

                by_parity(k, h)

            ring.by_colour(f)

        @pl.when(jnp.logical_and(t >= 1 * LAG, t - 1 * LAG < K))
        def _():
            k = K - 1 - t + 1 * LAG

            def f(col):
                sib(k, col).wait_recv()

                def body(xx, carry):
                    g_ref[k, xx, :, 0] = add(g_ref[k, xx, :, 0], pp[k % 2, xx, :, col]).astype(BF16)
                    return carry

                lax.fori_loop(0, 4, body, 0)

                def h(par):
                    if par == 0:
                        p1(k, 0, 2, ring.bp, col).start()
                        p1(k, 2, 3, ring.bm, col).start()
                    else:
                        p1(k, 0, 2, ring.bm, col).start()
                        p1(k, 1, 1, ring.bp, col).start()

                by_parity(k, h)

            ring.by_colour(f)

        @pl.when(t < K)
        def _():
            k = K - 1 - t

            @pl.when(t >= 2)
            def _():
                ring.by_colour(lambda col: sib(k + 2, col).wait_send())

            def body(xx, carry):
                rows = pl.ds(pl.multiple_of(xx * QUARTER, 16), QUARTER)
                part = nn(leftt[rows, :], right[k]).astype(BF16)
                pp[k % 2, xx] = part.reshape(4, 2, 48, PW)
                return carry

            lax.fori_loop(0, 4, body, 0)

            if high >= K - 1:
                pl.when(k == 0)(pack)

            ring.by_colour(lambda col: sib(k, col).start())

    def finish_one(k, carry):
        def f(col):
            @pl.when(k < 2)
            def _():
                sib(k, col).wait_send()
                put_wait(k)

            for i in range(3):
                p1(k, i, 1, ring.bp, col).wait_send()

        ring.by_colour(f)
        for i in range(3):
            p2(k, i, 1, ring.ap).wait_send()
        return carry

    return step, lambda: lax.fori_loop(0, K, finish_one, 0)


def whole_kernel(
    gelu_ref, lru_ref, out_ref, gate_ref, up_ref, down_ref, small_ref, xin_ref, ein_ref, mask_ref,
    hid_out, grad_out, gelu_o, lru_o, out_o, gate_o, up_o, down_o, small_o,
    g_ref, xall, left, right, pf, cv, rg, ig, st, mid, own, sb, rb, gmid, rw, vec, vgrad, gains, gsum, gpart, sgrad, acc,
    leftt, pp, stage, staget, res,
    lsem, psem_s, psem_r, free, hand_s, hand_r, back_s, back_r, *more,
):
    sec = lax.axis_index("section")
    t = lax.axis_index("tensor")
    ring = Ring()
    barrier = pltpu.get_barrier_semaphore()
    others = [{"dp": d} for d in (ring.ap, ring.am, ring.bp, ring.bm, ring.sib)] + [{"tensor": 1 - t}, {"section": 1 - sec}, {"section": 1 - sec, "tensor": 1 - t}]
    for dev in others:
        pl.semaphore_signal(barrier, inc=1, device_id=dev, device_id_type=MESH)
    loads = []

    def load(src, col, width, piece, lane):
        part = src.at[:, pl.ds(col, width)]
        to = g_ref.at[piece, ring.x, ring.z, ring.c, :, pl.ds(lane, width)]
        loads.append(pltpu.make_async_copy(part, to, lsem.at[len(loads)]))

    load(down_ref, 2048, 256, 0, 0)
    load(small_ref, 0, 256, 0, 256)
    for i in range(2):
        load(gelu_ref, i * 512, 512, 1 + i, 0)
        load(lru_ref, i * 512, 512, 3 + i, 0)
        load(out_ref, i * 512, 512, 5 + i, 0)
    for i in range(9):
        load(gate_ref, i * 256, 256, 7 + i, 0)
        load(up_ref, i * 256, 256, 7 + i, 256)
    for i in range(4):
        load(down_ref, i * 512, 512, 16 + i, 0)
    for copy in loads:
        copy.start()
    my = pl.ds(pl.multiple_of(t * HALF, 16), HALF)
    his = pl.ds(pl.multiple_of((1 - t) * HALF, 16), HALF)
    xcopy = pltpu.make_async_copy(xin_ref, xall.at[t], lsem.at[30])
    ecopy = pltpu.make_async_copy(ein_ref, left.at[3, my], lsem.at[31])

    @pl.when(sec == 0)
    def _():
        xcopy.start()

    @pl.when(sec == 1)
    def _():
        ecopy.start()

    pl.semaphore_wait(barrier, 8)
    for copy in loads:
        copy.wait()

    def pair(src, dst, i):
        return go(src, dst, {"tensor": 1 - t}, psem_s.at[i], psem_r.at[i])

    def share(li, i):
        return pair(left.at[li, my], left.at[li, my], i)

    def shared(li, i):
        return pair(left.at[li, his], left.at[li, his], i)

    def rows48(i):
        return pl.ds(pl.multiple_of(i * 48, 16), 48)

    def half48(h, i):
        return pl.ds(pl.multiple_of(h * HALF + i * 48, 16), 48)

    def hand(to, r):
        dev = {"section": 1 - sec, "tensor": (t + to) % 2}
        return go(res.at[rows48(r)], xall.at[t, rows48(r)], dev, hand_s.at[to, r], hand_r.at[t, r])

    def handed(h, r):
        to = xall.at[h, rows48(r)]
        return go(to, to, {"section": 1 - sec}, hand_s.at[0, r], hand_r.at[h, r])

    def hand_back(to, r):
        dev = {"section": 1 - sec, "tensor": (t + to) % 2}
        return go(res.at[rows48(r)], left.at[3, half48(t, r)], dev, back_s.at[to, r], back_r.at[t, r])

    def handed_back(h, r):
        to = left.at[3, half48(h, r)]
        return go(to, to, {"section": 1 - sec}, back_s.at[0, r], back_r.at[h, r])

    ag_step, ag_ready, ag_finish = gather_steps(ring, g_ref, more[0:6])
    deal = deal_steps(ring, res, hid_out, more[6:13])

    @pl.when(sec == 0)
    def _():
        def body(i, carry):
            ag_step(i)
            return carry
        lax.fori_loop(0, 5, body, 0)
        ag_ready(0)
        xcopy.wait()

    @pl.when(sec == 1)
    def _():
        ecopy.wait()
        share(3, 10).start()

        def body(i, carry):
            ag_step(i)
            return carry

        lax.fori_loop(0, PIECES + 4, body, 0)

        def await_piece(i, carry):
            ag_ready(i)
            return carry

        lax.fori_loop(0, PIECES, await_piece, 0)

    def beside(step, piece=None):
        @pl.when(sec == 0)
        def _():
            ag_step(step)
            if piece is not None:
                ag_ready(piece)

    def wt(piece, lane):
        return g_ref[piece, :, :, :, :, pl.ds(pl.multiple_of(lane, TILE), TILE)].reshape(D, TILE)

    def wc(piece):
        return g_ref[piece].reshape(D, PW)

    def wq(piece, x, width=PW):
        return g_ref[piece, x, :, :, :, 0:width].reshape(QUARTER, width)

    right[0] = jnp.zeros((ALL, PW), BF16)
    small = wt(0, TILE)

    def unpack(j, carry):
        ci, r = iota((128, D), 0), iota((128, D), 1)
        sel = onehot(r == (ci // 4) * 48 + j * 4 + ci % 4)
        rw[j] = nn(sel, small).astype(BF16)
        return carry

    lax.fori_loop(0, 8, unpack, 0)
    dpi, r = iota((32, D), 0), iota((32, D), 1)
    t32 = nn(onehot(r == dpi * 48 + 32), small).astype(BF16)
    d1 = onehot(iota((32, 128), 1) // 4 == iota((32, 128), 0))
    e1 = tn(t32, d1)
    e1 = jnp.where(iota((256, 128), 0) % 4 == iota((256, 128), 1) % 4, e1, 0.0).astype(BF16)
    v1 = nn(onehot(iota((64, 256), 1) // 4 == iota((64, 256), 0)), e1)
    for i in range(64):
        vec[i] = v1[i:i + 1, :]
    t33 = nn(onehot(r == dpi * 48 + 33), small).astype(BF16)
    d2 = onehot(jnp.logical_and(r >= dpi * 48, r < dpi * 48 + 48))
    e2 = tn(t33[:, 0:128], d2)
    within = iota((128, D), 1) % 48
    q = iota((128, D), 0)
    gains[0] = jnp.sum(jnp.where(q == within, e2, 0.0), axis=0, keepdims=True)
    gains[1] = jnp.sum(jnp.where(q == within + 48, e2, 0.0), axis=0, keepdims=True)

    def scale_of(v):
        return lax.rsqrt(jnp.mean(v * v, axis=1, keepdims=True) + EPS)

    def norm_one(h, i):
        v = xall[h, rows48(i), :].astype(F32)
        left[0, half48(h, i), :] = (v * scale_of(v) * gains[0]).astype(BF16)

    def into_branches(rows, first):
        def body(i, carry):
            if first:
                beside(5 + i, 1 + i)
            elif first is False:
                pl.when(i < 2)(lambda: beside(9 + i, 5 + i))
            pf[i, rows, :] = nn(left[0, rows, :], wc(1 + i))
            return carry
        lax.fori_loop(0, 4, body, 0)

    @pl.when(sec == 0)
    def _():
        def body(i, carry):
            norm_one(t, i)
            return carry

        lax.fori_loop(0, 3, body, 0)
        share(0, 0).start()
        into_branches(my, True)
        shared(0, 0).wait_recv()
        into_branches(his, False)

    @pl.when(sec == 1)
    def _():
        def body(i, carry):
            for h in range(2):
                handed(h, i).wait_recv()
                norm_one(h, i)
            return carry

        lax.fori_loop(0, 3, body, 0)
        into_branches(slice(None), None)

    def vrow(a, j):
        return vec[a * 8 + j]

    def lanes_of(i, h):
        return pl.ds(pl.multiple_of((i % 2) * 256 + h * 128, 128), 128)

    def mixer(i, carry):
        beside(11 + i, 7 + i)
        for h in range(2):
            j = i * 2 + h
            lanes = lanes_of(i, h)
            feature = to_natural(pf[2 + i // 2, :, lanes])
            filtered = vrow(7, j)
            for k in range(4):
                filtered = filtered + vrow(3 + k, j) * (down(feature, k) * mask_ref[k - 1] if k else feature)
            low = filtered.astype(BF16)
            cv[j] = low
            conv = low.astype(F32)
            pre = nn(low, rw[j])
            rate = sigmoid(pre[:, 0:128] + vrow(0, j))
            inp = sigmoid(pre[:, 128:256] + vrow(1, j))
            rg[j] = rate
            ig[j] = inp
            decay = jnp.exp(-8.0 * rate * softplus(-vrow(2, j)))
            scale_in = jnp.sqrt(jnp.maximum(1.0 - decay * decay, FLOOR))
            state = scan_down(decay * mask_ref[0], scale_in * inp * conv)
            st[j] = state
            right[5 + i // 2, :, lanes] = (to_exchange(state) * gelu(pf[i // 2, :, lanes])).astype(BF16)
        return carry

    lax.fori_loop(0, 4, mixer, 0)

    def reduce_out(pieces, base, turn, also):
        def body(x, carry):
            total = None
            for piece in pieces:
                width = PW if piece else TILE
                part = nt(right[piece, :, 0:width], wq(piece, x, width))
                total = part if total is None else total + part
            acc[...] = total
            sb[x] = acc[his, :].astype(BF16)
            pair(sb.at[x], rb.at[turn, x], base + x).start()
            own[x] = acc[my, :]
            also(x)
            return carry

        lax.fori_loop(0, 4, body, 0)

    def reduce_wait(base, turn):
        for x in range(4):
            pair(sb.at[x], rb.at[turn, x], base + x).wait()

    def summed(i, turn):
        rows = rows48(i)
        return jnp.concatenate([own[x, rows, :] + rb[turn, x, rows, :].astype(F32) for x in range(4)], axis=1)

    reduce_out((5, 6), 1, 0, lambda x: beside(15 + x, 11 + x))
    reduce_wait(1, 0)

    def norm_two(i, carry):
        v = xall[t, rows48(i), :].astype(F32) + summed(i, 0)
        mid[rows48(i), :] = v
        left[2, half48(t, i), :] = (v * scale_of(v) * gains[1]).astype(BF16)
        return carry

    lax.fori_loop(0, 3, norm_two, 0)
    share(2, 5).start()

    def hidden_at(i):
        return (16 + i // 2) % PIECES, pl.multiple_of((i % 2) * TILE, TILE)

    def feed(rows, first):
        def body(i, carry):
            if first:
                pl.when(i % 4 == 0)(lambda: beside(19 + i // 4, 15 + i // 4))
            else:
                pl.when(jnp.logical_or(i == 3, i == 7))(lambda: beside(22 + i // 7, 18 + i // 7))
            both = nn(left[2, rows, :], wc(7 + i))
            pg, pu = both[:, 0:TILE], both[:, TILE:PW]
            right[7 + i, rows, :] = both.astype(BF16)
            piece, lane = hidden_at(i)
            right[piece, rows, pl.ds(lane, TILE)] = (gelu(pg) * pu).astype(BF16)
            return carry
        lax.fori_loop(0, 9, body, 0)

    feed(my, True)
    shared(2, 5).wait_recv()
    feed(his, False)
    reduce_out((16, 17, 18, 19, 0), 6, 1, lambda x: None)
    reduce_wait(6, 1)

    def finish_forward(i, carry):
        v = mid[rows48(i), :] + summed(i, 1)
        res[rows48(i), :] = v.astype(BF16)

        @pl.when(sec == 0)
        def _():
            hand(0, i).start()
            hand(1, i).start()

        return carry

    lax.fori_loop(0, 3, finish_forward, 0)

    @pl.when(sec == 0)
    def _():
        for i in range(5):
            deal(i)
        for h in range(2):
            for r in range(3):
                handed_back(h, r).wait_recv()

    def deal_beside(i):
        @pl.when(sec == 1)
        def _():
            deal(i)

    deal_beside(0)
    ag_finish()
    @pl.when(sec == 1)
    def _():
        shared(3, 10).wait_recv()

    def feed_back(i, carry):
        piece, lane = hidden_at(i)
        gh = nn(left[3], wt(piece, lane))
        pg = right[7 + i, :, 0:TILE].astype(F32)
        pu = right[7 + i, :, TILE:PW].astype(F32)
        act, slope = gelu_parts(pg)
        right[7 + i, :, 0:TILE] = (gh * pu * slope).astype(BF16)
        right[7 + i, :, TILE:PW] = (gh * act).astype(BF16)
        return carry

    lax.fori_loop(0, 9, feed_back, 0)
    around = (ring.ap, ring.am, ring.bp, ring.bm, ring.sib)

    def release(group):
        for dev in around:
            pl.semaphore_signal(free.at[group], inc=1, device_id={"dp": dev}, device_id_type=MESH)

    rs_step, rs_finish = reduce_steps(ring, g_ref, left, right, leftt, pp, (gelu_o, lru_o, out_o, gate_o, up_o, down_o, small_o), stage, staget, free, lambda: pack_small(), more[13:20])

    def sum_beside(i, low, high):
        @pl.when(sec == 0)
        def _():
            rs_step(i, low, high)

    release(0)
    deal_beside(1)
    reduce_out(tuple(range(7, 16)), 11, 0, lambda x: sum_beside(x, 0, 3))
    release(1)
    reduce_wait(11, 0)

    def eight(v):
        total = v[0:8]
        for i in range(1, 6):
            total = total + v[i * 8:i * 8 + 8]
        return total

    def middle_back(i, carry):
        ng = summed(i, 0)
        m = mid[rows48(i), :]
        sc = scale_of(m)
        u = ng * gains[1]
        e = left[3, half48(t, i), :].astype(F32)
        gm = e + sc * u - m * (sc * sc * sc) * jnp.mean(u * m, axis=1, keepdims=True)
        gmid[rows48(i), :] = gm
        left[1, half48(t, i), :] = gm.astype(BF16)
        return carry + eight(ng * m * sc)

    gpart[1] = lax.fori_loop(0, 3, middle_back, jnp.zeros((8, D), F32))
    share(1, 15).start()
    deal_beside(2)
    sum_beside(4, 4, 4)
    shared(1, 15).wait_recv()

    def mixer_back(i, carry):
        gmix = nn(left[1], wt(5 + i // 2, (i % 2) * TILE))
        sum_beside(5 + i, 5, 8)
        for h in range(2):
            j = i * 2 + h
            lanes = lanes_of(i, h)
            gm = gmix[:, h * 128:h * 128 + 128]
            act, slope = gelu_parts(pf[i // 2, :, lanes])
            state = st[j]
            right[1 + i // 2, :, lanes] = (gm * to_exchange(state) * slope).astype(BF16)
            grad_state = to_natural(gm * act)
            rate, inp = rg[j], ig[j]
            conv = cv[j].astype(F32)
            forget = softplus(-vrow(2, j))
            decay = jnp.exp(-8.0 * rate * forget)
            spare = 1.0 - decay * decay
            scale_in = jnp.sqrt(jnp.maximum(spare, FLOOR))
            m1 = mask_ref[0]
            drive = scan_up(up(decay * m1, 1), grad_state)
            grad_spare = jnp.where(spare > FLOOR, 0.5 * (drive * inp * conv) / scale_in, 0.0)
            grad_decay = drive * down(state, 1) * m1 - 2.0 * decay * grad_spare
            grad_log = grad_decay * decay
            rate_low = (grad_log * (-8.0 * forget) * rate * (1.0 - rate)).astype(BF16)
            driven = drive * scale_in
            input_low = (driven * conv * inp * (1.0 - inp)).astype(BF16)
            both = jnp.concatenate([rate_low, input_low], axis=1)
            back = nt(both, rw[j])
            vgrad[0 * 8 + j] = jnp.sum(rate_low.astype(F32), axis=0, keepdims=True)
            vgrad[1 * 8 + j] = jnp.sum(input_low.astype(F32), axis=0, keepdims=True)
            grad_forget = jnp.sum(grad_log * (-8.0 * rate), axis=0, keepdims=True)
            vgrad[2 * 8 + j] = -grad_forget * sigmoid(-vrow(2, j))
            sgrad[j] = tn(cv[j], both).astype(BF16)
            grad_conv = driven * inp + back
            feature = to_natural(pf[2 + i // 2, :, lanes])
            grad_feature = None
            for k in range(4):
                masked = grad_conv * mask_ref[k - 1] if k else grad_conv
                vgrad[(3 + k) * 8 + j] = jnp.sum(masked * down(feature, k), axis=0, keepdims=True)
                term = up(masked, k) * vrow(3 + k, j)
                grad_feature = term if grad_feature is None else grad_feature + term
            vgrad[7 * 8 + j] = jnp.sum(grad_conv, axis=0, keepdims=True)
            right[3 + i // 2, :, lanes] = to_exchange(grad_feature).astype(BF16)
        return carry

    lax.fori_loop(0, 4, mixer_back, 0)
    release(2)
    deal_beside(3)
    reduce_out((1, 2, 3, 4), 16, 1, lambda x: sum_beside(9 + x, 9, 12))
    release(3)
    reduce_wait(16, 1)

    def first_back(i, carry):
        fg = summed(i, 1)
        v = xall[t, rows48(i), :].astype(F32)
        sc = scale_of(v)
        u = fg * gains[0]
        gv = gmid[rows48(i), :] + sc * u - v * (sc * sc * sc) * jnp.mean(u * v, axis=1, keepdims=True)
        mid[rows48(i), :] = gv

        @pl.when(sec == 1)
        def _():
            res[rows48(i), :] = gv.astype(BF16)
            hand_back(0, i).start()
            hand_back(1, i).start()

        return carry + eight(fg * v * sc)

    gpart[0] = lax.fori_loop(0, 3, first_back, jnp.zeros((8, D), F32))
    pair(gpart, gsum, 20).start()
    grad_copy = pltpu.make_async_copy(mid, grad_out, lsem.at[0])
    grad_copy.start()
    deal_beside(4)

    v2 = jnp.concatenate([vgrad[i] for i in range(64)], axis=0).astype(BF16)
    e2 = nn(onehot(iota((256, 64), 0) // 4 == iota((256, 64), 1)), v2)
    e2 = jnp.where(iota((256, 128), 0) % 4 == iota((256, 128), 1) % 4, e2, 0.0).astype(BF16)
    t32 = nt(d1, e2).astype(BF16)
    pair(gpart, gsum, 20).wait()
    n1 = jnp.sum(gpart[0] + gsum[0], axis=0, keepdims=True)
    n2 = jnp.sum(gpart[1] + gsum[1], axis=0, keepdims=True)
    spread = jnp.where(q == within, n1, jnp.where(q == within + 48, n2, 0.0)).astype(BF16)
    t33 = nt(d2, spread).astype(BF16)
    t33 = jnp.concatenate([t33, jnp.zeros((32, 128), BF16)], axis=1)

    def pack_part(x, carry):
        r = iota((QUARTER, 128), 0) + x * QUARTER
        ci = iota((QUARTER, 128), 1)
        total = None
        for j in range(8):
            sel = onehot(r == (ci // 4) * 48 + j * 4 + ci % 4)
            part = nn(sel, sgrad[j])
            total = part if total is None else total + part
        r = iota((QUARTER, 32), 0) + x * QUARTER
        dpi = iota((QUARTER, 32), 1)
        total = total + nn(onehot(r == dpi * 48 + 32), t32) + nn(onehot(r == dpi * 48 + 33), t33)
        pp[0, x, :, :, :, TILE:PW] = total.astype(BF16).reshape(4, 2, 48, TILE)
        return carry

    def pack_small():
        lax.fori_loop(0, 4, pack_part, 0)

    def last(i, carry):
        rs_step(i, 0, PIECES + 5 * LAG - 1)
        return carry

    lax.fori_loop(jnp.where(sec == 0, 13, 0), PIECES + 5 * LAG, last, 0)
    rs_finish()
    deal(5)
    share(2, 5).wait_send()
    share(1, 15).wait_send()

    @pl.when(sec == 0)
    def _():
        share(0, 0).wait_send()
        for to in range(2):
            for r in range(3):
                hand(to, r).wait_send()

    @pl.when(sec == 1)
    def _():
        share(3, 10).wait_send()
        for to in range(2):
            for r in range(3):
                hand_back(to, r).wait_send()

    grad_copy.wait()


def whole(gelu, lru, out, gate, up_, down_, small, xin, ein, masks):
    K = PIECES
    dma = pltpu.SemaphoreType.DMA
    vmem = pl.BlockSpec(memory_space=pltpu.VMEM)
    hbm = pl.BlockSpec(memory_space=pl.ANY)
    sds = jax.ShapeDtypeStruct
    return pl.pallas_call(
        whole_kernel,
        name="whole",
        out_shape=(
            sds((4, 4, 2, HALF, D), BF16), sds((HALF, D), F32),
            sds((48, 1024), F32), sds((48, 1024), F32), sds((1024, 48), F32),
            sds((48, 2304), F32), sds((48, 2304), F32), sds((2304, 48), F32), sds((48, TILE), F32),
        ),
        in_specs=[hbm] * 9 + [vmem],
        out_specs=(hbm,) * 9,
        scratch_shapes=[
            pltpu.VMEM((K, 4, 4, 2, 48, PW), BF16),
            pltpu.VMEM((2, HALF, D), BF16),
            pltpu.VMEM((4, ALL, D), BF16),
            pltpu.VMEM((K, ALL, PW), BF16),
            pltpu.VMEM((4, ALL, PW), F32),
            pltpu.VMEM((8, ALL, 128), BF16),
            pltpu.VMEM((8, ALL, 128), F32),
            pltpu.VMEM((8, ALL, 128), F32),
            pltpu.VMEM((8, ALL, 128), F32),
            pltpu.VMEM((HALF, D), F32),
            pltpu.VMEM((4, HALF, QUARTER), F32),
            pltpu.VMEM((4, HALF, QUARTER), BF16),
            pltpu.VMEM((2, 4, HALF, QUARTER), BF16),
            pltpu.VMEM((HALF, D), F32),
            pltpu.VMEM((8, 128, 256), BF16),
            pltpu.VMEM((64, 1, 128), F32),
            pltpu.VMEM((64, 1, 128), F32),
            pltpu.VMEM((2, 1, D), F32),
            pltpu.VMEM((2, 8, D), F32),
            pltpu.VMEM((2, 8, D), F32),
            pltpu.VMEM((8, 128, 256), BF16),
            pltpu.VMEM((ALL, QUARTER), F32),
            pltpu.VMEM((D, ALL), BF16),
            pltpu.VMEM((2, 4, 4, 2, 48, PW), BF16),
            pltpu.VMEM((2, 48, PW), F32),
            pltpu.VMEM((2, PW, 48), F32),
            pltpu.VMEM((HALF, D), BF16),
            dma((32,)), dma((21,)), dma((21,)), pltpu.SemaphoreType.REGULAR((4,)),
            dma((2, 3)), dma((2, 3)), dma((2, 3)), dma((2, 3)),
            dma((K, 3)), dma((K, 3)), dma((K, 3)), dma((K, 3)), dma((K, 4)), dma((K, 4)),
            dma((4,)), dma((4,)), dma((4,)), dma((4,)), dma((4,)), dma((4,)), dma(()),
            dma((K,)), dma((K,)), dma((K, 3)), dma((K, 3)), dma((K, 3)), dma((K, 3)), dma((2, 2)),
        ],
        compiler_params=pltpu.CompilerParams(
            collective_id=1, has_side_effects=True, vmem_limit_bytes=VMEM_LIMIT
        ),
    )(gelu, lru, out, gate, up_, down_, small, xin, ein, masks)


def document_masks(doc_lengths):
    ends = jnp.cumsum(doc_lengths, axis=-1, dtype=jnp.int32)
    position = jnp.arange(HALF, dtype=jnp.int32)
    ident = jnp.sum((position[None, :, None] >= ends[:, None, :]).astype(jnp.int32), axis=-1, dtype=jnp.int32)
    masks = []
    for offset in range(1, 4):
        before = jnp.pad(ident, ((0, 0), (offset, 0)), constant_values=-1)[:, :HALF]
        masks.append((before == ident).astype(F32).reshape(ALL, 1))
    return jnp.broadcast_to(jnp.stack(masks), (3, ALL, 128))


def pack_small_shard(rate_weight, input_weight, rate_bias, input_bias, decay_param, filter_taps, filter_bias, norm_first, norm_second):
    vectors = jnp.concatenate([v[0].reshape(-1) for v in (rate_bias, input_bias, decay_param, filter_taps, filter_bias)]).reshape(1, 256)
    gains = jnp.concatenate([norm_first[0], norm_second[0], jnp.zeros((160,), BF16)]).reshape(1, 256)
    gates = jnp.concatenate([rate_weight[0].reshape(32, 128), input_weight[0].reshape(32, 128)], axis=1)
    return jnp.concatenate([gates, vectors, gains, jnp.zeros((14, 256), BF16)], axis=0)


def shards(
    inputs, out_grad, lengths, order, gelu_weight, lru_weight, rate_weight, input_weight, rate_bias, input_bias,
    decay_param, filter_taps, filter_bias, out_weight, gate_weight, up_weight, down_weight, norm_first, norm_second
):
    group = lax.axis_index("dp")
    masks = document_masks(lax.dynamic_index_in_dim(lengths, group, 1, keepdims=False))
    small = pack_small_shard(rate_weight, input_weight, rate_bias, input_bias, decay_param, filter_taps, filter_bias, norm_first, norm_second)
    every, grad, gelu_grad, lru_grad, out_wgrad, gate_grad, up_grad, down_grad, tiny = whole(
        gelu_weight[0], lru_weight[0], out_weight[0].T, gate_weight[0], up_weight[0], down_weight[0].T, small,
        inputs.reshape(HALF, D), out_grad.reshape(HALF, D), masks
    )
    slots = jnp.arange(32, dtype=jnp.int32)
    source = jnp.sum(jnp.where(order == group, slots[None, :], 0), axis=1, dtype=jnp.int32)
    every = every.reshape(32, 2, 72, D)
    hidden = jnp.stack(
        [lax.dynamic_index_in_dim(every[:, m], source[m], 0, keepdims=False) for m in range(2)]
    ).astype(F32)[None]
    input_grad = grad.reshape(1, 2, 72, D)

    vec = tiny[32].reshape(8, 8, 4)
    return (
        hidden, input_grad, gelu_grad[None], lru_grad[None],
        tiny[0:32, 0:128].reshape(1, 8, 4, 128), tiny[0:32, 128:256].reshape(1, 8, 4, 128),
        vec[0][None], vec[1][None], vec[2][None], vec[3:7][None], vec[7][None],
        out_wgrad[None], gate_grad[None], up_grad[None], down_grad[None],
        tiny[33, 0:48][None], tiny[33, 48:96][None],
    )


def solution(mesh):
    rows = P(None, ("dp", "tensor"), None)
    tall = P("section", "dp", "tensor")
    wide = P("section", "tensor", "dp")
    block = P("section", "tensor", "dp", None)
    taps = P("section", None, "tensor", "dp")
    gain = P("section", "dp")
    params = (tall, tall, block, block, wide, wide, wide, taps, wide, wide, tall, tall, wide, gain, gain)
    out_rows = P("section", None, ("dp", "tensor"), None)
    return jax.shard_map(
        shards,
        mesh=mesh,
        in_specs=(rows, rows, P(), P()) + params,
        out_specs=(out_rows, out_rows) + params,
        check_vma=False,
    )
```

```python
import jax
import jax.numpy as jnp
from jax import lax
from jax.experimental import pallas as pl
from jax.experimental.pallas import tpu as pltpu
from jax.sharding import PartitionSpec as P

MESH = pl.DeviceIdType.MESH
F32 = jnp.float32
BF16 = jnp.bfloat16
EPS = 1e-06
FLOOR = 0.01
PIECES = 20
PW = 512
TILE = 256
HALF = 144
ALL = 288
D = 1536
QUARTER = 384
LAG = 2
SLACK = 2
VMEM_LIMIT = 63 * 2**20


def nn(a, b):
    return lax.dot_general(a, b, (((1,), (0,)), ((), ())), preferred_element_type=F32)


def nt(a, b):
    return lax.dot_general(a, b, (((1,), (1,)), ((), ())), preferred_element_type=F32)


def tn(a, b):
    return lax.dot_general(a, b, (((0,), (0,)), ((), ())), preferred_element_type=F32)


def gelu_parts(v):
    k = 0.7978845608028654
    th = jnp.tanh(k * (v + 0.044715 * v * v * v))
    half = 0.5 * (1.0 + th)
    slope = half + 0.5 * v * (1.0 - th * th) * (k * (1.0 + 0.134145 * v * v))
    return v * half, slope


def gelu(v):
    k = 0.7978845608028654
    return 0.5 * v * (1.0 + jnp.tanh(k * (v + 0.044715 * v * v * v)))


def sigmoid(v):
    return 1.0 / (1.0 + jnp.exp(-v))


def softplus(v):
    return jnp.maximum(v, 0.0) + jnp.log(1.0 + jnp.exp(-jnp.abs(v)))


def to_natural(v):
    return jnp.concatenate([v[0:72], v[144:216], v[72:144], v[216:288]], axis=0)


def to_exchange(v):
    return jnp.concatenate([v[0:72], v[144:216], v[72:144], v[216:288]], axis=0)


def down(v, k):
    return pltpu.roll(v, k, 0) if k else v


def up(v, k):
    return pltpu.roll(v, ALL - k, 0) if k else v


def scan_down(a, b):
    for s in (1, 2, 4, 8, 16, 32, 64):
        b = a * down(b, s) + b
        if s < 64:
            a = a * down(a, s)
    return b


def scan_up(a, b):
    for s in (1, 2, 4, 8, 16, 32, 64):
        b = a * up(b, s) + b
        if s < 64:
            a = a * up(a, s)
    return b


def iota(shape, dim):
    return lax.broadcasted_iota(jnp.int32, shape, dim)


def onehot(cond):
    return jnp.where(cond, 1.0, 0.0).astype(BF16)


class Ring:
    def __init__(self):
        dp = lax.axis_index("dp")
        c, z, x = dp % 2, (dp // 2) % 4, dp // 8
        self.dp, self.c, self.z, self.x = dp, c, z, x

        def at(dx, dz):
            return ((x + dx) % 4) * 8 + ((z + dz) % 4) * 2 + c

        self.ap, self.am = at(1 - c, c), at(3 * (1 - c), 3 * c)
        self.bp, self.bm = at(c, 1 - c), at(3 * c, 3 * (1 - c))
        self.sib = dp + 1 - 2 * c

    def by_colour(self, fn):
        @pl.when(self.c == 0)
        def _():
            fn(0)

        @pl.when(self.c == 1)
        def _():
            fn(1)


def by_parity(k, fn):
    @pl.when(k % 2 == 0)
    def _():
        fn(0)

    @pl.when(k % 2 == 1)
    def _():
        fn(1)


def go(src, dst, dev, ssem, rsem):
    return pltpu.make_async_remote_copy(
        src_ref=src, dst_ref=dst, send_sem=ssem, recv_sem=rsem, device_id=dev, device_id_type=MESH
    )


def gather_steps(ring, g_ref, sems):
    s1s, s1r, s2s, s2r, s3s, s3r = sems
    c, x, z = ring.c, ring.x, ring.z
    K = PIECES

    def send(r, dev, ssem, rsem):
        return go(r, r, {"dp": dev}, ssem, rsem)

    def one(k, j):
        return g_ref.at[k, (x + j * (1 - c)) % 4, (z + j * c) % 4, c]

    def p1(k, j, recv):
        if j == 0:
            return send(one(k, 3 if recv else 0), ring.ap, s1s.at[k, 0], s1r.at[k, 0])
        return send(one(k, 1 if recv else 0), ring.am, s1s.at[k, 1], s1r.at[k, 1])

    def p1f(k, par, recv):
        if par == 0:
            return send(one(k, 2 if recv else 3), ring.ap, s1s.at[k, 2], s1r.at[k, 2])
        return send(one(k, 2 if recv else 1), ring.am, s1s.at[k, 2], s1r.at[k, 2])

    def row(k, j, col):
        if col == 0:
            return g_ref.at[k, :, (z + j) % 4, 0]
        return g_ref.at[k, (x + j) % 4, :, 1]

    def p2(k, j, recv, col):
        if j == 0:
            return send(row(k, 3 if recv else 0, col), ring.bp, s2s.at[k, 0], s2r.at[k, 0])
        return send(row(k, 1 if recv else 0, col), ring.bm, s2s.at[k, 1], s2r.at[k, 1])

    def p2f(k, par, recv, col):
        if par == 0:
            return send(row(k, 2 if recv else 3, col), ring.bp, s2s.at[k, 2], s2r.at[k, 2])
        return send(row(k, 2 if recv else 1, col), ring.bm, s2s.at[k, 2], s2r.at[k, 2])

    def sb(k, j, col):
        return send(row(k, j, col), ring.sib, s3s.at[k, j], s3r.at[k, j])

    def step(t):
        @pl.when(t < K)
        def _():
            p1(t, 0, False).start()
            p1(t, 1, False).start()

        @pl.when(jnp.logical_and(t >= SLACK, t - SLACK < K))
        def _():
            k = t - SLACK

            def f(par):
                p1(k, par, True).wait_recv()
                p1f(k, par, False).start()
                p1(k, 1 - par, True).wait_recv()

            by_parity(k, f)

        @pl.when(jnp.logical_and(t >= 2 * SLACK, t - 2 * SLACK < K))
        def _():
            k = t - 2 * SLACK
            by_parity(k, lambda par: p1f(k, par, True).wait_recv())

            def f(col):
                p2(k, 0, False, col).start()
                p2(k, 1, False, col).start()
                sb(k, 0, col).start()

            ring.by_colour(f)

        @pl.when(jnp.logical_and(t >= 3 * SLACK, t - 3 * SLACK < K))
        def _():
            k = t - 3 * SLACK

            def f(col):
                def h(par):
                    p2(k, par, True, col).wait_recv()
                    p2f(k, par, False, col).start()
                    p2(k, 1 - par, True, col).wait_recv()

                by_parity(k, h)
                sb(k, 1, col).start()
                sb(k, 3, col).start()

            ring.by_colour(f)

        @pl.when(t >= 4 * SLACK)
        def _():
            k = t - 4 * SLACK

            def f(col):
                by_parity(k, lambda par: p2f(k, par, True, col).wait_recv())
                sb(k, 2, col).start()

            ring.by_colour(f)

    def ready(k):
        def f(col):
            for j in range(4):
                send(row(k, j, 1 - col), ring.sib, s3s.at[k, j], s3r.at[k, j]).wait_recv()

        ring.by_colour(f)

    def finish(k, carry):
        p1(k, 0, False).wait_send()
        p1(k, 1, False).wait_send()
        by_parity(k, lambda par: p1f(k, par, False).wait_send())

        def f(col):
            p2(k, 0, False, col).wait_send()
            p2(k, 1, False, col).wait_send()
            by_parity(k, lambda par: p2f(k, par, False, col).wait_send())
            for j in range(4):
                sb(k, j, col).wait_send()

        ring.by_colour(f)
        return carry

    return step, ready, lambda: lax.fori_loop(0, K, finish, 0)


def deal_steps(ring, res, hid, sems):
    s1s, s1r, s2s, s2r, s3s, s3r, lsem = sems
    c, x, z = ring.c, ring.x, ring.z
    parts = (pl.ds(0, 80), pl.ds(80, 64))

    def send(r, dev, ssem, rsem):
        return go(r, r, {"dp": dev}, ssem, rsem)

    def one(j):
        return hid.at[(x + j * (1 - c)) % 4, (z + j * c) % 4, c]

    def row(j, col):
        if col == 0:
            return hid.at[:, (z + j) % 4, 0]
        return hid.at[(x + j) % 4, :, 1]

    def p1(i, recv):
        if i == 0:
            return send(one(3 if recv else 0), ring.ap, s1s.at[0], s1r.at[0])
        if i == 1:
            return send(one(1 if recv else 0), ring.am, s1s.at[1], s1r.at[1])
        if i == 2:
            return send(one(2 if recv else 3).at[parts[0]], ring.ap, s1s.at[2], s1r.at[2])
        return send(one(2 if recv else 1).at[parts[1]], ring.am, s1s.at[3], s1r.at[3])

    def p2(i, recv, col):
        if i == 0:
            return send(row(3 if recv else 0, col), ring.bp, s2s.at[0], s2r.at[0])
        if i == 1:
            return send(row(1 if recv else 0, col), ring.bm, s2s.at[1], s2r.at[1])
        if i == 2:
            return send(row(2 if recv else 3, col).at[:, parts[0]], ring.bp, s2s.at[2], s2r.at[2])
        return send(row(2 if recv else 1, col).at[:, parts[1]], ring.bm, s2s.at[3], s2r.at[3])

    def sb(j, col):
        return send(row(j, col), ring.sib, s3s.at[j], s3r.at[j])

    def step(t):
        if t == 0:
            local = pltpu.make_async_copy(res, one(0), lsem)
            local.start()
            local.wait()
            p1(0, False).start()
            p1(1, False).start()
        elif t == 1:
            p1(0, True).wait_recv()
            p1(2, False).start()
            p1(1, True).wait_recv()
            p1(3, False).start()
        elif t == 2:
            p1(2, True).wait_recv()
            p1(3, True).wait_recv()

            def f(col):
                p2(0, False, col).start()
                p2(1, False, col).start()
                sb(0, col).start()

            ring.by_colour(f)
        elif t == 3:
            def f(col):
                p2(0, True, col).wait_recv()
                p2(2, False, col).start()
                sb(3, col).start()
                p2(1, True, col).wait_recv()
                p2(3, False, col).start()
                sb(1, col).start()

            ring.by_colour(f)
        elif t == 4:
            def f(col):
                p2(2, True, col).wait_recv()
                p2(3, True, col).wait_recv()
                sb(2, col).start()

            ring.by_colour(f)
        else:
            for i in range(4):
                p1(i, False).wait_send()

            def f(col):
                for i in range(4):
                    p2(i, False, col).wait_send()
                    sb(i, col).wait_send()
                    send(row(i, 1 - col), ring.sib, s3s.at[i], s3r.at[i]).wait_recv()

            ring.by_colour(f)

    return step


def reduce_steps(ring, g_ref, left, right, leftt, pp, outs, stage, free, pack, sems):
    sbs, sbr, s1s, s1r, s2s, s2r, osem = sems
    c, x, z = ring.c, ring.x, ring.z
    K = PIECES

    def send(src, dst, dev, ssem, rsem):
        return go(src, dst, {"dp": dev}, ssem, rsem)

    def turn_left(li):
        def body(i, carry):
            cols = pl.ds(pl.multiple_of(i * 128, 128), 128)
            leftt[cols, :] = left[li, :, cols].T
            return carry
        lax.fori_loop(0, 12, body, 0)

    def one(k, j):
        return k, (x + j * (1 - c)) % 4, (z + j * c) % 4, 0

    def row(k, j, col):
        if col == 0:
            return k, slice(None), (z + j) % 4, 0
        return k, (x + j) % 4, slice(None), 0

    def sib(k, col):
        return send(pp.at[k % 2, :, :, 1 - col], g_ref.at[k, :, :, 0], ring.sib, sbs.at[k], sbr.at[k])

    def p1(k, i, j, dev, col):
        return send(g_ref.at[row(k, j, col)], g_ref.at[k, i, :, 1], dev, s1s.at[k, i], s1r.at[k, i])

    def p2(k, i, j, dev):
        return send(g_ref.at[one(k, j)], g_ref.at[k, 3, i, 1], dev, s2s.at[k, i], s2r.at[k, i])

    def add(a, b):
        return a.astype(F32) + b.astype(F32)

    gelu_o, lru_o, out_o, gate_o, up_o, down_o, small_o = outs

    def groups(k):
        slot = k % 2

        def flat(ref, first, width=PW, lane=0, sem=0):
            to = ref.at[:, pl.ds(pl.multiple_of(first, 128), width)]
            return pltpu.make_async_copy(stage.at[slot, :, pl.ds(lane, width)], to, osem.at[slot, sem])

        def between(low, high):
            return jnp.logical_and(k >= low, k <= high)

        return (
            (between(1, 2), lambda: (flat(gelu_o, (k - 1) * PW),)),
            (between(3, 4), lambda: (flat(lru_o, (k - 3) * PW),)),
            (between(5, 6), lambda: (flat(out_o, (k - 5) * PW),)),
            (between(7, 15), lambda: (flat(gate_o, (k - 7) * TILE, TILE), flat(up_o, (k - 7) * TILE, TILE, TILE, 1))),
            (between(16, 19), lambda: (flat(down_o, (k - 16) * PW),)),
            (k == 0, lambda: (flat(down_o, 4 * PW, TILE), flat(small_o, 0, TILE, TILE, 1))),
        )

    def put(k, value):
        stage[k % 2] = value
        for cond, copies in groups(k):
            @pl.when(cond)
            def _(copies=copies):
                for copy in copies():
                    copy.start()

    def put_wait(k):
        for cond, copies in groups(k):
            @pl.when(cond)
            def _(copies=copies):
                for copy in copies():
                    copy.wait()

    def step(t, low, high):
        for li, when in ((3, 0), (2, 4), (1, 13), (0, 15), (3, 19)):
            if not low <= when <= high:
                continue

            @pl.when(t == when)
            def _(li=li):
                turn_left(li)

        for group, when in ((0, 0), (1, 4), (2, 13), (3, 15)):
            if not low <= when <= high:
                continue

            @pl.when(t == when)
            def _(group=group):
                pl.semaphore_wait(free.at[group], 5)

        @pl.when(jnp.logical_and(t >= 5 * LAG, t - 5 * LAG < K))
        def _():
            k = K - 1 - t + 5 * LAG
            p2(k, 1, 1, ring.ap).wait_recv()
            p2(k, 2, 3, ring.am).wait_recv()

            @pl.when(t >= 5 * LAG + 2)
            def _():
                put_wait(k + 2)

            put(k, add(g_ref[one(k, 0)], g_ref[k, 3, 1, 1]) + g_ref[k, 3, 2, 1].astype(F32))

        @pl.when(jnp.logical_and(t >= 4 * LAG, t - 4 * LAG < K))
        def _():
            k = K - 1 - t + 4 * LAG

            def h(par):
                j = 1 if par == 0 else 3
                p2(k, 0, 2, ring.ap).wait_recv()
                g_ref[one(k, j)] = add(g_ref[one(k, j)], g_ref[k, 3, 0, 1]).astype(BF16)
                if par == 0:
                    p2(k, 1, 1, ring.ap).start()
                else:
                    p2(k, 2, 3, ring.am).start()

            by_parity(k, h)

        @pl.when(jnp.logical_and(t >= 3 * LAG, t - 3 * LAG < K))
        def _():
            k = K - 1 - t + 3 * LAG

            def f(col):
                p1(k, 1, 1, ring.bp, col).wait_recv()
                p1(k, 2, 3, ring.bm, col).wait_recv()
                mine = row(k, 0, col)
                g_ref[mine] = (add(g_ref[mine], g_ref[k, 1, :, 1]) + g_ref[k, 2, :, 1].astype(F32)).astype(BF16)

            ring.by_colour(f)

            def h(par):
                if par == 0:
                    p2(k, 0, 2, ring.ap).start()
                    p2(k, 2, 3, ring.am).start()
                else:
                    p2(k, 0, 2, ring.am).start()
                    p2(k, 1, 1, ring.ap).start()

            by_parity(k, h)

        @pl.when(jnp.logical_and(t >= 2 * LAG, t - 2 * LAG < K))
        def _():
            k = K - 1 - t + 2 * LAG

            def f(col):
                def h(par):
                    j = 1 if par == 0 else 3
                    p1(k, 0, 2, ring.bp, col).wait_recv()
                    g_ref[row(k, j, col)] = add(g_ref[row(k, j, col)], g_ref[k, 0, :, 1]).astype(BF16)
                    if par == 0:
                        p1(k, 1, 1, ring.bp, col).start()
                    else:
                        p1(k, 2, 3, ring.bm, col).start()

                by_parity(k, h)

            ring.by_colour(f)

        @pl.when(jnp.logical_and(t >= 1 * LAG, t - 1 * LAG < K))
        def _():
            k = K - 1 - t + 1 * LAG

            def f(col):
                sib(k, col).wait_recv()

                def body(xx, carry):
                    g_ref[k, xx, :, 0] = add(g_ref[k, xx, :, 0], pp[k % 2, xx, :, col]).astype(BF16)
                    return carry

                lax.fori_loop(0, 4, body, 0)

                def h(par):
                    if par == 0:
                        p1(k, 0, 2, ring.bp, col).start()
                        p1(k, 2, 3, ring.bm, col).start()
                    else:
                        p1(k, 0, 2, ring.bm, col).start()
                        p1(k, 1, 1, ring.bp, col).start()

                by_parity(k, h)

            ring.by_colour(f)

        @pl.when(t < K)
        def _():
            k = K - 1 - t

            @pl.when(t >= 2)
            def _():
                ring.by_colour(lambda col: sib(k + 2, col).wait_send())

            def body(xx, carry):
                rows = pl.ds(pl.multiple_of(xx * QUARTER, 16), QUARTER)
                part = nn(leftt[rows, :], right[k]).astype(BF16)
                pp[k % 2, xx] = part.reshape(4, 2, 48, PW)
                return carry

            lax.fori_loop(0, 4, body, 0)

            if high >= K - 1:
                pl.when(k == 0)(pack)

            ring.by_colour(lambda col: sib(k, col).start())

    def finish_one(k, carry):
        def f(col):
            @pl.when(k < 2)
            def _():
                sib(k, col).wait_send()
                put_wait(k)

            for i in range(3):
                p1(k, i, 1, ring.bp, col).wait_send()

        ring.by_colour(f)
        for i in range(3):
            p2(k, i, 1, ring.ap).wait_send()
        return carry

    return step, lambda: lax.fori_loop(0, K, finish_one, 0)


def whole_kernel(
    gelu_ref, lru_ref, out_ref, gate_ref, up_ref, down_ref, small_ref, xin_ref, ein_ref, mask_ref,
    hid_out, grad_out, gelu_o, lru_o, out_o, gate_o, up_o, down_o, small_o,
    g_ref, xall, left, right, pf, cv, rg, ig, st, mid, own, sb, rb, gmid, rw, vec, vgrad, gains, gsum, gpart, sgrad, acc,
    leftt, pp, stage, res,
    lsem, psem_s, psem_r, free, hand_s, hand_r, back_s, back_r, *more,
):
    sec = lax.axis_index("section")
    t = lax.axis_index("tensor")
    ring = Ring()
    barrier = pltpu.get_barrier_semaphore()
    others = [{"dp": d} for d in (ring.ap, ring.am, ring.bp, ring.bm, ring.sib)] + [{"tensor": 1 - t}, {"section": 1 - sec}, {"section": 1 - sec, "tensor": 1 - t}]
    for dev in others:
        pl.semaphore_signal(barrier, inc=1, device_id=dev, device_id_type=MESH)
    loads = []

    def load(src, col, width, piece, lane):
        part = src.at[:, pl.ds(col, width)]
        to = g_ref.at[piece, ring.x, ring.z, ring.c, :, pl.ds(lane, width)]
        loads.append(pltpu.make_async_copy(part, to, lsem.at[len(loads)]))

    load(down_ref, 2048, 256, 0, 0)
    load(small_ref, 0, 256, 0, 256)
    for i in range(2):
        load(gelu_ref, i * 512, 512, 1 + i, 0)
        load(lru_ref, i * 512, 512, 3 + i, 0)
        load(out_ref, i * 512, 512, 5 + i, 0)
    for i in range(9):
        load(gate_ref, i * 256, 256, 7 + i, 0)
        load(up_ref, i * 256, 256, 7 + i, 256)
    for i in range(4):
        load(down_ref, i * 512, 512, 16 + i, 0)
    for copy in loads:
        copy.start()
    my = pl.ds(pl.multiple_of(t * HALF, 16), HALF)
    his = pl.ds(pl.multiple_of((1 - t) * HALF, 16), HALF)
    xcopy = pltpu.make_async_copy(xin_ref, xall.at[t], lsem.at[30])
    ecopy = pltpu.make_async_copy(ein_ref, left.at[3, my], lsem.at[31])

    @pl.when(sec == 0)
    def _():
        xcopy.start()

    @pl.when(sec == 1)
    def _():
        ecopy.start()

    pl.semaphore_wait(barrier, 8)
    for copy in loads:
        copy.wait()

    def pair(src, dst, i):
        return go(src, dst, {"tensor": 1 - t}, psem_s.at[i], psem_r.at[i])

    def share(li, i):
        return pair(left.at[li, my], left.at[li, my], i)

    def shared(li, i):
        return pair(left.at[li, his], left.at[li, his], i)

    def rows48(i):
        return pl.ds(pl.multiple_of(i * 48, 16), 48)

    def half48(h, i):
        return pl.ds(pl.multiple_of(h * HALF + i * 48, 16), 48)

    def hand(to, r):
        dev = {"section": 1 - sec, "tensor": (t + to) % 2}
        return go(res.at[rows48(r)], xall.at[t, rows48(r)], dev, hand_s.at[to, r], hand_r.at[t, r])

    def handed(h, r):
        to = xall.at[h, rows48(r)]
        return go(to, to, {"section": 1 - sec}, hand_s.at[0, r], hand_r.at[h, r])

    def hand_back(to, r):
        dev = {"section": 1 - sec, "tensor": (t + to) % 2}
        return go(res.at[rows48(r)], left.at[3, half48(t, r)], dev, back_s.at[to, r], back_r.at[t, r])

    def handed_back(h, r):
        to = left.at[3, half48(h, r)]
        return go(to, to, {"section": 1 - sec}, back_s.at[0, r], back_r.at[h, r])

    ag_step, ag_ready, ag_finish = gather_steps(ring, g_ref, more[0:6])
    deal = deal_steps(ring, res, hid_out, more[6:13])

    @pl.when(sec == 0)
    def _():
        def body(i, carry):
            ag_step(i)
            return carry
        lax.fori_loop(0, 4 * SLACK + 1, body, 0)
        ag_ready(0)
        xcopy.wait()

    @pl.when(sec == 1)
    def _():
        ecopy.wait()
        share(3, 10).start()

        def body(i, carry):
            ag_step(i)
            return carry

        lax.fori_loop(0, PIECES + 4 * SLACK, body, 0)

        def await_piece(i, carry):
            ag_ready(i)
            return carry

        lax.fori_loop(0, PIECES, await_piece, 0)

    def beside(piece):
        @pl.when(sec == 0)
        def _():
            ag_step(piece + 4 * SLACK)
            ag_ready(piece)

    def wt(piece, lane):
        return g_ref[piece, :, :, :, :, pl.ds(pl.multiple_of(lane, TILE), TILE)].reshape(D, TILE)

    def wc(piece):
        return g_ref[piece].reshape(D, PW)

    def wq(piece, x, width=PW):
        return g_ref[piece, x, :, :, :, 0:width].reshape(QUARTER, width)

    right[0] = jnp.zeros((ALL, PW), BF16)
    small = wt(0, TILE)

    def unpack(j, carry):
        ci, r = iota((128, D), 0), iota((128, D), 1)
        sel = onehot(r == (ci // 4) * 48 + j * 4 + ci % 4)
        rw[j] = nn(sel, small).astype(BF16)
        return carry

    lax.fori_loop(0, 8, unpack, 0)
    dpi, r = iota((32, D), 0), iota((32, D), 1)
    t32 = nn(onehot(r == dpi * 48 + 32), small).astype(BF16)
    d1 = onehot(iota((32, 128), 1) // 4 == iota((32, 128), 0))
    e1 = tn(t32, d1)
    e1 = jnp.where(iota((256, 128), 0) % 4 == iota((256, 128), 1) % 4, e1, 0.0).astype(BF16)
    v1 = nn(onehot(iota((64, 256), 1) // 4 == iota((64, 256), 0)), e1)
    for i in range(64):
        vec[i] = v1[i:i + 1, :]
    t33 = nn(onehot(r == dpi * 48 + 33), small).astype(BF16)
    d2 = onehot(jnp.logical_and(r >= dpi * 48, r < dpi * 48 + 48))
    e2 = tn(t33[:, 0:128], d2)
    within = iota((128, D), 1) % 48
    q = iota((128, D), 0)
    gains[0] = jnp.sum(jnp.where(q == within, e2, 0.0), axis=0, keepdims=True)
    gains[1] = jnp.sum(jnp.where(q == within + 48, e2, 0.0), axis=0, keepdims=True)

    def scale_of(v):
        return lax.rsqrt(jnp.mean(v * v, axis=1, keepdims=True) + EPS)

    def norm_one(h, i):
        v = xall[h, rows48(i), :].astype(F32)
        left[0, half48(h, i), :] = (v * scale_of(v) * gains[0]).astype(BF16)

    def into_branches(rows, first):
        def body(i, carry):
            if first:
                beside(1 + i)
            elif first is False:
                pl.when(i < 2)(lambda: beside(5 + i))
            pf[i, rows, :] = nn(left[0, rows, :], wc(1 + i))
            return carry
        lax.fori_loop(0, 4, body, 0)

    @pl.when(sec == 0)
    def _():
        def body(i, carry):
            norm_one(t, i)
            return carry

        lax.fori_loop(0, 3, body, 0)
        share(0, 0).start()
        into_branches(my, True)
        shared(0, 0).wait_recv()
        into_branches(his, False)

    @pl.when(sec == 1)
    def _():
        def body(i, carry):
            for h in range(2):
                handed(h, i).wait_recv()
                norm_one(h, i)
            return carry

        lax.fori_loop(0, 3, body, 0)
        into_branches(slice(None), None)

    def vrow(a, j):
        return vec[a * 8 + j]

    def lanes_of(i, h):
        return pl.ds(pl.multiple_of((i % 2) * 256 + h * 128, 128), 128)

    def mixer(i, carry):
        beside(7 + i)
        for h in range(2):
            j = i * 2 + h
            lanes = lanes_of(i, h)
            feature = to_natural(pf[2 + i // 2, :, lanes])
            filtered = vrow(7, j)
            for k in range(4):
                filtered = filtered + vrow(3 + k, j) * (down(feature, k) * mask_ref[k - 1] if k else feature)
            low = filtered.astype(BF16)
            cv[j] = low
            conv = low.astype(F32)
            pre = nn(low, rw[j])
            rate = sigmoid(pre[:, 0:128] + vrow(0, j))
            inp = sigmoid(pre[:, 128:256] + vrow(1, j))
            rg[j] = rate
            ig[j] = inp
            decay = jnp.exp(-8.0 * rate * softplus(-vrow(2, j)))
            scale_in = jnp.sqrt(jnp.maximum(1.0 - decay * decay, FLOOR))
            state = scan_down(decay * mask_ref[0], scale_in * inp * conv)
            st[j] = state
            right[5 + i // 2, :, lanes] = (to_exchange(state) * gelu(pf[i // 2, :, lanes])).astype(BF16)
        return carry

    lax.fori_loop(0, 4, mixer, 0)

    def reduce_out(pieces, base, turn, also):
        def body(x, carry):
            total = None
            for piece in pieces:
                width = PW if piece else TILE
                part = nt(right[piece, :, 0:width], wq(piece, x, width))
                total = part if total is None else total + part
            acc[...] = total
            sb[x] = acc[his, :].astype(BF16)
            pair(sb.at[x], rb.at[turn, x], base + x).start()
            own[x] = acc[my, :]
            also(x)
            return carry

        lax.fori_loop(0, 4, body, 0)

    def reduce_wait(base, turn):
        for x in range(4):
            pair(sb.at[x], rb.at[turn, x], base + x).wait()

    def summed(i, turn):
        rows = rows48(i)
        return jnp.concatenate([own[x, rows, :] + rb[turn, x, rows, :].astype(F32) for x in range(4)], axis=1)

    reduce_out((5, 6), 1, 0, lambda x: beside(11 + x))
    reduce_wait(1, 0)

    def norm_two(i, carry):
        v = xall[t, rows48(i), :].astype(F32) + summed(i, 0)
        mid[rows48(i), :] = v
        left[2, half48(t, i), :] = (v * scale_of(v) * gains[1]).astype(BF16)
        return carry

    lax.fori_loop(0, 3, norm_two, 0)
    share(2, 5).start()

    def hidden_at(i):
        return (16 + i // 2) % PIECES, pl.multiple_of((i % 2) * TILE, TILE)

    def feed(rows, first):
        def body(i, carry):
            if first:
                pl.when(i % 4 == 0)(lambda: beside(15 + i // 4))
            else:
                pl.when(jnp.logical_or(i == 3, i == 7))(lambda: beside(18 + i // 7))
            both = nn(left[2, rows, :], wc(7 + i))
            pg, pu = both[:, 0:TILE], both[:, TILE:PW]
            right[7 + i, rows, :] = both.astype(BF16)
            piece, lane = hidden_at(i)
            right[piece, rows, pl.ds(lane, TILE)] = (gelu(pg) * pu).astype(BF16)
            return carry
        lax.fori_loop(0, 9, body, 0)

    feed(my, True)
    shared(2, 5).wait_recv()
    feed(his, False)
    reduce_out((16, 17, 18, 19, 0), 6, 1, lambda x: None)
    reduce_wait(6, 1)

    def finish_forward(i, carry):
        v = mid[rows48(i), :] + summed(i, 1)
        res[rows48(i), :] = v.astype(BF16)

        @pl.when(sec == 0)
        def _():
            hand(0, i).start()
            hand(1, i).start()

        return carry

    lax.fori_loop(0, 3, finish_forward, 0)

    @pl.when(sec == 0)
    def _():
        for i in range(5):
            deal(i)
        for h in range(2):
            for r in range(3):
                handed_back(h, r).wait_recv()

    def deal_beside(i):
        @pl.when(sec == 1)
        def _():
            deal(i)

    deal_beside(0)
    ag_finish()
    @pl.when(sec == 1)
    def _():
        shared(3, 10).wait_recv()

    def feed_back(i, carry):
        piece, lane = hidden_at(i)
        gh = nn(left[3], wt(piece, lane))
        pg = right[7 + i, :, 0:TILE].astype(F32)
        pu = right[7 + i, :, TILE:PW].astype(F32)
        act, slope = gelu_parts(pg)
        right[7 + i, :, 0:TILE] = (gh * pu * slope).astype(BF16)
        right[7 + i, :, TILE:PW] = (gh * act).astype(BF16)
        return carry

    lax.fori_loop(0, 9, feed_back, 0)
    around = (ring.ap, ring.am, ring.bp, ring.bm, ring.sib)

    def release(group):
        for dev in around:
            pl.semaphore_signal(free.at[group], inc=1, device_id={"dp": dev}, device_id_type=MESH)

    rs_step, rs_finish = reduce_steps(ring, g_ref, left, right, leftt, pp, (gelu_o, lru_o, out_o, gate_o, up_o, down_o, small_o), stage, free, lambda: pack_small(), more[13:20])

    def sum_beside(i, low, high):
        @pl.when(sec == 0)
        def _():
            rs_step(i, low, high)

    release(0)
    deal_beside(1)
    reduce_out(tuple(range(7, 16)), 11, 0, lambda x: sum_beside(x, 0, 3))
    release(1)
    reduce_wait(11, 0)

    def eight(v):
        total = v[0:8]
        for i in range(1, 6):
            total = total + v[i * 8:i * 8 + 8]
        return total

    def middle_back(i, carry):
        ng = summed(i, 0)
        m = mid[rows48(i), :]
        sc = scale_of(m)
        u = ng * gains[1]
        e = left[3, half48(t, i), :].astype(F32)
        gm = e + sc * u - m * (sc * sc * sc) * jnp.mean(u * m, axis=1, keepdims=True)
        gmid[rows48(i), :] = gm
        left[1, half48(t, i), :] = gm.astype(BF16)
        return carry + eight(ng * m * sc)

    gpart[1] = lax.fori_loop(0, 3, middle_back, jnp.zeros((8, D), F32))
    share(1, 15).start()
    deal_beside(2)
    sum_beside(4, 4, 4)
    shared(1, 15).wait_recv()

    def mixer_back(i, carry):
        gmix = nn(left[1], wt(5 + i // 2, (i % 2) * TILE))
        sum_beside(5 + i, 5, 8)
        for h in range(2):
            j = i * 2 + h
            lanes = lanes_of(i, h)
            gm = gmix[:, h * 128:h * 128 + 128]
            act, slope = gelu_parts(pf[i // 2, :, lanes])
            state = st[j]
            right[1 + i // 2, :, lanes] = (gm * to_exchange(state) * slope).astype(BF16)
            grad_state = to_natural(gm * act)
            rate, inp = rg[j], ig[j]
            conv = cv[j].astype(F32)
            forget = softplus(-vrow(2, j))
            decay = jnp.exp(-8.0 * rate * forget)
            spare = 1.0 - decay * decay
            scale_in = jnp.sqrt(jnp.maximum(spare, FLOOR))
            m1 = mask_ref[0]
            drive = scan_up(up(decay * m1, 1), grad_state)
            grad_spare = jnp.where(spare > FLOOR, 0.5 * (drive * inp * conv) / scale_in, 0.0)
            grad_decay = drive * down(state, 1) * m1 - 2.0 * decay * grad_spare
            grad_log = grad_decay * decay
            rate_low = (grad_log * (-8.0 * forget) * rate * (1.0 - rate)).astype(BF16)
            driven = drive * scale_in
            input_low = (driven * conv * inp * (1.0 - inp)).astype(BF16)
            both = jnp.concatenate([rate_low, input_low], axis=1)
            back = nt(both, rw[j])
            vgrad[0 * 8 + j] = jnp.sum(rate_low.astype(F32), axis=0, keepdims=True)
            vgrad[1 * 8 + j] = jnp.sum(input_low.astype(F32), axis=0, keepdims=True)
            grad_forget = jnp.sum(grad_log * (-8.0 * rate), axis=0, keepdims=True)
            vgrad[2 * 8 + j] = -grad_forget * sigmoid(-vrow(2, j))
            sgrad[j] = tn(cv[j], both).astype(BF16)
            grad_conv = driven * inp + back
            feature = to_natural(pf[2 + i // 2, :, lanes])
            grad_feature = None
            for k in range(4):
                masked = grad_conv * mask_ref[k - 1] if k else grad_conv
                vgrad[(3 + k) * 8 + j] = jnp.sum(masked * down(feature, k), axis=0, keepdims=True)
                term = up(masked, k) * vrow(3 + k, j)
                grad_feature = term if grad_feature is None else grad_feature + term
            vgrad[7 * 8 + j] = jnp.sum(grad_conv, axis=0, keepdims=True)
            right[3 + i // 2, :, lanes] = to_exchange(grad_feature).astype(BF16)
        return carry

    lax.fori_loop(0, 4, mixer_back, 0)
    release(2)
    deal_beside(3)
    reduce_out((1, 2, 3, 4), 16, 1, lambda x: sum_beside(9 + x, 9, 12))
    release(3)
    reduce_wait(16, 1)

    def first_back(i, carry):
        fg = summed(i, 1)
        v = xall[t, rows48(i), :].astype(F32)
        sc = scale_of(v)
        u = fg * gains[0]
        gv = gmid[rows48(i), :] + sc * u - v * (sc * sc * sc) * jnp.mean(u * v, axis=1, keepdims=True)
        mid[rows48(i), :] = gv

        @pl.when(sec == 1)
        def _():
            res[rows48(i), :] = gv.astype(BF16)
            hand_back(0, i).start()
            hand_back(1, i).start()

        return carry + eight(fg * v * sc)

    gpart[0] = lax.fori_loop(0, 3, first_back, jnp.zeros((8, D), F32))
    pair(gpart, gsum, 20).start()
    grad_copy = pltpu.make_async_copy(mid, grad_out, lsem.at[0])
    grad_copy.start()
    deal_beside(4)

    v2 = jnp.concatenate([vgrad[i] for i in range(64)], axis=0).astype(BF16)
    e2 = nn(onehot(iota((256, 64), 0) // 4 == iota((256, 64), 1)), v2)
    e2 = jnp.where(iota((256, 128), 0) % 4 == iota((256, 128), 1) % 4, e2, 0.0).astype(BF16)
    t32 = nt(d1, e2).astype(BF16)
    pair(gpart, gsum, 20).wait()
    n1 = jnp.sum(gpart[0] + gsum[0], axis=0, keepdims=True)
    n2 = jnp.sum(gpart[1] + gsum[1], axis=0, keepdims=True)
    spread = jnp.where(q == within, n1, jnp.where(q == within + 48, n2, 0.0)).astype(BF16)
    t33 = nt(d2, spread).astype(BF16)
    t33 = jnp.concatenate([t33, jnp.zeros((32, 128), BF16)], axis=1)

    def pack_part(x, carry):
        r = iota((QUARTER, 128), 0) + x * QUARTER
        ci = iota((QUARTER, 128), 1)
        total = None
        for j in range(8):
            sel = onehot(r == (ci // 4) * 48 + j * 4 + ci % 4)
            part = nn(sel, sgrad[j])
            total = part if total is None else total + part
        r = iota((QUARTER, 32), 0) + x * QUARTER
        dpi = iota((QUARTER, 32), 1)
        total = total + nn(onehot(r == dpi * 48 + 32), t32) + nn(onehot(r == dpi * 48 + 33), t33)
        pp[0, x, :, :, :, TILE:PW] = total.astype(BF16).reshape(4, 2, 48, TILE)
        return carry

    def pack_small():
        lax.fori_loop(0, 4, pack_part, 0)

    def last(i, carry):
        rs_step(i, 0, PIECES + 5 * LAG - 1)
        return carry

    lax.fori_loop(jnp.where(sec == 0, 13, 0), PIECES + 5 * LAG, last, 0)
    rs_finish()
    deal(5)
    share(2, 5).wait_send()
    share(1, 15).wait_send()

    @pl.when(sec == 0)
    def _():
        share(0, 0).wait_send()
        for to in range(2):
            for r in range(3):
                hand(to, r).wait_send()

    @pl.when(sec == 1)
    def _():
        share(3, 10).wait_send()
        for to in range(2):
            for r in range(3):
                hand_back(to, r).wait_send()

    grad_copy.wait()


def whole(gelu, lru, out, gate, up_, down_, small, xin, ein, masks):
    K = PIECES
    dma = pltpu.SemaphoreType.DMA
    vmem = pl.BlockSpec(memory_space=pltpu.VMEM)
    hbm = pl.BlockSpec(memory_space=pl.ANY)
    sds = jax.ShapeDtypeStruct
    return pl.pallas_call(
        whole_kernel,
        name="whole",
        out_shape=(
            sds((4, 4, 2, HALF, D), BF16), sds((HALF, D), F32),
            sds((48, 1024), F32), sds((48, 1024), F32), sds((48, 1024), F32),
            sds((48, 2304), F32), sds((48, 2304), F32), sds((48, 2304), F32), sds((48, TILE), F32),
        ),
        in_specs=[hbm] * 9 + [vmem],
        out_specs=(hbm,) * 9,
        scratch_shapes=[
            pltpu.VMEM((K, 4, 4, 2, 48, PW), BF16),
            pltpu.VMEM((2, HALF, D), BF16),
            pltpu.VMEM((4, ALL, D), BF16),
            pltpu.VMEM((K, ALL, PW), BF16),
            pltpu.VMEM((4, ALL, PW), F32),
            pltpu.VMEM((8, ALL, 128), BF16),
            pltpu.VMEM((8, ALL, 128), F32),
            pltpu.VMEM((8, ALL, 128), F32),
            pltpu.VMEM((8, ALL, 128), F32),
            pltpu.VMEM((HALF, D), F32),
            pltpu.VMEM((4, HALF, QUARTER), F32),
            pltpu.VMEM((4, HALF, QUARTER), BF16),
            pltpu.VMEM((2, 4, HALF, QUARTER), BF16),
            pltpu.VMEM((HALF, D), F32),
            pltpu.VMEM((8, 128, 256), BF16),
            pltpu.VMEM((64, 1, 128), F32),
            pltpu.VMEM((64, 1, 128), F32),
            pltpu.VMEM((2, 1, D), F32),
            pltpu.VMEM((2, 8, D), F32),
            pltpu.VMEM((2, 8, D), F32),
            pltpu.VMEM((8, 128, 256), BF16),
            pltpu.VMEM((ALL, QUARTER), F32),
            pltpu.VMEM((D, ALL), BF16),
            pltpu.VMEM((2, 4, 4, 2, 48, PW), BF16),
            pltpu.VMEM((2, 48, PW), F32),
            pltpu.VMEM((HALF, D), BF16),
            dma((32,)), dma((21,)), dma((21,)), pltpu.SemaphoreType.REGULAR((4,)),
            dma((2, 3)), dma((2, 3)), dma((2, 3)), dma((2, 3)),
            dma((K, 3)), dma((K, 3)), dma((K, 3)), dma((K, 3)), dma((K, 4)), dma((K, 4)),
            dma((4,)), dma((4,)), dma((4,)), dma((4,)), dma((4,)), dma((4,)), dma(()),
            dma((K,)), dma((K,)), dma((K, 3)), dma((K, 3)), dma((K, 3)), dma((K, 3)), dma((2, 2)),
        ],
        compiler_params=pltpu.CompilerParams(
            collective_id=1, has_side_effects=True, vmem_limit_bytes=VMEM_LIMIT
        ),
    )(gelu, lru, out, gate, up_, down_, small, xin, ein, masks)


def settle_kernel(source_ref, every, *refs):
    ins, outs, (buf, sem, pick) = refs[0:7], refs[7:15], refs[15:18]
    hid_o = outs[0]
    picks = [pltpu.make_async_copy(every.at[source_ref[m]], buf.at[m], pick.at[m]) for m in range(2)]
    for copy in picks:
        copy.start()
    copies = [pltpu.make_async_copy(a, b, sem.at[i]) for i, (a, b) in enumerate(zip(ins, outs[1:]))]
    for copy in copies:
        copy.start()
    for copy in picks:
        copy.wait()
    hid_o[0:72, :] = buf[0].astype(F32)[0:72]
    hid_o[72:144, :] = buf[1].astype(F32)[72:144]
    for copy in copies:
        copy.wait()


def settle(source, every, *results):
    vmem = pl.BlockSpec(memory_space=pltpu.VMEM)
    hbm = pl.BlockSpec(memory_space=pl.ANY)
    return pl.pallas_call(
        settle_kernel,
        name="settle",
        out_shape=(jax.ShapeDtypeStruct((HALF, D), F32),) + tuple(jax.ShapeDtypeStruct(r.shape, F32) for r in results),
        in_specs=[pl.BlockSpec(memory_space=pltpu.SMEM), hbm] + [vmem] * 7,
        out_specs=(vmem,) + (hbm,) * 7,
        scratch_shapes=[pltpu.VMEM((2, HALF, D), BF16), pltpu.SemaphoreType.DMA((7,)), pltpu.SemaphoreType.DMA((2,))],
        compiler_params=pltpu.CompilerParams(vmem_limit_bytes=32 * 2**20),
    )(source, every, *results)


def document_masks(doc_lengths):
    ends = jnp.cumsum(doc_lengths, axis=-1, dtype=jnp.int32)
    position = jnp.arange(HALF, dtype=jnp.int32)
    ident = jnp.sum((position[None, :, None] >= ends[:, None, :]).astype(jnp.int32), axis=-1, dtype=jnp.int32)
    masks = []
    for offset in range(1, 4):
        before = jnp.pad(ident, ((0, 0), (offset, 0)), constant_values=-1)[:, :HALF]
        masks.append((before == ident).astype(F32).reshape(ALL, 1))
    return jnp.broadcast_to(jnp.stack(masks), (3, ALL, 128))


def pack_small_shard(rate_weight, input_weight, rate_bias, input_bias, decay_param, filter_taps, filter_bias, norm_first, norm_second):
    vectors = jnp.concatenate([v[0].reshape(-1) for v in (rate_bias, input_bias, decay_param, filter_taps, filter_bias)]).reshape(1, 256)
    gains = jnp.concatenate([norm_first[0], norm_second[0], jnp.zeros((160,), BF16)]).reshape(1, 256)
    gates = jnp.concatenate([rate_weight[0].reshape(32, 128), input_weight[0].reshape(32, 128)], axis=1)
    return jnp.concatenate([gates, vectors, gains, jnp.zeros((14, 256), BF16)], axis=0)


def shards(
    inputs, out_grad, lengths, order, gelu_weight, lru_weight, rate_weight, input_weight, rate_bias, input_bias,
    decay_param, filter_taps, filter_bias, out_weight, gate_weight, up_weight, down_weight, norm_first, norm_second
):
    group = lax.axis_index("dp")
    masks = document_masks(lax.dynamic_index_in_dim(lengths, group, 1, keepdims=False))
    small = pack_small_shard(rate_weight, input_weight, rate_bias, input_bias, decay_param, filter_taps, filter_bias, norm_first, norm_second)
    every, grad, gelu_grad, lru_grad, out_wgrad, gate_grad, up_grad, down_grad, tiny = whole(
        gelu_weight[0], lru_weight[0], out_weight[0].T, gate_weight[0], up_weight[0], down_weight[0].T, small,
        inputs.reshape(HALF, D), out_grad.reshape(HALF, D), masks
    )
    slots = jnp.arange(32, dtype=jnp.int32)
    source = jnp.sum(jnp.where(order == group, slots[None, :], 0), axis=1, dtype=jnp.int32)
    hidden, grad, gelu_grad, lru_grad, out_wgrad, gate_grad, up_grad, down_grad = settle(
        source, every.reshape(32, HALF, D), grad, gelu_grad, lru_grad, out_wgrad, gate_grad, up_grad, down_grad
    )
    hidden = hidden.reshape(1, 2, 72, D)
    input_grad = grad.reshape(1, 2, 72, D)
    vec = tiny[32].reshape(8, 8, 4)
    return (
        hidden, input_grad, gelu_grad[None], lru_grad[None],
        tiny[0:32, 0:128].reshape(1, 8, 4, 128), tiny[0:32, 128:256].reshape(1, 8, 4, 128),
        vec[0][None], vec[1][None], vec[2][None], vec[3:7][None], vec[7][None],
        out_wgrad.T[None], gate_grad[None], up_grad[None], down_grad.T[None],
        tiny[33, 0:48][None], tiny[33, 48:96][None],
    )


def solution(mesh):
    rows = P(None, ("dp", "tensor"), None)
    tall = P("section", "dp", "tensor")
    wide = P("section", "tensor", "dp")
    block = P("section", "tensor", "dp", None)
    taps = P("section", None, "tensor", "dp")
    gain = P("section", "dp")
    params = (tall, tall, block, block, wide, wide, wide, taps, wide, wide, tall, tall, wide, gain, gain)
    out_rows = P("section", None, ("dp", "tensor"), None)
    return jax.shard_map(
        shards,
        mesh=mesh,
        in_specs=(rows, rows, P(), P()) + params,
        out_specs=(out_rows, out_rows) + params,
        check_vma=False,
    )
```

```python
import jax
import jax.numpy as jnp
from jax import lax
from jax.experimental import pallas as pl
from jax.experimental.pallas import tpu as pltpu
from jax.sharding import PartitionSpec as P

MESH = pl.DeviceIdType.MESH
F32 = jnp.float32
BF16 = jnp.bfloat16
EPS = 1e-06
FLOOR = 0.01
PIECES = 20
PW = 512
TILE = 256
HALF = 144
ALL = 288
D = 1536
QUARTER = 384
LAG = 2
SLACK = 2
VMEM_LIMIT = 63 * 2**20


def nn(a, b):
    return lax.dot_general(a, b, (((1,), (0,)), ((), ())), preferred_element_type=F32)


def nt(a, b):
    return lax.dot_general(a, b, (((1,), (1,)), ((), ())), preferred_element_type=F32)


def tn(a, b):
    return lax.dot_general(a, b, (((0,), (0,)), ((), ())), preferred_element_type=F32)


def gelu_parts(v):
    k = 0.7978845608028654
    th = jnp.tanh(k * (v + 0.044715 * v * v * v))
    half = 0.5 * (1.0 + th)
    slope = half + 0.5 * v * (1.0 - th * th) * (k * (1.0 + 0.134145 * v * v))
    return v * half, slope


def gelu(v):
    k = 0.7978845608028654
    return 0.5 * v * (1.0 + jnp.tanh(k * (v + 0.044715 * v * v * v)))


def sigmoid(v):
    return 1.0 / (1.0 + jnp.exp(-v))


def softplus(v):
    return jnp.maximum(v, 0.0) + jnp.log(1.0 + jnp.exp(-jnp.abs(v)))


def to_natural(v):
    return jnp.concatenate([v[0:72], v[144:216], v[72:144], v[216:288]], axis=0)


def to_exchange(v):
    return jnp.concatenate([v[0:72], v[144:216], v[72:144], v[216:288]], axis=0)


def down(v, k):
    return pltpu.roll(v, k, 0) if k else v


def up(v, k):
    return pltpu.roll(v, ALL - k, 0) if k else v


def scan_down(a, b):
    for s in (1, 2, 4, 8, 16, 32, 64):
        b = a * down(b, s) + b
        if s < 64:
            a = a * down(a, s)
    return b


def scan_up(a, b):
    for s in (1, 2, 4, 8, 16, 32, 64):
        b = a * up(b, s) + b
        if s < 64:
            a = a * up(a, s)
    return b


def iota(shape, dim):
    return lax.broadcasted_iota(jnp.int32, shape, dim)


def onehot(cond):
    return jnp.where(cond, 1.0, 0.0).astype(BF16)


class Ring:
    def __init__(self):
        dp = lax.axis_index("dp")
        c, z, x = dp % 2, (dp // 2) % 4, dp // 8
        self.dp, self.c, self.z, self.x = dp, c, z, x

        def at(dx, dz):
            return ((x + dx) % 4) * 8 + ((z + dz) % 4) * 2 + c

        self.ap, self.am = at(1 - c, c), at(3 * (1 - c), 3 * c)
        self.bp, self.bm = at(c, 1 - c), at(3 * c, 3 * (1 - c))
        self.sib = dp + 1 - 2 * c

    def by_colour(self, fn):
        @pl.when(self.c == 0)
        def _():
            fn(0)

        @pl.when(self.c == 1)
        def _():
            fn(1)


def by_parity(k, fn):
    @pl.when(k % 2 == 0)
    def _():
        fn(0)

    @pl.when(k % 2 == 1)
    def _():
        fn(1)


def go(src, dst, dev, ssem, rsem):
    return pltpu.make_async_remote_copy(
        src_ref=src, dst_ref=dst, send_sem=ssem, recv_sem=rsem, device_id=dev, device_id_type=MESH
    )


def gather_steps(ring, g_ref, sems):
    s1s, s1r, s2s, s2r, s3s, s3r = sems
    c, x, z = ring.c, ring.x, ring.z
    K = PIECES

    def send(r, dev, ssem, rsem):
        return go(r, r, {"dp": dev}, ssem, rsem)

    def one(k, j):
        return g_ref.at[k, (x + j * (1 - c)) % 4, (z + j * c) % 4, c]

    def p1(k, j, recv):
        if j == 0:
            return send(one(k, 3 if recv else 0), ring.ap, s1s.at[k, 0], s1r.at[k, 0])
        return send(one(k, 1 if recv else 0), ring.am, s1s.at[k, 1], s1r.at[k, 1])

    def p1f(k, par, recv):
        if par == 0:
            return send(one(k, 2 if recv else 3), ring.ap, s1s.at[k, 2], s1r.at[k, 2])
        return send(one(k, 2 if recv else 1), ring.am, s1s.at[k, 2], s1r.at[k, 2])

    def row(k, j, col):
        if col == 0:
            return g_ref.at[k, :, (z + j) % 4, 0]
        return g_ref.at[k, (x + j) % 4, :, 1]

    def p2(k, j, recv, col):
        if j == 0:
            return send(row(k, 3 if recv else 0, col), ring.bp, s2s.at[k, 0], s2r.at[k, 0])
        return send(row(k, 1 if recv else 0, col), ring.bm, s2s.at[k, 1], s2r.at[k, 1])

    def p2f(k, par, recv, col):
        if par == 0:
            return send(row(k, 2 if recv else 3, col), ring.bp, s2s.at[k, 2], s2r.at[k, 2])
        return send(row(k, 2 if recv else 1, col), ring.bm, s2s.at[k, 2], s2r.at[k, 2])

    def sb(k, j, col):
        return send(row(k, j, col), ring.sib, s3s.at[k, j], s3r.at[k, j])

    def step(t):
        @pl.when(t < K)
        def _():
            p1(t, 0, False).start()
            p1(t, 1, False).start()

        @pl.when(jnp.logical_and(t >= SLACK, t - SLACK < K))
        def _():
            k = t - SLACK

            def f(par):
                p1(k, par, True).wait_recv()
                p1f(k, par, False).start()
                p1(k, 1 - par, True).wait_recv()

            by_parity(k, f)

        @pl.when(jnp.logical_and(t >= 2 * SLACK, t - 2 * SLACK < K))
        def _():
            k = t - 2 * SLACK
            by_parity(k, lambda par: p1f(k, par, True).wait_recv())

            def f(col):
                p2(k, 0, False, col).start()
                p2(k, 1, False, col).start()
                sb(k, 0, col).start()

            ring.by_colour(f)

        @pl.when(jnp.logical_and(t >= 3 * SLACK, t - 3 * SLACK < K))
        def _():
            k = t - 3 * SLACK

            def f(col):
                def h(par):
                    p2(k, par, True, col).wait_recv()
                    p2f(k, par, False, col).start()
                    p2(k, 1 - par, True, col).wait_recv()

                by_parity(k, h)
                sb(k, 1, col).start()
                sb(k, 3, col).start()

            ring.by_colour(f)

        @pl.when(t >= 4 * SLACK)
        def _():
            k = t - 4 * SLACK

            def f(col):
                by_parity(k, lambda par: p2f(k, par, True, col).wait_recv())
                sb(k, 2, col).start()

            ring.by_colour(f)

    def ready(k):
        def f(col):
            for j in range(4):
                send(row(k, j, 1 - col), ring.sib, s3s.at[k, j], s3r.at[k, j]).wait_recv()

        ring.by_colour(f)

    def finish(k, carry):
        p1(k, 0, False).wait_send()
        p1(k, 1, False).wait_send()
        by_parity(k, lambda par: p1f(k, par, False).wait_send())

        def f(col):
            p2(k, 0, False, col).wait_send()
            p2(k, 1, False, col).wait_send()
            by_parity(k, lambda par: p2f(k, par, False, col).wait_send())
            for j in range(4):
                sb(k, j, col).wait_send()

        ring.by_colour(f)
        return carry

    return step, ready, lambda: lax.fori_loop(0, K, finish, 0)


def deal_steps(ring, res, hid, sems):
    s1s, s1r, s2s, s2r, s3s, s3r, lsem = sems
    c, x, z = ring.c, ring.x, ring.z
    parts = (pl.ds(0, 80), pl.ds(80, 64))

    def send(r, dev, ssem, rsem):
        return go(r, r, {"dp": dev}, ssem, rsem)

    def one(j):
        return hid.at[(x + j * (1 - c)) % 4, (z + j * c) % 4, c]

    def row(j, col):
        if col == 0:
            return hid.at[:, (z + j) % 4, 0]
        return hid.at[(x + j) % 4, :, 1]

    def p1(i, recv):
        if i == 0:
            return send(one(3 if recv else 0), ring.ap, s1s.at[0], s1r.at[0])
        if i == 1:
            return send(one(1 if recv else 0), ring.am, s1s.at[1], s1r.at[1])
        if i == 2:
            return send(one(2 if recv else 3).at[parts[0]], ring.ap, s1s.at[2], s1r.at[2])
        return send(one(2 if recv else 1).at[parts[1]], ring.am, s1s.at[3], s1r.at[3])

    def p2(i, recv, col):
        if i == 0:
            return send(row(3 if recv else 0, col), ring.bp, s2s.at[0], s2r.at[0])
        if i == 1:
            return send(row(1 if recv else 0, col), ring.bm, s2s.at[1], s2r.at[1])
        if i == 2:
            return send(row(2 if recv else 3, col).at[:, parts[0]], ring.bp, s2s.at[2], s2r.at[2])
        return send(row(2 if recv else 1, col).at[:, parts[1]], ring.bm, s2s.at[3], s2r.at[3])

    def sb(j, col):
        return send(row(j, col), ring.sib, s3s.at[j], s3r.at[j])

    def step(t):
        if t == 0:
            local = pltpu.make_async_copy(res, one(0), lsem)
            local.start()
            local.wait()
            p1(0, False).start()
            p1(1, False).start()
        elif t == 1:
            p1(0, True).wait_recv()
            p1(2, False).start()
            p1(1, True).wait_recv()
            p1(3, False).start()
        elif t == 2:
            p1(2, True).wait_recv()
            p1(3, True).wait_recv()

            def f(col):
                p2(0, False, col).start()
                p2(1, False, col).start()
                sb(0, col).start()

            ring.by_colour(f)
        elif t == 3:
            def f(col):
                p2(0, True, col).wait_recv()
                p2(2, False, col).start()
                sb(3, col).start()
                p2(1, True, col).wait_recv()
                p2(3, False, col).start()
                sb(1, col).start()

            ring.by_colour(f)
        elif t == 4:
            def f(col):
                p2(2, True, col).wait_recv()
                p2(3, True, col).wait_recv()
                sb(2, col).start()

            ring.by_colour(f)
        else:
            for i in range(4):
                p1(i, False).wait_send()

            def f(col):
                for i in range(4):
                    p2(i, False, col).wait_send()
                    sb(i, col).wait_send()
                    send(row(i, 1 - col), ring.sib, s3s.at[i], s3r.at[i]).wait_recv()

            ring.by_colour(f)

    return step


def reduce_steps(ring, g_ref, left, right, leftt, pp, outs, stage, free, pack, sems):
    sbs, sbr, s1s, s1r, s2s, s2r, osem = sems
    c, x, z = ring.c, ring.x, ring.z
    K = PIECES

    def send(src, dst, dev, ssem, rsem):
        return go(src, dst, {"dp": dev}, ssem, rsem)

    def turn_left(li):
        def body(i, carry):
            cols = pl.ds(pl.multiple_of(i * 128, 128), 128)
            leftt[cols, :] = left[li, :, cols].T
            return carry
        lax.fori_loop(0, 12, body, 0)

    def one(k, j):
        return k, (x + j * (1 - c)) % 4, (z + j * c) % 4, 0

    def row(k, j, col):
        if col == 0:
            return k, slice(None), (z + j) % 4, 0
        return k, (x + j) % 4, slice(None), 0

    def sib(k, col):
        return send(pp.at[k % 2, :, :, 1 - col], g_ref.at[k, :, :, 0], ring.sib, sbs.at[k], sbr.at[k])

    def p1(k, i, j, dev, col):
        return send(g_ref.at[row(k, j, col)], g_ref.at[k, i, :, 1], dev, s1s.at[k, i], s1r.at[k, i])

    def p2(k, i, j, dev):
        return send(g_ref.at[one(k, j)], g_ref.at[k, 3, i, 1], dev, s2s.at[k, i], s2r.at[k, i])

    def add(a, b):
        return a.astype(F32) + b.astype(F32)

    gelu_o, lru_o, out_o, gate_o, up_o, down_o, small_o = outs

    def groups(k):
        slot = k % 2

        def flat(ref, first, width=PW, lane=0, sem=0):
            to = ref.at[:, pl.ds(pl.multiple_of(first, 128), width)]
            return pltpu.make_async_copy(stage.at[slot, :, pl.ds(lane, width)], to, osem.at[slot, sem])

        def between(low, high):
            return jnp.logical_and(k >= low, k <= high)

        return (
            (between(1, 2), lambda: (flat(gelu_o, (k - 1) * PW),)),
            (between(3, 4), lambda: (flat(lru_o, (k - 3) * PW),)),
            (between(5, 6), lambda: (flat(out_o, (k - 5) * PW),)),
            (between(7, 15), lambda: (flat(gate_o, (k - 7) * TILE, TILE), flat(up_o, (k - 7) * TILE, TILE, TILE, 1))),
            (between(16, 19), lambda: (flat(down_o, (k - 16) * PW),)),
            (k == 0, lambda: (flat(down_o, 4 * PW, TILE), flat(small_o, 0, TILE, TILE, 1))),
        )

    def put(k, value):
        stage[k % 2] = value
        for cond, copies in groups(k):
            @pl.when(cond)
            def _(copies=copies):
                for copy in copies():
                    copy.start()

    def put_wait(k):
        for cond, copies in groups(k):
            @pl.when(cond)
            def _(copies=copies):
                for copy in copies():
                    copy.wait()

    def step(t, low, high):
        for li, when in ((3, 0), (2, 4), (1, 13), (0, 15), (3, 19)):
            if not low <= when <= high:
                continue

            @pl.when(t == when)
            def _(li=li):
                turn_left(li)

        for group, when in ((0, 0), (1, 4), (2, 13), (3, 15)):
            if not low <= when <= high:
                continue

            @pl.when(t == when)
            def _(group=group):
                pl.semaphore_wait(free.at[group], 5)

        @pl.when(jnp.logical_and(t >= 5 * LAG, t - 5 * LAG < K))
        def _():
            k = K - 1 - t + 5 * LAG
            p2(k, 1, 1, ring.ap).wait_recv()
            p2(k, 2, 3, ring.am).wait_recv()

            @pl.when(t >= 5 * LAG + 2)
            def _():
                put_wait(k + 2)

            put(k, add(g_ref[one(k, 0)], g_ref[k, 3, 1, 1]) + g_ref[k, 3, 2, 1].astype(F32))

        @pl.when(jnp.logical_and(t >= 4 * LAG, t - 4 * LAG < K))
        def _():
            k = K - 1 - t + 4 * LAG

            def h(par):
                j = 1 if par == 0 else 3
                p2(k, 0, 2, ring.ap).wait_recv()
                g_ref[one(k, j)] = add(g_ref[one(k, j)], g_ref[k, 3, 0, 1]).astype(BF16)
                if par == 0:
                    p2(k, 1, 1, ring.ap).start()
                else:
                    p2(k, 2, 3, ring.am).start()

            by_parity(k, h)

        @pl.when(jnp.logical_and(t >= 3 * LAG, t - 3 * LAG < K))
        def _():
            k = K - 1 - t + 3 * LAG

            def f(col):
                p1(k, 1, 1, ring.bp, col).wait_recv()
                p1(k, 2, 3, ring.bm, col).wait_recv()
                mine = row(k, 0, col)
                g_ref[mine] = (add(g_ref[mine], g_ref[k, 1, :, 1]) + g_ref[k, 2, :, 1].astype(F32)).astype(BF16)

            ring.by_colour(f)

            def h(par):
                if par == 0:
                    p2(k, 0, 2, ring.ap).start()
                    p2(k, 2, 3, ring.am).start()
                else:
                    p2(k, 0, 2, ring.am).start()
                    p2(k, 1, 1, ring.ap).start()

            by_parity(k, h)

        @pl.when(jnp.logical_and(t >= 2 * LAG, t - 2 * LAG < K))
        def _():
            k = K - 1 - t + 2 * LAG

            def f(col):
                def h(par):
                    j = 1 if par == 0 else 3
                    p1(k, 0, 2, ring.bp, col).wait_recv()
                    g_ref[row(k, j, col)] = add(g_ref[row(k, j, col)], g_ref[k, 0, :, 1]).astype(BF16)
                    if par == 0:
                        p1(k, 1, 1, ring.bp, col).start()
                    else:
                        p1(k, 2, 3, ring.bm, col).start()

                by_parity(k, h)

            ring.by_colour(f)

        @pl.when(jnp.logical_and(t >= 1 * LAG, t - 1 * LAG < K))
        def _():
            k = K - 1 - t + 1 * LAG

            def f(col):
                sib(k, col).wait_recv()

                def body(xx, carry):
                    g_ref[k, xx, :, 0] = add(g_ref[k, xx, :, 0], pp[k % 2, xx, :, col]).astype(BF16)
                    return carry

                lax.fori_loop(0, 4, body, 0)

                def h(par):
                    if par == 0:
                        p1(k, 0, 2, ring.bp, col).start()
                        p1(k, 2, 3, ring.bm, col).start()
                    else:
                        p1(k, 0, 2, ring.bm, col).start()
                        p1(k, 1, 1, ring.bp, col).start()

                by_parity(k, h)

            ring.by_colour(f)

        @pl.when(t < K)
        def _():
            k = K - 1 - t

            @pl.when(t >= 2)
            def _():
                ring.by_colour(lambda col: sib(k + 2, col).wait_send())

            def body(xx, carry):
                rows = pl.ds(pl.multiple_of(xx * QUARTER, 16), QUARTER)
                part = nn(leftt[rows, :], right[k]).astype(BF16)
                pp[k % 2, xx] = part.reshape(4, 2, 48, PW)
                return carry

            lax.fori_loop(0, 4, body, 0)

            if high >= K - 1:
                pl.when(k == 0)(pack)

            ring.by_colour(lambda col: sib(k, col).start())

    def finish_one(k, carry):
        def f(col):
            @pl.when(k < 2)
            def _():
                sib(k, col).wait_send()
                put_wait(k)

            for i in range(3):
                p1(k, i, 1, ring.bp, col).wait_send()

        ring.by_colour(f)
        for i in range(3):
            p2(k, i, 1, ring.ap).wait_send()
        return carry

    return step, lambda: lax.fori_loop(0, K, finish_one, 0)


def whole_kernel(
    gelu_ref, lru_ref, out_ref, gate_ref, up_ref, down_ref, small_ref, xin_ref, ein_ref, mask_ref,
    hid_out, grad_out, gelu_o, lru_o, out_o, gate_o, up_o, down_o, small_o,
    g_ref, xall, left, right, pf, cv, rg, ig, st, mid, own, sb, rb, gmid, rw, vec, vgrad, gains, gsum, gpart, sgrad, acc,
    leftt, pp, stage, res,
    lsem, psem_s, psem_r, free, hand_s, hand_r, back_s, back_r, *more,
):
    sec = lax.axis_index("section")
    t = lax.axis_index("tensor")
    ring = Ring()
    barrier = pltpu.get_barrier_semaphore()
    others = [{"dp": d} for d in (ring.ap, ring.am, ring.bp, ring.bm, ring.sib)] + [{"tensor": 1 - t}, {"section": 1 - sec}, {"section": 1 - sec, "tensor": 1 - t}]
    for dev in others:
        pl.semaphore_signal(barrier, inc=1, device_id=dev, device_id_type=MESH)
    loads = []

    def load(src, col, width, piece, lane):
        part = src.at[:, pl.ds(col, width)]
        to = g_ref.at[piece, ring.x, ring.z, ring.c, :, pl.ds(lane, width)]
        loads.append(pltpu.make_async_copy(part, to, lsem.at[len(loads)]))

    load(down_ref, 2048, 256, 0, 0)
    load(small_ref, 0, 256, 0, 256)
    for i in range(2):
        load(gelu_ref, i * 512, 512, 1 + i, 0)
        load(lru_ref, i * 512, 512, 3 + i, 0)
        load(out_ref, i * 512, 512, 5 + i, 0)
    for i in range(9):
        load(gate_ref, i * 256, 256, 7 + i, 0)
        load(up_ref, i * 256, 256, 7 + i, 256)
    for i in range(4):
        load(down_ref, i * 512, 512, 16 + i, 0)
    for copy in loads:
        copy.start()
    my = pl.ds(pl.multiple_of(t * HALF, 16), HALF)
    his = pl.ds(pl.multiple_of((1 - t) * HALF, 16), HALF)
    xcopy = pltpu.make_async_copy(xin_ref, xall.at[t], lsem.at[30])
    ecopy = pltpu.make_async_copy(ein_ref, left.at[3, my], lsem.at[31])

    @pl.when(sec == 0)
    def _():
        xcopy.start()

    @pl.when(sec == 1)
    def _():
        ecopy.start()

    pl.semaphore_wait(barrier, 8)
    for copy in loads:
        copy.wait()

    def pair(src, dst, i):
        return go(src, dst, {"tensor": 1 - t}, psem_s.at[i], psem_r.at[i])

    def share(li, i):
        return pair(left.at[li, my], left.at[li, my], i)

    def shared(li, i):
        return pair(left.at[li, his], left.at[li, his], i)

    def rows48(i):
        return pl.ds(pl.multiple_of(i * 48, 16), 48)

    def half48(h, i):
        return pl.ds(pl.multiple_of(h * HALF + i * 48, 16), 48)

    def hand(to, r):
        dev = {"section": 1 - sec, "tensor": (t + to) % 2}
        return go(res.at[rows48(r)], xall.at[t, rows48(r)], dev, hand_s.at[to, r], hand_r.at[t, r])

    def handed(h, r):
        to = xall.at[h, rows48(r)]
        return go(to, to, {"section": 1 - sec}, hand_s.at[0, r], hand_r.at[h, r])

    def hand_back(to, r):
        dev = {"section": 1 - sec, "tensor": (t + to) % 2}
        return go(res.at[rows48(r)], left.at[3, half48(t, r)], dev, back_s.at[to, r], back_r.at[t, r])

    def handed_back(h, r):
        to = left.at[3, half48(h, r)]
        return go(to, to, {"section": 1 - sec}, back_s.at[0, r], back_r.at[h, r])

    ag_step, ag_ready, ag_finish = gather_steps(ring, g_ref, more[0:6])
    deal = deal_steps(ring, res, hid_out, more[6:13])

    @pl.when(sec == 0)
    def _():
        def body(i, carry):
            ag_step(i)
            return carry
        lax.fori_loop(0, 4 * SLACK + 1, body, 0)
        ag_ready(0)
        xcopy.wait()

    @pl.when(sec == 1)
    def _():
        ecopy.wait()
        share(3, 10).start()

        def body(i, carry):
            ag_step(i)
            return carry

        lax.fori_loop(0, PIECES + 4 * SLACK, body, 0)

        def await_piece(i, carry):
            ag_ready(i)
            return carry

        lax.fori_loop(0, PIECES, await_piece, 0)

    def beside(piece):
        @pl.when(sec == 0)
        def _():
            ag_step(piece + 4 * SLACK)
            ag_ready(piece)

    def wt(piece, lane):
        return g_ref[piece, :, :, :, :, pl.ds(pl.multiple_of(lane, TILE), TILE)].reshape(D, TILE)

    def wc(piece):
        return g_ref[piece].reshape(D, PW)

    def wq(piece, x, width=PW):
        return g_ref[piece, x, :, :, :, 0:width].reshape(QUARTER, width)

    right[0] = jnp.zeros((ALL, PW), BF16)
    small = wt(0, TILE)

    def unpack(j, carry):
        ci, r = iota((128, D), 0), iota((128, D), 1)
        sel = onehot(r == (ci // 4) * 48 + j * 4 + ci % 4)
        rw[j] = nn(sel, small).astype(BF16)
        return carry

    lax.fori_loop(0, 8, unpack, 0)
    dpi, r = iota((32, D), 0), iota((32, D), 1)
    t32 = nn(onehot(r == dpi * 48 + 32), small).astype(BF16)
    d1 = onehot(iota((32, 128), 1) // 4 == iota((32, 128), 0))
    e1 = tn(t32, d1)
    e1 = jnp.where(iota((256, 128), 0) % 4 == iota((256, 128), 1) % 4, e1, 0.0).astype(BF16)
    v1 = nn(onehot(iota((64, 256), 1) // 4 == iota((64, 256), 0)), e1)
    for i in range(64):
        vec[i] = v1[i:i + 1, :]
    t33 = nn(onehot(r == dpi * 48 + 33), small).astype(BF16)
    d2 = onehot(jnp.logical_and(r >= dpi * 48, r < dpi * 48 + 48))
    e2 = tn(t33[:, 0:128], d2)
    within = iota((128, D), 1) % 48
    q = iota((128, D), 0)
    gains[0] = jnp.sum(jnp.where(q == within, e2, 0.0), axis=0, keepdims=True)
    gains[1] = jnp.sum(jnp.where(q == within + 48, e2, 0.0), axis=0, keepdims=True)

    def scale_of(v):
        return lax.rsqrt(jnp.mean(v * v, axis=1, keepdims=True) + EPS)

    def norm_one(h, i):
        v = xall[h, rows48(i), :].astype(F32)
        left[0, half48(h, i), :] = (v * scale_of(v) * gains[0]).astype(BF16)

    def into_branches(rows, first):
        def body(i, carry):
            if first:
                beside(1 + i)
            elif first is False:
                pl.when(i < 2)(lambda: beside(5 + i))
            pf[i, rows, :] = nn(left[0, rows, :], wc(1 + i))
            return carry
        lax.fori_loop(0, 4, body, 0)

    @pl.when(sec == 0)
    def _():
        def body(i, carry):
            norm_one(t, i)
            return carry

        lax.fori_loop(0, 3, body, 0)
        share(0, 0).start()
        into_branches(my, True)
        shared(0, 0).wait_recv()
        into_branches(his, False)

    @pl.when(sec == 1)
    def _():
        def body(i, carry):
            for h in range(2):
                handed(h, i).wait_recv()
                norm_one(h, i)
            return carry

        lax.fori_loop(0, 3, body, 0)
        into_branches(slice(None), None)

    def vrow(a, j):
        return vec[a * 8 + j]

    def lanes_of(i, h):
        return pl.ds(pl.multiple_of((i % 2) * 256 + h * 128, 128), 128)

    def mixer(i, carry):
        beside(7 + i)
        for h in range(2):
            j = i * 2 + h
            lanes = lanes_of(i, h)
            feature = to_natural(pf[2 + i // 2, :, lanes])
            filtered = vrow(7, j)
            for k in range(4):
                filtered = filtered + vrow(3 + k, j) * (down(feature, k) * mask_ref[k - 1] if k else feature)
            low = filtered.astype(BF16)
            cv[j] = low
            conv = low.astype(F32)
            pre = nn(low, rw[j])
            rate = sigmoid(pre[:, 0:128] + vrow(0, j))
            inp = sigmoid(pre[:, 128:256] + vrow(1, j))
            rg[j] = rate
            ig[j] = inp
            decay = jnp.exp(-8.0 * rate * softplus(-vrow(2, j)))
            scale_in = jnp.sqrt(jnp.maximum(1.0 - decay * decay, FLOOR))
            state = scan_down(decay * mask_ref[0], scale_in * inp * conv)
            st[j] = state
            right[5 + i // 2, :, lanes] = (to_exchange(state) * gelu(pf[i // 2, :, lanes])).astype(BF16)
        return carry

    lax.fori_loop(0, 4, mixer, 0)

    def reduce_out(pieces, base, turn, also):
        def body(x, carry):
            total = None
            for piece in pieces:
                width = PW if piece else TILE
                part = nt(right[piece, :, 0:width], wq(piece, x, width))
                total = part if total is None else total + part
            acc[...] = total
            sb[x] = acc[his, :].astype(BF16)
            pair(sb.at[x], rb.at[turn, x], base + x).start()
            own[x] = acc[my, :]
            also(x)
            return carry

        lax.fori_loop(0, 4, body, 0)

    def reduce_wait(base, turn):
        for x in range(4):
            pair(sb.at[x], rb.at[turn, x], base + x).wait()

    def summed(i, turn):
        rows = rows48(i)
        return jnp.concatenate([own[x, rows, :] + rb[turn, x, rows, :].astype(F32) for x in range(4)], axis=1)

    reduce_out((5, 6), 1, 0, lambda x: beside(11 + x))
    reduce_wait(1, 0)

    def norm_two(i, carry):
        v = xall[t, rows48(i), :].astype(F32) + summed(i, 0)
        mid[rows48(i), :] = v
        left[2, half48(t, i), :] = (v * scale_of(v) * gains[1]).astype(BF16)
        return carry

    lax.fori_loop(0, 3, norm_two, 0)
    share(2, 5).start()

    def hidden_at(i):
        return (16 + i // 2) % PIECES, pl.multiple_of((i % 2) * TILE, TILE)

    def feed(rows, first):
        def body(i, carry):
            if first:
                pl.when(i % 4 == 0)(lambda: beside(15 + i // 4))
            else:
                pl.when(jnp.logical_or(i == 3, i == 7))(lambda: beside(18 + i // 7))
            both = nn(left[2, rows, :], wc(7 + i))
            pg, pu = both[:, 0:TILE], both[:, TILE:PW]
            right[7 + i, rows, :] = both.astype(BF16)
            piece, lane = hidden_at(i)
            right[piece, rows, pl.ds(lane, TILE)] = (gelu(pg) * pu).astype(BF16)
            return carry
        lax.fori_loop(0, 9, body, 0)

    feed(my, True)
    shared(2, 5).wait_recv()
    feed(his, False)
    reduce_out((16, 17, 18, 19, 0), 6, 1, lambda x: None)
    reduce_wait(6, 1)

    def finish_forward(i, carry):
        v = mid[rows48(i), :] + summed(i, 1)
        res[rows48(i), :] = v.astype(BF16)

        @pl.when(sec == 0)
        def _():
            hand(0, i).start()
            hand(1, i).start()

        return carry

    lax.fori_loop(0, 3, finish_forward, 0)

    @pl.when(sec == 0)
    def _():
        for i in range(5):
            deal(i)
        for h in range(2):
            for r in range(3):
                handed_back(h, r).wait_recv()

    def deal_beside(i):
        @pl.when(sec == 1)
        def _():
            deal(i)

    deal_beside(0)
    ag_finish()
    @pl.when(sec == 1)
    def _():
        shared(3, 10).wait_recv()

    def feed_back(i, carry):
        piece, lane = hidden_at(i)
        gh = nn(left[3], wt(piece, lane))
        pg = right[7 + i, :, 0:TILE].astype(F32)
        pu = right[7 + i, :, TILE:PW].astype(F32)
        act, slope = gelu_parts(pg)
        right[7 + i, :, 0:TILE] = (gh * pu * slope).astype(BF16)
        right[7 + i, :, TILE:PW] = (gh * act).astype(BF16)
        return carry

    lax.fori_loop(0, 9, feed_back, 0)
    around = (ring.ap, ring.am, ring.bp, ring.bm, ring.sib)

    def release(group):
        for dev in around:
            pl.semaphore_signal(free.at[group], inc=1, device_id={"dp": dev}, device_id_type=MESH)

    rs_step, rs_finish = reduce_steps(ring, g_ref, left, right, leftt, pp, (gelu_o, lru_o, out_o, gate_o, up_o, down_o, small_o), stage, free, lambda: pack_small(), more[13:20])

    def sum_beside(i, low, high):
        @pl.when(sec == 0)
        def _():
            rs_step(i, low, high)

    release(0)
    deal_beside(1)
    reduce_out(tuple(range(7, 16)), 11, 0, lambda x: sum_beside(x, 0, 3))
    release(1)
    sum_beside(4, 4, 4)
    reduce_wait(11, 0)

    def eight(v):
        total = v[0:8]
        for i in range(1, 6):
            total = total + v[i * 8:i * 8 + 8]
        return total

    def middle_back(i, carry):
        ng = summed(i, 0)
        m = mid[rows48(i), :]
        sc = scale_of(m)
        u = ng * gains[1]
        e = left[3, half48(t, i), :].astype(F32)
        gm = e + sc * u - m * (sc * sc * sc) * jnp.mean(u * m, axis=1, keepdims=True)
        gmid[rows48(i), :] = gm
        left[1, half48(t, i), :] = gm.astype(BF16)
        return carry + eight(ng * m * sc)

    gpart[1] = lax.fori_loop(0, 3, middle_back, jnp.zeros((8, D), F32))
    share(1, 15).start()
    deal_beside(2)
    sum_beside(5, 5, 5)
    sum_beside(6, 6, 6)
    shared(1, 15).wait_recv()

    def mixer_back(i, carry):
        gmix = nn(left[1], wt(5 + i // 2, (i % 2) * TILE))
        sum_beside(7 + i, 7, 10)
        for h in range(2):
            j = i * 2 + h
            lanes = lanes_of(i, h)
            gm = gmix[:, h * 128:h * 128 + 128]
            act, slope = gelu_parts(pf[i // 2, :, lanes])
            state = st[j]
            right[1 + i // 2, :, lanes] = (gm * to_exchange(state) * slope).astype(BF16)
            grad_state = to_natural(gm * act)
            rate, inp = rg[j], ig[j]
            conv = cv[j].astype(F32)
            forget = softplus(-vrow(2, j))
            decay = jnp.exp(-8.0 * rate * forget)
            spare = 1.0 - decay * decay
            scale_in = jnp.sqrt(jnp.maximum(spare, FLOOR))
            m1 = mask_ref[0]
            drive = scan_up(up(decay * m1, 1), grad_state)
            grad_spare = jnp.where(spare > FLOOR, 0.5 * (drive * inp * conv) / scale_in, 0.0)
            grad_decay = drive * down(state, 1) * m1 - 2.0 * decay * grad_spare
            grad_log = grad_decay * decay
            rate_low = (grad_log * (-8.0 * forget) * rate * (1.0 - rate)).astype(BF16)
            driven = drive * scale_in
            input_low = (driven * conv * inp * (1.0 - inp)).astype(BF16)
            both = jnp.concatenate([rate_low, input_low], axis=1)
            back = nt(both, rw[j])
            vgrad[0 * 8 + j] = jnp.sum(rate_low.astype(F32), axis=0, keepdims=True)
            vgrad[1 * 8 + j] = jnp.sum(input_low.astype(F32), axis=0, keepdims=True)
            grad_forget = jnp.sum(grad_log * (-8.0 * rate), axis=0, keepdims=True)
            vgrad[2 * 8 + j] = -grad_forget * sigmoid(-vrow(2, j))
            sgrad[j] = tn(cv[j], both).astype(BF16)
            grad_conv = driven * inp + back
            feature = to_natural(pf[2 + i // 2, :, lanes])
            grad_feature = None
            for k in range(4):
                masked = grad_conv * mask_ref[k - 1] if k else grad_conv
                vgrad[(3 + k) * 8 + j] = jnp.sum(masked * down(feature, k), axis=0, keepdims=True)
                term = up(masked, k) * vrow(3 + k, j)
                grad_feature = term if grad_feature is None else grad_feature + term
            vgrad[7 * 8 + j] = jnp.sum(grad_conv, axis=0, keepdims=True)
            right[3 + i // 2, :, lanes] = to_exchange(grad_feature).astype(BF16)
        return carry

    lax.fori_loop(0, 4, mixer_back, 0)
    release(2)
    deal_beside(3)
    reduce_out((1, 2, 3, 4), 16, 1, lambda x: sum_beside(11 + x, 11, 14))
    release(3)
    sum_beside(15, 15, 15)
    sum_beside(16, 16, 16)
    reduce_wait(16, 1)

    def first_back(i, carry):
        fg = summed(i, 1)
        v = xall[t, rows48(i), :].astype(F32)
        sc = scale_of(v)
        u = fg * gains[0]
        gv = gmid[rows48(i), :] + sc * u - v * (sc * sc * sc) * jnp.mean(u * v, axis=1, keepdims=True)
        mid[rows48(i), :] = gv

        @pl.when(sec == 1)
        def _():
            res[rows48(i), :] = gv.astype(BF16)
            hand_back(0, i).start()
            hand_back(1, i).start()

        return carry + eight(fg * v * sc)

    gpart[0] = lax.fori_loop(0, 3, first_back, jnp.zeros((8, D), F32))
    pair(gpart, gsum, 20).start()
    grad_copy = pltpu.make_async_copy(mid, grad_out, lsem.at[0])
    grad_copy.start()
    deal_beside(4)

    v2 = jnp.concatenate([vgrad[i] for i in range(64)], axis=0).astype(BF16)
    e2 = nn(onehot(iota((256, 64), 0) // 4 == iota((256, 64), 1)), v2)
    e2 = jnp.where(iota((256, 128), 0) % 4 == iota((256, 128), 1) % 4, e2, 0.0).astype(BF16)
    t32 = nt(d1, e2).astype(BF16)
    pair(gpart, gsum, 20).wait()
    n1 = jnp.sum(gpart[0] + gsum[0], axis=0, keepdims=True)
    n2 = jnp.sum(gpart[1] + gsum[1], axis=0, keepdims=True)
    spread = jnp.where(q == within, n1, jnp.where(q == within + 48, n2, 0.0)).astype(BF16)
    t33 = nt(d2, spread).astype(BF16)
    t33 = jnp.concatenate([t33, jnp.zeros((32, 128), BF16)], axis=1)

    def pack_part(x, carry):
        r = iota((QUARTER, 128), 0) + x * QUARTER
        ci = iota((QUARTER, 128), 1)
        total = None
        for j in range(8):
            sel = onehot(r == (ci // 4) * 48 + j * 4 + ci % 4)
            part = nn(sel, sgrad[j])
            total = part if total is None else total + part
        r = iota((QUARTER, 32), 0) + x * QUARTER
        dpi = iota((QUARTER, 32), 1)
        total = total + nn(onehot(r == dpi * 48 + 32), t32) + nn(onehot(r == dpi * 48 + 33), t33)
        pp[0, x, :, :, :, TILE:PW] = total.astype(BF16).reshape(4, 2, 48, TILE)
        return carry

    def pack_small():
        lax.fori_loop(0, 4, pack_part, 0)

    def last(i, carry):
        rs_step(i, 0, PIECES + 5 * LAG - 1)
        return carry

    lax.fori_loop(jnp.where(sec == 0, 17, 0), PIECES + 5 * LAG, last, 0)
    rs_finish()
    deal(5)
    share(2, 5).wait_send()
    share(1, 15).wait_send()

    @pl.when(sec == 0)
    def _():
        share(0, 0).wait_send()
        for to in range(2):
            for r in range(3):
                hand(to, r).wait_send()

    @pl.when(sec == 1)
    def _():
        share(3, 10).wait_send()
        for to in range(2):
            for r in range(3):
                hand_back(to, r).wait_send()

    grad_copy.wait()


def whole(gelu, lru, out, gate, up_, down_, small, xin, ein, masks):
    K = PIECES
    dma = pltpu.SemaphoreType.DMA
    vmem = pl.BlockSpec(memory_space=pltpu.VMEM)
    hbm = pl.BlockSpec(memory_space=pl.ANY)
    sds = jax.ShapeDtypeStruct
    return pl.pallas_call(
        whole_kernel,
        name="whole",
        out_shape=(
            sds((4, 4, 2, HALF, D), BF16), sds((HALF, D), F32),
            sds((48, 1024), F32), sds((48, 1024), F32), sds((48, 1024), F32),
            sds((48, 2304), F32), sds((48, 2304), F32), sds((48, 2304), F32), sds((48, TILE), F32),
        ),
        in_specs=[hbm] * 9 + [vmem],
        out_specs=(hbm,) * 9,
        scratch_shapes=[
            pltpu.VMEM((K, 4, 4, 2, 48, PW), BF16),
            pltpu.VMEM((2, HALF, D), BF16),
            pltpu.VMEM((4, ALL, D), BF16),
            pltpu.VMEM((K, ALL, PW), BF16),
            pltpu.VMEM((4, ALL, PW), F32),
            pltpu.VMEM((8, ALL, 128), BF16),
            pltpu.VMEM((8, ALL, 128), F32),
            pltpu.VMEM((8, ALL, 128), F32),
            pltpu.VMEM((8, ALL, 128), F32),
            pltpu.VMEM((HALF, D), F32),
            pltpu.VMEM((4, HALF, QUARTER), F32),
            pltpu.VMEM((4, HALF, QUARTER), BF16),
            pltpu.VMEM((2, 4, HALF, QUARTER), BF16),
            pltpu.VMEM((HALF, D), F32),
            pltpu.VMEM((8, 128, 256), BF16),
            pltpu.VMEM((64, 1, 128), F32),
            pltpu.VMEM((64, 1, 128), F32),
            pltpu.VMEM((2, 1, D), F32),
            pltpu.VMEM((2, 8, D), F32),
            pltpu.VMEM((2, 8, D), F32),
            pltpu.VMEM((8, 128, 256), BF16),
            pltpu.VMEM((ALL, QUARTER), F32),
            pltpu.VMEM((D, ALL), BF16),
            pltpu.VMEM((2, 4, 4, 2, 48, PW), BF16),
            pltpu.VMEM((2, 48, PW), F32),
            pltpu.VMEM((HALF, D), BF16),
            dma((32,)), dma((21,)), dma((21,)), pltpu.SemaphoreType.REGULAR((4,)),
            dma((2, 3)), dma((2, 3)), dma((2, 3)), dma((2, 3)),
            dma((K, 3)), dma((K, 3)), dma((K, 3)), dma((K, 3)), dma((K, 4)), dma((K, 4)),
            dma((4,)), dma((4,)), dma((4,)), dma((4,)), dma((4,)), dma((4,)), dma(()),
            dma((K,)), dma((K,)), dma((K, 3)), dma((K, 3)), dma((K, 3)), dma((K, 3)), dma((2, 2)),
        ],
        compiler_params=pltpu.CompilerParams(
            collective_id=1, has_side_effects=True, vmem_limit_bytes=VMEM_LIMIT
        ),
    )(gelu, lru, out, gate, up_, down_, small, xin, ein, masks)


def settle_kernel(source_ref, every, *refs):
    ins, outs, held = refs[0:7], refs[7:15], refs[15:22]
    buf, sem, back, pick = refs[22:26]
    hid_o = outs[0]
    picks = [pltpu.make_async_copy(every.at[source_ref[m]], buf.at[m], pick.at[m]) for m in range(2)]
    for copy in picks:
        copy.start()
    loads = [pltpu.make_async_copy(a, b, sem.at[i]) for i, (a, b) in enumerate(zip(ins, held))]
    copies = [pltpu.make_async_copy(a, b, back.at[i]) for i, (a, b) in enumerate(zip(held, outs[1:]))]
    for copy in loads:
        copy.start()
    for copy in picks:
        copy.wait()
    for load, copy in zip(loads, copies):
        load.wait()
        copy.start()
    hid_o[0:72, :] = buf[0].astype(F32)[0:72]
    hid_o[72:144, :] = buf[1].astype(F32)[72:144]
    for copy in copies:
        copy.wait()


def settle(source, every, *results):
    vmem = pl.BlockSpec(memory_space=pltpu.VMEM)
    hbm = pl.BlockSpec(memory_space=pl.ANY)
    return pl.pallas_call(
        settle_kernel,
        name="settle",
        out_shape=(jax.ShapeDtypeStruct((HALF, D), F32),) + tuple(jax.ShapeDtypeStruct(r.shape, F32) for r in results),
        in_specs=[pl.BlockSpec(memory_space=pltpu.SMEM)] + [hbm] * 8,
        out_specs=(vmem,) + (hbm,) * 7,
        scratch_shapes=[pltpu.VMEM(r.shape, F32) for r in results]
        + [pltpu.VMEM((2, HALF, D), BF16)] + [pltpu.SemaphoreType.DMA((n,)) for n in (7, 7, 2)],
        compiler_params=pltpu.CompilerParams(vmem_limit_bytes=60 * 2**20),
    )(source, every, *results)


def document_masks(doc_lengths):
    ends = jnp.cumsum(doc_lengths, axis=-1, dtype=jnp.int32)
    position = jnp.arange(HALF, dtype=jnp.int32)
    ident = jnp.sum((position[None, :, None] >= ends[:, None, :]).astype(jnp.int32), axis=-1, dtype=jnp.int32)
    masks = []
    for offset in range(1, 4):
        before = jnp.pad(ident, ((0, 0), (offset, 0)), constant_values=-1)[:, :HALF]
        masks.append((before == ident).astype(F32).reshape(ALL, 1))
    return jnp.broadcast_to(jnp.stack(masks), (3, ALL, 128))


def pack_small_shard(rate_weight, input_weight, rate_bias, input_bias, decay_param, filter_taps, filter_bias, norm_first, norm_second):
    vectors = jnp.concatenate([v[0].reshape(-1) for v in (rate_bias, input_bias, decay_param, filter_taps, filter_bias)]).reshape(1, 256)
    gains = jnp.concatenate([norm_first[0], norm_second[0], jnp.zeros((160,), BF16)]).reshape(1, 256)
    gates = jnp.concatenate([rate_weight[0].reshape(32, 128), input_weight[0].reshape(32, 128)], axis=1)
    return jnp.concatenate([gates, vectors, gains, jnp.zeros((14, 256), BF16)], axis=0)


def shards(
    inputs, out_grad, lengths, order, gelu_weight, lru_weight, rate_weight, input_weight, rate_bias, input_bias,
    decay_param, filter_taps, filter_bias, out_weight, gate_weight, up_weight, down_weight, norm_first, norm_second
):
    group = lax.axis_index("dp")
    masks = document_masks(lax.dynamic_index_in_dim(lengths, group, 1, keepdims=False))
    small = pack_small_shard(rate_weight, input_weight, rate_bias, input_bias, decay_param, filter_taps, filter_bias, norm_first, norm_second)
    every, grad, gelu_grad, lru_grad, out_wgrad, gate_grad, up_grad, down_grad, tiny = whole(
        gelu_weight[0], lru_weight[0], out_weight[0].T, gate_weight[0], up_weight[0], down_weight[0].T, small,
        inputs.reshape(HALF, D), out_grad.reshape(HALF, D), masks
    )
    slots = jnp.arange(32, dtype=jnp.int32)
    source = jnp.sum(jnp.where(order == group, slots[None, :], 0), axis=1, dtype=jnp.int32)
    hidden, grad, gelu_grad, lru_grad, out_wgrad, gate_grad, up_grad, down_grad = settle(
        source, every.reshape(32, HALF, D), grad, gelu_grad, lru_grad, out_wgrad, gate_grad, up_grad, down_grad
    )
    hidden = hidden.reshape(1, 2, 72, D)
    input_grad = grad.reshape(1, 2, 72, D)
    vec = tiny[32].reshape(8, 8, 4)
    return (
        hidden, input_grad, gelu_grad[None], lru_grad[None],
        tiny[0:32, 0:128].reshape(1, 8, 4, 128), tiny[0:32, 128:256].reshape(1, 8, 4, 128),
        vec[0][None], vec[1][None], vec[2][None], vec[3:7][None], vec[7][None],
        out_wgrad.T[None], gate_grad[None], up_grad[None], down_grad.T[None],
        tiny[33, 0:48][None], tiny[33, 48:96][None],
    )


def solution(mesh):
    rows = P(None, ("dp", "tensor"), None)
    tall = P("section", "dp", "tensor")
    wide = P("section", "tensor", "dp")
    block = P("section", "tensor", "dp", None)
    taps = P("section", None, "tensor", "dp")
    gain = P("section", "dp")
    params = (tall, tall, block, block, wide, wide, wide, taps, wide, wide, tall, tall, wide, gain, gain)
    out_rows = P("section", None, ("dp", "tensor"), None)
    return jax.shard_map(
        shards,
        mesh=mesh,
        in_specs=(rows, rows, P(), P()) + params,
        out_specs=(out_rows, out_rows) + params,
        check_vma=False,
    )
```
